128 devices in a mesh: face: 16 (over y, z_hi, core), sample: 8 (over x, z_lo).
Axes of the slice: x: 4, y: 4, z: 4 (z_hi: 2, z_lo: 2; z = z_hi * 2 + z_lo), core: 2. Of those that a mesh axis runs over, the one named last changes fastest.
Arguments:
- fields: bfloat16 [24, 48, 128, 256], P('sample', 'face'), may hold values from -6 to 6
- sample_index: int32 [16], P('sample'), may hold values from 0 to 2
- halo_index: int32 [48, 68], P('face'), may hold values from 0 to 3071, as said below
- channel_mask: int32 [128], replicated, may hold values 0 or 1
- weight: bfloat16 [1152, 256], replicated, may hold values from -0.1875 to 0.1875
Outputs:
- moments: float32 [1152, 1408], P(('face', 'sample'))
The draws below stay inside these ranges and needn't reach their ends.
Inputs may be any that keep to these rules, and one draw needn't show every extreme that they name: `halo_index`: every cycle pixel names an edge-table entry; the four sides of a subface each follow one edge of some subface, in one of the two directions.
All inputs are finite; a program needn't handle non-finite values.
Results may differ from the reference program's by a relative error of at most 0.0005.
Values may be sent and summed in bfloat16 or wider, within the bound.
No kernel may reach another device: no remote copies, remote signals or barrier semaphores. Data moves between devices by JAX's collectives and lax.ppermute only.
A program may use at most 64 MiB of HBM per device.

```python
import jax
import jax.numpy as jnp
from jax import lax

CI = 128
CO = 256
K = 1152
P_SIZE = 16
SAMP_DEV = 2
POOL_DEV = 3
SUBS = 48
SAMPLES = 16
POOL = 24


def draw_halo_index(key, part):
    key = jax.random.fold_in(key, 5)
    keys = jax.random.split(key, 4)
    neighbour = jax.random.randint(keys[0], (SUBS, 4), 0, SUBS)
    other_side = jax.random.randint(keys[1], (SUBS, 4), 0, 4)
    flipped = jax.random.randint(keys[2], (SUBS, 4), 0, 2)
    along = jnp.arange(P_SIZE, dtype=jnp.int32)
    position = jnp.where(flipped[..., None] == 1, P_SIZE - 1 - along, along)
    side_index = neighbour[..., None] * (4 * P_SIZE) + other_side[..., None] * P_SIZE + position
    corners = jax.random.randint(keys[3], (SUBS, 4), 0, SUBS * 4 * P_SIZE)
    corners = corners.at[0, 0].set(SUBS * 4 * P_SIZE - 1).at[0, 1].set(0)
    top = jnp.concatenate([corners[:, 0:1], side_index[:, 0], corners[:, 1:2]], axis=1)
    bottom = jnp.concatenate([corners[:, 2:3], side_index[:, 1], corners[:, 3:4]], axis=1)
    return jnp.concatenate([top, bottom, side_index[:, 2], side_index[:, 3]], axis=1).astype(jnp.int32)


def touch_ends(drawn, stream_key, low, high):
    longest = drawn.shape.index(max(drawn.shape))
    spots = []
    for shift in (0, 1):
        where = [jax.random.randint(jax.random.fold_in(stream_key, axis), (), 0, length) for axis, length in enumerate(drawn.shape)]
        where[longest] = (where[longest] + shift) % drawn.shape[longest]
        spots.append(tuple(where))
    return drawn.at[spots[0]].set(low).at[spots[1]].set(high)


def level_of(rng, extent, cuts, least, largest):
    level = 1.0
    for axis_at, blocks in cuts:
        steps = jax.random.uniform(jax.random.fold_in(jax.random.fold_in(rng, 6), axis_at), (blocks,), jnp.float32, least / len(cuts), largest / len(cuts))
        level = level * jnp.repeat(jnp.exp(steps), extent[axis_at] // blocks).reshape((-1,) + (1,) * (len(extent) - 1 - axis_at))
    return level


def normal_values(key, extent, deviation, reach, cuts=(), kind=jnp.bfloat16):
    values = jax.random.normal(key, extent, jnp.float32) * deviation
    if len(cuts) > 0:
        values = level_of(key, extent, cuts, -0.22, 0.18) * values
    return jnp.clip(values, min=-reach, max=reach).astype(kind)


def setup_inputs(seed: int = 0) -> dict:
    streams_of = jax.random.split(jax.random.key(seed), 6)
    return {
        "fields": normal_values(streams_of[0], (POOL, SUBS, CI, P_SIZE * P_SIZE), 1.0, 6.0, ((0, 8), (1, 16))),
        "sample_index": touch_ends(jax.random.randint(streams_of[1], (SAMPLES,), 0, POOL_DEV), jax.random.fold_in(streams_of[1], 1), 0, POOL_DEV - 1).astype(jnp.int32),
        "halo_index": draw_halo_index(jax.random.fold_in(streams_of[5], 71), 0),
        "channel_mask": touch_ends((jax.random.randint(streams_of[3], (CI,), 0, 4) < 3).astype(jnp.int32), jax.random.fold_in(streams_of[3], 1), 0, 1),
        "weight": normal_values(streams_of[4], (K, CO), K ** -0.5, 0.1875),
    }


def strip_edges(selected, side):
    grid = selected.reshape(selected.shape[0], selected.shape[1], selected.shape[2], side, side)
    edges = jnp.concatenate([grid[..., 0, :], grid[..., side - 1, :], grid[..., :, 0], grid[..., :, side - 1]], axis=-1)
    edges = jnp.transpose(edges, (0, 2, 1, 3))
    return edges.reshape(edges.shape[0], edges.shape[1], -1)


def build_patches(selected, table, halo_index, side):
    count = selected.shape[0]
    subs = selected.shape[1]
    chans = selected.shape[2]
    flat = halo_index.reshape(-1).astype(jnp.int32)
    cycle = jnp.take(table, flat, axis=2).reshape(count, chans, subs, 4 * side + 4)
    cycle = jnp.transpose(cycle, (0, 2, 1, 3))
    grid = selected.reshape(count, subs, chans, side, side)
    top = cycle[..., 0:side + 2]
    bottom = cycle[..., side + 2:2 * side + 4]
    left = cycle[..., 2 * side + 4:3 * side + 4]
    right = cycle[..., 3 * side + 4:4 * side + 4]
    middle = jnp.concatenate([left[..., :, None], grid, right[..., :, None]], axis=-1)
    padded = jnp.concatenate([top[..., None, :], middle, bottom[..., None, :]], axis=-2)
    taps = [padded[..., dy:dy + side, dx:dx + side] for dy in range(3) for dx in range(3)]
    stacked = jnp.stack(taps, axis=2)
    stacked = jnp.transpose(stacked, (0, 1, 4, 5, 2, 3))
    return stacked.reshape(count * subs * side * side, 9 * chans)


def kept_and_rhs(patches, channel_mask, weight):
    target = jnp.dot(patches, weight, preferred_element_type=jnp.float32).astype(jnp.bfloat16)
    column_mask = jnp.tile(channel_mask, 9).astype(patches.dtype)
    kept = patches * column_mask[None, :]
    return kept, jnp.concatenate([kept, target], axis=1)


def reference(fields, sample_index, halo_index, channel_mask, weight):
    pool_id = (sample_index + (jnp.arange(SAMPLES, dtype=jnp.int32) // SAMP_DEV) * POOL_DEV).astype(jnp.int32)

    def one_sample(total, index):
        selected = lax.dynamic_index_in_dim(fields, index, 0, keepdims=True)
        table = strip_edges(selected, P_SIZE)
        patches = build_patches(selected, table, halo_index, P_SIZE)
        kept, right_side = kept_and_rhs(patches, channel_mask, weight)
        term = lax.dot_general(kept, right_side, (((0,), (0,)), ((), ())), preferred_element_type=jnp.float32)
        return total + term, None

    start = jnp.zeros((K, K + CO), jnp.float32)
    total, unused = lax.scan(one_sample, start, pool_id)
    return total / (SAMPLES * SUBS * P_SIZE * P_SIZE)
```

```python
import functools

import jax
import jax.numpy as jnp
import ml_dtypes
import numpy as np
from jax import lax
from jax.experimental import pallas as pl
from jax.experimental.pallas import tpu as pltpu
from jax.sharding import PartitionSpec as P

SIDE = 16
PIX = SIDE * SIDE
CH = 128
TAPS = 9
K = TAPS * CH
HALF = K // 2
CYCLE = 4 * SIDE + 4
ROWS = 88
AXES = ("face", "sample")
NT = (((1,), (1,)), ((), ()))
SIDE_AT = (1, 19, 36, 52)
CORNER_AT = (0, 17, 18, 35)


def edge_picker():
    out = np.zeros((4 * SIDE, PIX), np.float32)
    for i in range(SIDE):
        out[i, i] = 1
        out[SIDE + i, (SIDE - 1) * SIDE + i] = 1
        out[2 * SIDE + i, i * SIDE] = 1
        out[3 * SIDE + i, i * SIDE + SIDE - 1] = 1
    return out.astype(ml_dtypes.bfloat16)


def tap_matrices():
    out = np.zeros((TAPS, PIX + CH, PIX), np.float32)
    for t in range(TAPS):
        for y in range(SIDE):
            for x in range(SIDE):
                u, v = y + t // 3, x + t % 3
                if u == 0:
                    k = PIX + v
                elif u == SIDE + 1:
                    k = PIX + SIDE + 2 + v
                elif v == 0:
                    k = PIX + 2 * SIDE + 4 + u - 1
                elif v == SIDE + 1:
                    k = PIX + 3 * SIDE + 4 + u - 1
                else:
                    k = (u - 1) * SIDE + v - 1
                out[t, k, y * SIDE + x] = 1
    return out.astype(ml_dtypes.bfloat16)


def source_base():
    out = np.full((1, CH), -1000, np.int32)
    for e, at in enumerate(SIDE_AT):
        out[0, at : at + SIDE] = e * SIDE
    for e, at in enumerate(CORNER_AT):
        out[0, at] = (4 + e) * SIDE
    return out


def edges_kernel(index_ref, fields_ref, pick_ref, copies_ref, own_ref):
    subs = fields_ref.shape[1]
    for s in range(2):
        for f in range(subs):
            x = fields_ref[index_ref[s], f]
            u = s * subs + f
            own_ref[u * CH : (u + 1) * CH, :] = x
            edges = lax.dot_general(pick_ref[...], x, NT, preferred_element_type=jnp.float32)
            edges = edges.astype(jnp.bfloat16)
            for d in range(copies_ref.shape[0]):
                copies_ref[d, u * 4 * SIDE : (u + 1) * 4 * SIDE, :] = edges


def moments_kernel(
    subs,
    core_ref,
    halo_own_ref,
    halo_other_ref,
    own_ref,
    other_ref,
    table_own_ref,
    table_other_ref,
    position_ref,
    base_ref,
    taps_ref,
    kept_row_ref,
    kept_lane_ref,
    message_ref,
    tiles,
    grid,
    patches,
    gram,
):
    core = core_ref[0]
    units = 4 * subs
    half = units // 2

    for side, halo_ref in enumerate((halo_own_ref, halo_other_ref)):
        for f in range(subs):
            for n, at in enumerate(SIDE_AT + CORNER_AT):
                index = halo_ref[f, at]
                sub = index // (4 * SIDE)
                edge = lax.rem(index // SIDE, 4)
                device = sub // subs
                local = sub - device * subs
                near = lax.rem(device, 2) == core
                for s in range(2):
                    row = pl.multiple_of((s * subs + local) * 4 * SIDE + edge * SIDE, SIDE)
                    mine = table_own_ref[device // 2, pl.ds(row, SIDE), :]
                    theirs = table_other_ref[device // 2, pl.ds(row, SIDE), :]
                    u = side * half + s * subs + f
                    tiles[u * CH + n * SIDE : u * CH + (n + 1) * SIDE, :] = jnp.where(near, mine, theirs)

    row_at = lax.broadcasted_iota(jnp.int32, (CH, CH), 0)
    col_at = lax.broadcasted_iota(jnp.int32, (CH, CH), 1)
    eye = jnp.where(row_at == col_at, 1.0, 0.0).astype(jnp.bfloat16)
    turned = lax.dot_general(eye, tiles[...], NT, preferred_element_type=jnp.float32).astype(jnp.bfloat16)
    largest = jnp.zeros((CH, CH), jnp.float32)
    for u in range(units):
        side, f = u // half, u % half % subs
        source = position_ref[side * subs + f : side * subs + f + 1, :] + base_ref[...]
        pick = jnp.where(row_at == source, 1.0, 0.0).astype(jnp.bfloat16)
        cycle = jnp.dot(turned[:, u * CH : (u + 1) * CH], pick, preferred_element_type=jnp.float32)
        x = (own_ref if side == 0 else other_ref)[(u % half) * CH : (u % half + 1) * CH, :]
        grid[u * CH : (u + 1) * CH, :PIX] = x
        grid[u * CH : (u + 1) * CH, PIX:] = cycle.astype(jnp.bfloat16)
        size = jnp.abs(x.astype(jnp.float32))
        largest = jnp.maximum(largest, jnp.maximum(size[:, :CH], size[:, CH:]))
        largest = jnp.maximum(largest, jnp.abs(cycle))

    kept_row = kept_row_ref[...]

    def exponent(values):
        top = jnp.maximum(jnp.max(values), 2.0**-60)
        return jnp.ceil(jnp.log2(jnp.full((8, CH), top, jnp.float32)))

    kept_exp = exponent(jnp.where(kept_row > 0, largest, 0.0))
    any_exp = exponent(largest)
    row_scale = jnp.where(kept_row > 0, jnp.exp2(-kept_exp[0:1, :]), 0.0)
    lane_exps = jnp.where(kept_lane_ref[...] > 0, kept_exp, any_exp)
    lane_scale = jnp.exp2(-lane_exps)

    chunk = units * CH // 3
    for t in range(TAPS):
        for m in range(0, units * CH, chunk):
            if t == TAPS // 2:
                values = grid[m : m + chunk, :PIX]
            else:
                values = jnp.dot(grid[m : m + chunk, :], taps_ref[t], preferred_element_type=jnp.float32)
                values = values.astype(jnp.bfloat16)
            for n in range(chunk // CH):
                u = m // CH + n
                patches[t * CH : (t + 1) * CH, u * PIX : (u + 1) * PIX] = values[n * CH : (n + 1) * CH, :]

    right = patches[pl.ds(pl.multiple_of(core * HALF, HALF), HALF), :]
    for t in range(0, TAPS, 3):
        block = lax.dot_general(
            patches[t * CH : (t + 3) * CH, :], right, NT, preferred_element_type=jnp.float32
        )
        for n in range(3):
            rows = block[n * CH : (n + 1) * CH, :]
            for l in range(4):
                part = rows[:, l * CH : (l + 1) * CH] * row_scale * lane_scale[0:1, :]
                gram[l, (t + n) * CH : (t + n + 1) * CH, :] = part
            part = rows[:, 4 * CH :] * row_scale[:, : CH // 2] * lane_scale[1:2, : CH // 2]
            gram[4, (t + n) * CH : (t + n + 1) * CH, : CH // 2] = part

    for g in range(8):
        for s in range(8):
            j = g * 8 + s
            at = g * 144 + s * 9
            for c in range(2):
                for l in range(4):
                    to = (c * 4 + l) * 9
                    message_ref[j, to : to + 9, :] = gram[l, at + c * 72 : at + c * 72 + 9, :]
                message_ref[j, 72:81, c * 64 : (c + 1) * 64] = gram[4, at + c * 72 : at + c * 72 + 9, : CH // 2]
            message_ref[j, 81:88, :] = (lane_exps + kept_exp)[0:7, :]


def rows_kernel(place_ref, mask_ref, near_ref, far_ref, weight_ref, kept_ref, out_ref, rows):
    core, owner = place_ref[0], place_ref[1]
    near, far = near_ref[...], far_ref[...]
    low = jnp.where(core == 0, near, far)
    high = jnp.where(core == 0, far, near)

    def mine(values, l):
        return jnp.where(core == 0, values[l * 9 : l * 9 + 9, :], values[(4 + l) * 9 : (4 + l) * 9 + 9, :])

    def middle(values):
        return jnp.where(core == 0, values[72:81, : CH // 2], values[72:81, CH // 2 :])

    for l in range(4):
        rows[0:9, l * CH : (l + 1) * CH] = mine(low, l)
        rows[0:9, HALF + l * CH : HALF + (l + 1) * CH] = mine(high, l)
    rows[0:9, 4 * CH : HALF] = middle(low)
    rows[0:9, HALF + 4 * CH :] = middle(high)

    at = lax.broadcasted_iota(jnp.int32, (9, CH), 0)
    keep = jnp.zeros((9, CH), jnp.float32)
    for k in range(9):
        bit = mask_ref[lax.rem(owner * 9 + k, CH)]
        keep = jnp.where(at == k, bit.astype(jnp.float32), keep)
    whole = rows[0:9, :]
    head = whole.astype(jnp.bfloat16)
    left = whole - head.astype(jnp.float32)
    tail = left.astype(jnp.bfloat16)
    rest = (left - tail.astype(jnp.float32)).astype(jnp.bfloat16)
    weight = weight_ref[...]
    product = jnp.dot(rest, weight, preferred_element_type=jnp.float32)
    product += jnp.dot(tail, weight, preferred_element_type=jnp.float32)
    product += jnp.dot(head, weight, preferred_element_type=jnp.float32)
    count = place_ref[2].astype(jnp.float32)
    kept = kept_ref[...]
    for t in range(TAPS):
        part = whole[:, t * CH : (t + 1) * CH]
        out_ref[:, t * CH : (t + 1) * CH] = jnp.where((keep > 0) & (kept > 0), part / count, 0.0)
    for n in range(2):
        part = product[:, n * CH : (n + 1) * CH]
        out_ref[:, K + n * CH : K + (n + 1) * CH] = jnp.where(keep > 0, part / count, 0.0)


VMEM = pl.BlockSpec(memory_space=pltpu.VMEM)
SMEM = pl.BlockSpec(memory_space=pltpu.SMEM)


def shape(dims, kind):
    return jax.ShapeDtypeStruct(dims, kind)


def per_device(fields, sample_index, halo_index, channel_mask, weight):
    faces, samples = lax.axis_size("face"), lax.axis_size("sample")
    face, sample = lax.axis_index("face"), lax.axis_index("sample")
    core = lax.rem(face, 2)
    subs = fields.shape[1]
    units = 4 * subs
    swap = [(f, f ^ 1) for f in range(faces)]
    bf16, f32 = jnp.bfloat16, jnp.float32

    copies, own = pl.pallas_call(
        edges_kernel,
        out_shape=(shape((faces // 2, 8 * subs * SIDE, CH), bf16), shape((units // 2 * CH, PIX), bf16)),
        in_specs=[SMEM, VMEM, VMEM],
        out_specs=(VMEM, VMEM),
        name="edges",
    )(sample_index, fields, jnp.asarray(edge_picker()))

    other = lax.ppermute(own, "face", swap)
    halo_other = lax.ppermute(halo_index, "face", swap)
    same_core = [[f for f in range(c, faces, 2)] for c in range(2)]
    table = lax.all_to_all(copies, "face", 0, 0, axis_index_groups=same_core)
    table_other = lax.ppermute(table, "face", swap)

    both = jnp.concatenate([halo_index, halo_other], axis=0)
    position = jnp.pad(lax.rem(both, SIDE), ((0, 0), (0, CH - CYCLE)))
    keep = channel_mask.astype(f32)
    kept_row = jnp.broadcast_to(keep[:, None], (CH, CH))
    rolled = jnp.where(core == 0, keep, jnp.roll(keep, CH // 2))
    folded = jnp.concatenate([rolled[: CH // 2], rolled[: CH // 2]])
    kept_lane = jnp.concatenate([rolled[None], jnp.broadcast_to(folded[None], (7, CH))], axis=0)

    message = pl.pallas_call(
        functools.partial(moments_kernel, subs),
        out_shape=shape((64, ROWS, CH), f32),
        in_specs=[SMEM] * 3 + [VMEM] * 9,
        out_specs=VMEM,
        scratch_shapes=[
            pltpu.VMEM((units * CH, CH), bf16),
            pltpu.VMEM((units * CH, PIX + CH), bf16),
            pltpu.VMEM((K, units * PIX), bf16),
            pltpu.VMEM((5, K, CH), f32),
        ],
        compiler_params=pltpu.CompilerParams(vmem_limit_bytes=56 * 2**20),
        name="moments",
    )(
        core[None],
        halo_index,
        halo_other,
        own,
        other,
        table,
        table_other,
        position,
        jnp.asarray(source_base()),
        jnp.asarray(tap_matrices()),
        kept_row,
        kept_lane,
    )

    groups = [[f * samples + s for f in range(c, faces, 2) for s in range(samples)] for c in range(2)]
    landed = lax.all_to_all(message.astype(jnp.float16), AXES, 0, 0, axis_index_groups=groups)
    landed = landed.astype(f32)
    exps = jnp.where(jnp.arange(ROWS)[None, :, None] < 72, landed[:, 81:82, :], landed[:, 82:83, :])
    near = jnp.sum(landed * jnp.exp2(exps), axis=0)
    far = lax.ppermute(near, "face", swap)

    pixels = 2 * subs * PIX * faces * samples
    place = jnp.stack([core, face * samples + sample, jnp.int32(pixels)])
    return pl.pallas_call(
        rows_kernel,
        out_shape=shape((TAPS, K + weight.shape[1]), f32),
        in_specs=[SMEM] * 2 + [VMEM] * 4,
        out_specs=VMEM,
        scratch_shapes=[pltpu.VMEM((16, K), f32)],
        name="rows",
    )(place, channel_mask, near, far, weight, keep[None])


def solution(mesh):
    placed = (P("sample", "face", None, None), P("sample"), P("face", None), P(), P())
    return jax.shard_map(
        per_device,
        mesh=mesh,
        in_specs=placed,
        out_specs=P(("face", "sample"), None),
        check_vma=False,
    )
```

```python
import functools

import jax
import jax.numpy as jnp
import ml_dtypes
import numpy as np
from jax import lax
from jax.experimental import pallas as pl
from jax.experimental.pallas import tpu as pltpu
from jax.sharding import PartitionSpec as P

SIDE = 16
PIX = SIDE * SIDE
CH = 128
TAPS = 9
K = TAPS * CH
HALF = K // 2
CYCLE = 4 * SIDE + 4
RIM = 64
ROWS = 88
AXES = ("face", "sample")
NT = (((1,), (1,)), ((), ()))
SIDE_AT = (1, 19, 36, 52)
CORNER_AT = (0, 17, 18, 35)


def edge_picker():
    out = np.zeros((4 * SIDE, PIX), np.float32)
    for i in range(SIDE):
        out[i, i] = 1
        out[SIDE + i, (SIDE - 1) * SIDE + i] = 1
        out[2 * SIDE + i, i * SIDE] = 1
        out[3 * SIDE + i, i * SIDE + SIDE - 1] = 1
    return out.astype(ml_dtypes.bfloat16)


def tap_matrices():
    whole = np.zeros((TAPS, PIX + CH, PIX), np.float32)
    for t in range(TAPS):
        for y in range(SIDE):
            for x in range(SIDE):
                u, v = y + t // 3, x + t % 3
                if u == 0:
                    k = PIX + v
                elif u == SIDE + 1:
                    k = PIX + SIDE + 2 + v
                elif v == 0:
                    k = PIX + 2 * SIDE + 4 + u - 1
                elif v == SIDE + 1:
                    k = PIX + 3 * SIDE + 4 + u - 1
                else:
                    k = (u - 1) * SIDE + v - 1
                whole[t, k, y * SIDE + x] = 1
    rim = [p for p in range(PIX) if p // SIDE in (0, SIDE - 1) or p % SIDE in (0, SIDE - 1)]
    inner = whole[:, :PIX].copy()
    inner[:, :, rim] = 0
    outer = np.zeros((PIX + CH, 640), np.float32)
    for t in range(TAPS):
        outer[:, t * RIM : t * RIM + len(rim)] = whole[t][:, rim]
    return inner.astype(ml_dtypes.bfloat16), outer.astype(ml_dtypes.bfloat16)


def edges_kernel(index_ref, fields_ref, pick_ref, copies_ref, own_ref):
    subs = fields_ref.shape[1]
    for s in range(2):
        for f in range(subs):
            x = fields_ref[index_ref[s], f]
            u = s * subs + f
            own_ref[u * CH : (u + 1) * CH, :] = x
            edges = lax.dot_general(pick_ref[...], x, NT, preferred_element_type=jnp.float32)
            edges = edges.astype(jnp.bfloat16)
            for d in range(copies_ref.shape[0]):
                copies_ref[d, u * 4 * SIDE : (u + 1) * 4 * SIDE, :] = edges


def inner_kernel(core_ref, own_ref, other_ref, taps_ref, gram_ref, patches):
    half = own_ref.shape[0] // CH
    for t in range(TAPS):
        for n, ref in enumerate((own_ref, other_ref)):
            values = jnp.dot(ref[...], taps_ref[t], preferred_element_type=jnp.float32)
            values = values.astype(jnp.bfloat16)
            for m in range(half):
                u = n * half + m
                patches[t * CH : (t + 1) * CH, u * PIX : (u + 1) * PIX] = values[m * CH : (m + 1) * CH, :]
    right = patches[pl.ds(pl.multiple_of(core_ref[0] * HALF, HALF), HALF), :]
    for t in range(0, TAPS, 3):
        rows = slice(t * CH, (t + 3) * CH)
        block = lax.dot_general(patches[rows, :], right, NT, preferred_element_type=jnp.float32)
        for l in range(4):
            gram_ref[l, rows, :] = block[:, l * CH : (l + 1) * CH]
        gram_ref[4, rows, : CH // 2] = block[:, 4 * CH :]


def outer_kernel(
    subs,
    core_ref,
    halo_own_ref,
    halo_other_ref,
    own_ref,
    other_ref,
    table_own_ref,
    table_other_ref,
    halo_rows_own_ref,
    halo_rows_other_ref,
    taps_ref,
    mask_ref,
    inner_ref,
    message_ref,
    tiles,
    grid,
    patches,
    gram,
    position,
):
    core = core_ref[0]
    units = 4 * subs
    half = units // 2

    for side, halo_ref in enumerate((halo_own_ref, halo_other_ref)):
        for f in range(subs):
            for n, at in enumerate(SIDE_AT + CORNER_AT):
                index = halo_ref[f, at]
                sub = index // (4 * SIDE)
                edge = lax.rem(index // SIDE, 4)
                device = sub // subs
                local = sub - device * subs
                near = lax.rem(device, 2) == core
                for s in range(2):
                    row = pl.multiple_of((s * subs + local) * 4 * SIDE + edge * SIDE, SIDE)
                    mine = table_own_ref[device // 2, pl.ds(row, SIDE), :]
                    theirs = table_other_ref[device // 2, pl.ds(row, SIDE), :]
                    u = side * half + s * subs + f
                    tiles[u * CH + n * SIDE : u * CH + (n + 1) * SIDE, :] = jnp.where(near, mine, theirs)

    lane = lax.broadcasted_iota(jnp.int32, (8, CH), 1)
    base = jnp.full((8, CH), -1000, jnp.int32)
    for e, at in enumerate(SIDE_AT):
        base = jnp.where((lane >= at) & (lane < at + SIDE), e * SIDE, base)
    for e, at in enumerate(CORNER_AT):
        base = jnp.where(lane == at, (4 + e) * SIDE, base)
    position[...] = jnp.zeros((8, CH), jnp.int32)
    position[0:subs, 0:CYCLE] = lax.rem(halo_rows_own_ref[...], SIDE)
    position[subs : 2 * subs, 0:CYCLE] = lax.rem(halo_rows_other_ref[...], SIDE)
    source = position[...] + base

    row_at = lax.broadcasted_iota(jnp.int32, (CH, CH), 0)
    col_at = lax.broadcasted_iota(jnp.int32, (CH, CH), 1)
    diagonal = row_at == col_at
    eye = jnp.where(diagonal, 1.0, 0.0).astype(jnp.bfloat16)
    turned = lax.dot_general(eye, tiles[...], NT, preferred_element_type=jnp.float32).astype(jnp.bfloat16)
    largest = jnp.zeros((CH, CH), jnp.float32)
    for u in range(units):
        side, f = u // half, u % half % subs
        at = side * subs + f
        pick = jnp.where(row_at == source[at : at + 1, :], 1.0, 0.0).astype(jnp.bfloat16)
        cycle = jnp.dot(turned[:, u * CH : (u + 1) * CH], pick, preferred_element_type=jnp.float32)
        x = (own_ref if side == 0 else other_ref)[(u % half) * CH : (u % half + 1) * CH, :]
        grid[u * CH : (u + 1) * CH, :PIX] = x
        grid[u * CH : (u + 1) * CH, PIX:] = cycle.astype(jnp.bfloat16)
        size = jnp.abs(x.astype(jnp.float32))
        largest = jnp.maximum(largest, jnp.maximum(size[:, :CH], size[:, CH:]))
        largest = jnp.maximum(largest, jnp.abs(cycle))

    kept = mask_ref[...].astype(jnp.float32)
    kept_row = jnp.sum(jnp.where(diagonal, kept, 0.0), axis=1, keepdims=True)
    turned_kept = pltpu.roll(jnp.broadcast_to(kept, (8, CH)), CH // 2, 1)
    kept = jnp.broadcast_to(kept, (8, CH))
    first, second = jnp.where(core == 0, kept, turned_kept), jnp.where(core == 0, turned_kept, kept)
    folded = jnp.where(lane < CH // 2, first, second)
    kept_lane = jnp.where(lax.broadcasted_iota(jnp.int32, (8, CH), 0) == 0, first, folded)

    def exponent(values):
        top = jnp.maximum(jnp.max(values), 2.0**-60)
        return jnp.ceil(jnp.log2(jnp.full((8, CH), top, jnp.float32)))

    kept_exp = exponent(jnp.where(kept_row > 0, largest, 0.0))
    any_exp = exponent(largest)
    row_scale = jnp.where(kept_row > 0, jnp.exp2(-kept_exp[0:1, :]), 0.0)
    lane_exps = jnp.where(kept_lane > 0, kept_exp, any_exp)
    lane_scale = jnp.exp2(-lane_exps)

    chunk = units * CH // 3
    for m in range(0, units * CH, chunk):
        values = jnp.dot(grid[m : m + chunk, :], taps_ref[...], preferred_element_type=jnp.float32)
        values = values.astype(jnp.bfloat16)
        for n in range(chunk // CH):
            u = m // CH + n
            for t in range(TAPS):
                part = values[n * CH : (n + 1) * CH, t * RIM : (t + 1) * RIM]
                patches[t * CH : (t + 1) * CH, u * RIM : (u + 1) * RIM] = part

    right = patches[pl.ds(pl.multiple_of(core * HALF, HALF), HALF), :]
    for t in range(0, TAPS, 3):
        block = lax.dot_general(
            patches[t * CH : (t + 3) * CH, :], right, NT, preferred_element_type=jnp.float32
        )
        for n in range(3):
            rows = block[n * CH : (n + 1) * CH, :]
            at = slice((t + n) * CH, (t + n + 1) * CH)
            for l in range(4):
                part = rows[:, l * CH : (l + 1) * CH] + inner_ref[l, at, :]
                gram[l, at, :] = part * row_scale * lane_scale[0:1, :]
            part = rows[:, 4 * CH :] + inner_ref[4, at, : CH // 2]
            gram[4, at, : CH // 2] = part * row_scale[:, : CH // 2] * lane_scale[1:2, : CH // 2]

    for g in range(8):
        for s in range(8):
            j = g * 8 + s
            at = g * 144 + s * 9
            for c in range(2):
                for l in range(4):
                    to = (c * 4 + l) * 9
                    message_ref[j, to : to + 9, :] = gram[l, at + c * 72 : at + c * 72 + 9, :]
                message_ref[j, 72:81, c * 64 : (c + 1) * 64] = gram[4, at + c * 72 : at + c * 72 + 9, : CH // 2]
            message_ref[j, 81:88, :] = (lane_exps + kept_exp)[0:7, :]


def rows_kernel(place_ref, mask_ref, near_ref, far_ref, weight_ref, kept_ref, out_ref, rows, split):
    core, owner = place_ref[0], place_ref[1]
    near, far = near_ref[...], far_ref[...]
    low = jnp.where(core == 0, near, far)
    high = jnp.where(core == 0, far, near)

    def mine(values, l):
        return jnp.where(core == 0, values[l * 9 : l * 9 + 9, :], values[(4 + l) * 9 : (4 + l) * 9 + 9, :])

    def middle(values):
        return jnp.where(core == 0, values[72:81, : CH // 2], values[72:81, CH // 2 :])

    rows[...] = jnp.zeros_like(rows)
    for l in range(4):
        rows[0:9, l * CH : (l + 1) * CH] = mine(low, l)
        rows[0:9, HALF + l * CH : HALF + (l + 1) * CH] = mine(high, l)
    rows[0:9, 4 * CH : HALF] = middle(low)
    rows[0:9, HALF + 4 * CH :] = middle(high)

    at = lax.broadcasted_iota(jnp.int32, (16, CH), 0)
    keep = jnp.zeros((16, CH), jnp.float32)
    for k in range(9):
        bit = mask_ref[lax.rem(owner * 9 + k, CH)]
        keep = jnp.where(at == k, bit.astype(jnp.float32), keep)
    whole = rows[...]
    head = whole.astype(jnp.bfloat16)
    left = whole - head.astype(jnp.float32)
    tail = left.astype(jnp.bfloat16)
    split[0:16, :] = head
    split[16:32, :] = tail
    split[32:48, :] = (left - tail.astype(jnp.float32)).astype(jnp.bfloat16)
    product = jnp.dot(split[...], weight_ref[...], preferred_element_type=jnp.float32)
    product = product[32:48, :] + product[16:32, :] + product[0:16, :]
    count = place_ref[2].astype(jnp.float32)
    kept = kept_ref[...] > 0
    for t in range(TAPS):
        part = whole[:, t * CH : (t + 1) * CH]
        part = jnp.where((keep > 0) & kept, part / count, 0.0)
        out_ref[:, t * CH : (t + 1) * CH] = part[0:9, :]
    for n in range(2):
        part = product[:, n * CH : (n + 1) * CH]
        part = jnp.where(keep > 0, part / count, 0.0)
        out_ref[:, K + n * CH : K + (n + 1) * CH] = part[0:9, :]


VMEM = pl.BlockSpec(memory_space=pltpu.VMEM)
SMEM = pl.BlockSpec(memory_space=pltpu.SMEM)


def shape(dims, kind):
    return jax.ShapeDtypeStruct(dims, kind)


def per_device(fields, sample_index, halo_index, channel_mask, weight):
    faces, samples = lax.axis_size("face"), lax.axis_size("sample")
    face, sample = lax.axis_index("face"), lax.axis_index("sample")
    core = lax.rem(face, 2)
    subs = fields.shape[1]
    units = 4 * subs
    swap = [(f, f ^ 1) for f in range(faces)]
    bf16, f32 = jnp.bfloat16, jnp.float32

    copies, own = pl.pallas_call(
        edges_kernel,
        out_shape=(shape((faces // 2, 8 * subs * SIDE, CH), bf16), shape((units // 2 * CH, PIX), bf16)),
        in_specs=[SMEM, VMEM, VMEM],
        out_specs=(VMEM, VMEM),
        name="edges",
    )(sample_index, fields, jnp.asarray(edge_picker()))

    other = lax.ppermute(own, "face", swap)
    halo_other = lax.ppermute(halo_index, "face", swap)
    same_core = [[f for f in range(c, faces, 2)] for c in range(2)]
    table = lax.all_to_all(copies, "face", 0, 0, axis_index_groups=same_core)
    table_other = lax.ppermute(table, "face", swap)

    mask_row = channel_mask[None]
    place = jnp.stack([core, face * samples + sample, jnp.int32(2 * subs * PIX * faces * samples)])
    inner_taps, outer_taps = tap_matrices()
    limit = pltpu.CompilerParams(vmem_limit_bytes=56 * 2**20)

    inner = pl.pallas_call(
        inner_kernel,
        out_shape=shape((5, K, CH), f32),
        in_specs=[SMEM] + [VMEM] * 3,
        out_specs=VMEM,
        scratch_shapes=[pltpu.VMEM((K, units * PIX), bf16)],
        compiler_params=limit,
        cost_estimate=pl.CostEstimate(flops=6 * 10**9, bytes_accessed=5 * 10**6, transcendentals=0),
        name="inner",
    )(place, own, other, jnp.asarray(inner_taps))

    message = pl.pallas_call(
        functools.partial(outer_kernel, subs),
        out_shape=shape((64, ROWS, CH), f32),
        in_specs=[SMEM] * 3 + [VMEM] * 9,
        out_specs=VMEM,
        scratch_shapes=[
            pltpu.VMEM((units * CH, CH), bf16),
            pltpu.VMEM((units * CH, PIX + CH), bf16),
            pltpu.VMEM((K, units * RIM), bf16),
            pltpu.VMEM((5, K, CH), f32),
            pltpu.VMEM((8, CH), jnp.int32),
        ],
        compiler_params=limit,
        name="outer",
    )(
        place,
        halo_index,
        halo_other,
        own,
        other,
        table,
        table_other,
        halo_index,
        halo_other,
        jnp.asarray(outer_taps),
        mask_row,
        inner,
    )

    groups = [[f * samples + s for f in range(c, faces, 2) for s in range(samples)] for c in range(2)]
    landed = lax.all_to_all(message.astype(jnp.float16), AXES, 0, 0, axis_index_groups=groups)
    landed = landed.astype(f32)
    exps = jnp.where(jnp.arange(ROWS)[None, :, None] < 72, landed[:, 81:82, :], landed[:, 82:83, :])
    near = jnp.sum(landed * jnp.exp2(exps), axis=0)
    far = lax.ppermute(near, "face", swap)

    return pl.pallas_call(
        rows_kernel,
        out_shape=shape((TAPS, K + weight.shape[1]), f32),
        in_specs=[SMEM] * 2 + [VMEM] * 4,
        out_specs=VMEM,
        scratch_shapes=[pltpu.VMEM((16, K), f32), pltpu.VMEM((48, K), bf16)],
        name="rows",
    )(place, channel_mask, near, far, weight, mask_row)


def solution(mesh):
    placed = (P("sample", "face", None, None), P("sample"), P("face", None), P(), P())
    return jax.shard_map(
        per_device,
        mesh=mesh,
        in_specs=placed,
        out_specs=P(("face", "sample"), None),
        check_vma=False,
    )
```

```python
import functools

import jax
import jax.numpy as jnp
import ml_dtypes
import numpy as np
from jax import lax
from jax.experimental import pallas as pl
from jax.experimental.pallas import tpu as pltpu
from jax.sharding import PartitionSpec as P

SIDE = 16
PIX = SIDE * SIDE
CH = 128
TAPS = 9
K = TAPS * CH
HALF = K // 2
CYCLE = 4 * SIDE + 4
RIM = 64
ROWS = 88
STEPS = 16
TOP = 32700.0
AXES = ("face", "sample")
NT = (((1,), (1,)), ((), ()))
SIDE_AT = (1, 19, 36, 52)
CORNER_AT = (0, 17, 18, 35)


def edge_picker():
    out = np.zeros((4 * SIDE, PIX), np.float32)
    for i in range(SIDE):
        out[i, i] = 1
        out[SIDE + i, (SIDE - 1) * SIDE + i] = 1
        out[2 * SIDE + i, i * SIDE] = 1
        out[3 * SIDE + i, i * SIDE + SIDE - 1] = 1
    return out.astype(ml_dtypes.bfloat16)


def tap_matrices():
    whole = np.zeros((TAPS, PIX + CH, PIX), np.float32)
    for t in range(TAPS):
        for y in range(SIDE):
            for x in range(SIDE):
                u, v = y + t // 3, x + t % 3
                if u == 0:
                    k = PIX + v
                elif u == SIDE + 1:
                    k = PIX + SIDE + 2 + v
                elif v == 0:
                    k = PIX + 2 * SIDE + 4 + u - 1
                elif v == SIDE + 1:
                    k = PIX + 3 * SIDE + 4 + u - 1
                else:
                    k = (u - 1) * SIDE + v - 1
                whole[t, k, y * SIDE + x] = 1
    rim = [p for p in range(PIX) if p // SIDE in (0, SIDE - 1) or p % SIDE in (0, SIDE - 1)]
    inner = whole[:, :PIX].copy()
    inner[:, :, rim] = 0
    outer = np.zeros((PIX + CH, 640), np.float32)
    for t in range(TAPS):
        outer[:, t * RIM : t * RIM + len(rim)] = whole[t][:, rim]
    return inner.astype(ml_dtypes.bfloat16), outer.astype(ml_dtypes.bfloat16)


def edges_kernel(index_ref, fields_ref, pick_ref, copies_ref):
    subs = fields_ref.shape[1]
    for s in range(2):
        for f in range(subs):
            x = fields_ref[index_ref[s], f]
            u = s * subs + f
            edges = lax.dot_general(pick_ref[...], x, NT, preferred_element_type=jnp.float32)
            edges = edges.astype(jnp.bfloat16)
            for d in range(copies_ref.shape[0]):
                copies_ref[d, u * 4 * SIDE : (u + 1) * 4 * SIDE, :] = edges


def inner_kernel(core_ref, index_ref, own_ref, other_ref, taps_ref, gram_ref, patches):
    subs = own_ref.shape[1]
    for t in range(TAPS):
        for n, ref in enumerate((own_ref, other_ref)):
            for s in range(2):
                x = ref[index_ref[s]].reshape(subs * CH, PIX)
                values = jnp.dot(x, taps_ref[t], preferred_element_type=jnp.float32)
                values = values.astype(jnp.bfloat16)
                for f in range(subs):
                    u = (n * 2 + s) * subs + f
                    patches[t * CH : (t + 1) * CH, u * PIX : (u + 1) * PIX] = values[f * CH : (f + 1) * CH, :]
    right = patches[pl.ds(pl.multiple_of(core_ref[0] * HALF, HALF), HALF), :]
    for t in range(0, TAPS, 3):
        rows = slice(t * CH, (t + 3) * CH)
        block = lax.dot_general(patches[rows, :], right, NT, preferred_element_type=jnp.float32)
        for l in range(4):
            gram_ref[l, rows, :] = block[:, l * CH : (l + 1) * CH]
        gram_ref[4, rows, : CH // 2] = block[:, 4 * CH :]


def outer_kernel(
    subs,
    core_ref,
    index_ref,
    halo_own_ref,
    halo_other_ref,
    own_ref,
    other_ref,
    table_own_ref,
    table_other_ref,
    halo_rows_own_ref,
    halo_rows_other_ref,
    taps_ref,
    mask_ref,
    inner_ref,
    message_ref,
    tiles,
    grid,
    patches,
    gram,
    position,
    stage,
):
    core = core_ref[0]
    units = 4 * subs
    half = units // 2

    for side, halo_ref in enumerate((halo_own_ref, halo_other_ref)):
        for f in range(subs):
            for n, at in enumerate(SIDE_AT + CORNER_AT):
                index = halo_ref[f, at]
                sub = index // (4 * SIDE)
                edge = lax.rem(index // SIDE, 4)
                device = sub // subs
                local = sub - device * subs
                near = lax.rem(device, 2) == core
                for s in range(2):
                    row = pl.multiple_of((s * subs + local) * 4 * SIDE + edge * SIDE, SIDE)
                    mine = table_own_ref[device // 2, pl.ds(row, SIDE), :]
                    theirs = table_other_ref[device // 2, pl.ds(row, SIDE), :]
                    u = side * half + s * subs + f
                    tiles[u * CH + n * SIDE : u * CH + (n + 1) * SIDE, :] = jnp.where(near, mine, theirs)

    lane = lax.broadcasted_iota(jnp.int32, (8, CH), 1)
    base = jnp.full((8, CH), -1000, jnp.int32)
    for e, at in enumerate(SIDE_AT):
        base = jnp.where((lane >= at) & (lane < at + SIDE), e * SIDE, base)
    for e, at in enumerate(CORNER_AT):
        base = jnp.where(lane == at, (4 + e) * SIDE, base)
    position[...] = jnp.zeros((8, CH), jnp.int32)
    position[0:subs, 0:CYCLE] = lax.rem(halo_rows_own_ref[...], SIDE)
    position[subs : 2 * subs, 0:CYCLE] = lax.rem(halo_rows_other_ref[...], SIDE)
    source = position[...] + base

    row_at = lax.broadcasted_iota(jnp.int32, (CH, CH), 0)
    col_at = lax.broadcasted_iota(jnp.int32, (CH, CH), 1)
    diagonal = row_at == col_at
    eye = jnp.where(diagonal, 1.0, 0.0).astype(jnp.bfloat16)
    turned = lax.dot_general(eye, tiles[...], NT, preferred_element_type=jnp.float32).astype(jnp.bfloat16)
    energy = jnp.zeros((CH, CH), jnp.float32)
    for u in range(units):
        side, f = u // half, u % half % subs
        at = side * subs + f
        pick = jnp.where(row_at == source[at : at + 1, :], 1.0, 0.0).astype(jnp.bfloat16)
        cycle = jnp.dot(turned[:, u * CH : (u + 1) * CH], pick, preferred_element_type=jnp.float32)
        x = (own_ref if side == 0 else other_ref)[index_ref[u % half // subs], f]
        grid[u * CH : (u + 1) * CH, :PIX] = x
        grid[u * CH : (u + 1) * CH, PIX:] = cycle.astype(jnp.bfloat16)
        x = x.astype(jnp.float32)
        energy += x[:, :CH] * x[:, :CH] + x[:, CH:] * x[:, CH:] + cycle * cycle
    kept = mask_ref[...].astype(jnp.float32)
    kept_row = jnp.sum(jnp.where(diagonal, kept, 0.0), axis=1, keepdims=True)
    turned_kept = pltpu.roll(jnp.broadcast_to(kept, (8, CH)), CH // 2, 1)
    kept = jnp.broadcast_to(kept, (8, CH))
    first, second = jnp.where(core == 0, kept, turned_kept), jnp.where(core == 0, turned_kept, kept)
    folded = jnp.where(lane < CH // 2, first, second)
    kept_lane = jnp.where(lax.broadcasted_iota(jnp.int32, (8, CH), 0) == 0, first, folded)

    energy = jnp.sum(energy, axis=1, keepdims=True)

    def exponent(values):
        top = jnp.full((8, CH), jnp.maximum(jnp.max(values), 2.0**-120), jnp.float32)
        return jnp.ceil(jnp.log2(top) * (STEPS / 2) + 0.1)

    kept_exp = exponent(jnp.where(kept_row > 0, energy, 0.0))
    any_exp = exponent(energy)
    row_scale = jnp.where(kept_row > 0, jnp.exp2(kept_exp[0:1, :] * (-1 / STEPS)), 0.0)
    lane_exps = jnp.where(kept_lane > 0, kept_exp, any_exp)
    lane_scale = jnp.exp2(lane_exps * (-1 / STEPS))

    def coded(values):
        return jnp.round(TOP * values * lax.rsqrt(jnp.maximum(jnp.abs(values), 1e-30)))

    chunk = units * CH // 3
    for m in range(0, units * CH, chunk):
        values = jnp.dot(grid[m : m + chunk, :], taps_ref[...], preferred_element_type=jnp.float32)
        values = values.astype(jnp.bfloat16)
        for n in range(chunk // CH):
            u = m // CH + n
            for t in range(TAPS):
                part = values[n * CH : (n + 1) * CH, t * RIM : (t + 1) * RIM]
                patches[t * CH : (t + 1) * CH, u * RIM : (u + 1) * RIM] = part

    right = patches[pl.ds(pl.multiple_of(core * HALF, HALF), HALF), :]
    for t in range(0, TAPS, 3):
        block = lax.dot_general(
            patches[t * CH : (t + 3) * CH, :], right, NT, preferred_element_type=jnp.float32
        )
        for n in range(3):
            rows = block[n * CH : (n + 1) * CH, :]
            at = slice((t + n) * CH, (t + n + 1) * CH)
            for l in range(4):
                part = rows[:, l * CH : (l + 1) * CH] + inner_ref[l, at, :]
                gram[l, at, :] = coded(part * row_scale * lane_scale[0:1, :])
            part = rows[:, 4 * CH :] + inner_ref[4, at, : CH // 2]
            gram[4, at, : CH // 2] = coded(part * row_scale[:, : CH // 2] * lane_scale[1:2, : CH // 2])

    for j in range(64):
        at = j // 8 * 144 + j % 8 * 9
        block = stage.at[j % 4]
        for c in range(2):
            rows = slice(at + c * 72, at + c * 72 + 9)
            for l in range(4):
                to = (c * 4 + l) * 9
                block[to : to + 9, :] = gram[l, rows, :]
            block[72:81, c * 64 : (c + 1) * 64] = gram[4, rows, : CH // 2]
        block[81:88, :] = (lane_exps + kept_exp)[0:7, :]
        message_ref[j] = block[...].astype(jnp.int32).astype(jnp.int16)


def rows_kernel(place_ref, mask_ref, near_ref, far_ref, weight_ref, kept_ref, out_ref, rows, split):
    core, owner = place_ref[0], place_ref[1]
    near, far = near_ref[...], far_ref[...]
    low = jnp.where(core == 0, near, far)
    high = jnp.where(core == 0, far, near)

    def mine(values, l):
        return jnp.where(core == 0, values[l * 9 : l * 9 + 9, :], values[(4 + l) * 9 : (4 + l) * 9 + 9, :])

    def middle(values):
        return jnp.where(core == 0, values[72:81, : CH // 2], values[72:81, CH // 2 :])

    rows[...] = jnp.zeros_like(rows)
    for l in range(4):
        rows[0:9, l * CH : (l + 1) * CH] = mine(low, l)
        rows[0:9, HALF + l * CH : HALF + (l + 1) * CH] = mine(high, l)
    rows[0:9, 4 * CH : HALF] = middle(low)
    rows[0:9, HALF + 4 * CH :] = middle(high)

    at = lax.broadcasted_iota(jnp.int32, (16, CH), 0)
    keep = jnp.zeros((16, CH), jnp.float32)
    for k in range(9):
        bit = mask_ref[lax.rem(owner * 9 + k, CH)]
        keep = jnp.where(at == k, bit.astype(jnp.float32), keep)
    whole = rows[...]
    head = whole.astype(jnp.bfloat16)
    left = whole - head.astype(jnp.float32)
    tail = left.astype(jnp.bfloat16)
    split[0:16, :] = head
    split[16:32, :] = tail
    split[32:48, :] = (left - tail.astype(jnp.float32)).astype(jnp.bfloat16)
    product = jnp.dot(split[...], weight_ref[...], preferred_element_type=jnp.float32)
    product = product[32:48, :] + product[16:32, :] + product[0:16, :]
    count = place_ref[2].astype(jnp.float32)
    kept = kept_ref[...] > 0
    for t in range(TAPS):
        part = whole[:, t * CH : (t + 1) * CH]
        part = jnp.where((keep > 0) & kept, part / count, 0.0)
        out_ref[:, t * CH : (t + 1) * CH] = part[0:9, :]
    for n in range(2):
        part = product[:, n * CH : (n + 1) * CH]
        part = jnp.where(keep > 0, part / count, 0.0)
        out_ref[:, K + n * CH : K + (n + 1) * CH] = part[0:9, :]


VMEM = pl.BlockSpec(memory_space=pltpu.VMEM)
SMEM = pl.BlockSpec(memory_space=pltpu.SMEM)


def shape(dims, kind):
    return jax.ShapeDtypeStruct(dims, kind)


def per_device(fields, sample_index, halo_index, channel_mask, weight):
    faces, samples = lax.axis_size("face"), lax.axis_size("sample")
    face, sample = lax.axis_index("face"), lax.axis_index("sample")
    core = lax.rem(face, 2)
    subs = fields.shape[1]
    units = 4 * subs
    swap = [(f, f ^ 1) for f in range(faces)]
    bf16, f32 = jnp.bfloat16, jnp.float32

    other = lax.ppermute(fields, "face", swap)
    halo_other = lax.ppermute(halo_index, "face", swap)
    copies = pl.pallas_call(
        edges_kernel,
        out_shape=shape((faces // 2, 8 * subs * SIDE, CH), bf16),
        in_specs=[SMEM, VMEM, VMEM],
        out_specs=VMEM,
        name="edges",
    )(sample_index, fields, jnp.asarray(edge_picker()))

    copies, other, halo_other = lax.optimization_barrier((copies, other, halo_other))
    same_core = [[f for f in range(c, faces, 2)] for c in range(2)]
    table = lax.all_to_all(copies, "face", 0, 0, axis_index_groups=same_core)

    mask_row = channel_mask[None]
    place = jnp.stack([core, face * samples + sample, jnp.int32(2 * subs * PIX * faces * samples)])
    inner_taps, outer_taps = tap_matrices()
    limit = pltpu.CompilerParams(vmem_limit_bytes=28 * 2**20)

    inner = pl.pallas_call(
        inner_kernel,
        out_shape=shape((5, K, CH), f32),
        in_specs=[SMEM] * 2 + [VMEM] * 3,
        out_specs=VMEM,
        scratch_shapes=[pltpu.VMEM((K, units * PIX), bf16)],
        compiler_params=limit,
        cost_estimate=pl.CostEstimate(flops=6 * 10**9, bytes_accessed=5 * 10**6, transcendentals=0),
        name="inner",
    )(place, sample_index, fields, other, jnp.asarray(inner_taps))

    table, inner = lax.optimization_barrier((table, inner))
    table_other = lax.ppermute(table, "face", swap)
    message = pl.pallas_call(
        functools.partial(outer_kernel, subs),
        out_shape=shape((64, ROWS, CH), jnp.int16),
        in_specs=[SMEM] * 4 + [VMEM] * 9,
        out_specs=VMEM,
        scratch_shapes=[
            pltpu.VMEM((units * CH, CH), bf16),
            pltpu.VMEM((units * CH, PIX + CH), bf16),
            pltpu.VMEM((K, units * RIM), bf16),
            pltpu.VMEM((5, K, CH), f32),
            pltpu.VMEM((8, CH), jnp.int32),
            pltpu.VMEM((4, ROWS, CH), f32),
        ],
        compiler_params=limit,
        name="outer",
    )(
        place,
        sample_index,
        halo_index,
        halo_other,
        fields,
        other,
        table,
        table_other,
        halo_index,
        halo_other,
        jnp.asarray(outer_taps),
        mask_row,
        inner,
    )

    groups = [[f * samples + s for f in range(c, faces, 2) for s in range(samples)] for c in range(2)]
    landed = lax.all_to_all(message, AXES, 0, 0, axis_index_groups=groups)
    landed = landed.astype(f32)
    exps = jnp.where(jnp.arange(ROWS)[None, :, None] < 72, landed[:, 81:82, :], landed[:, 82:83, :])
    near = jnp.sum(landed * jnp.abs(landed) * jnp.exp2(exps * (1 / STEPS)), axis=0) * TOP**-2
    far = lax.ppermute(near, "face", swap)

    return pl.pallas_call(
        rows_kernel,
        out_shape=shape((TAPS, K + weight.shape[1]), f32),
        in_specs=[SMEM] * 2 + [VMEM] * 4,
        out_specs=VMEM,
        scratch_shapes=[pltpu.VMEM((16, K), f32), pltpu.VMEM((48, K), bf16)],
        name="rows",
    )(place, channel_mask, near, far, weight, mask_row)


def solution(mesh):
    placed = (P("sample", "face", None, None), P("sample"), P("face", None), P(), P())
    return jax.shard_map(
        per_device,
        mesh=mesh,
        in_specs=placed,
        out_specs=P(("face", "sample"), None),
        check_vma=False,
    )
```

```python
import functools

import jax
import jax.numpy as jnp
import ml_dtypes
import numpy as np
from jax import lax
from jax.experimental import pallas as pl
from jax.experimental.pallas import tpu as pltpu
from jax.sharding import PartitionSpec as P

SIDE = 16
PIX = SIDE * SIDE
CH = 128
TAPS = 9
K = TAPS * CH
HALF = K // 2
CYCLE = 4 * SIDE + 4
RIM = 64
ROWS = 88
STEPS = 16
TOP = 32700.0
AXES = ("face", "sample")
NT = (((1,), (1,)), ((), ()))
SIDE_AT = (1, 19, 36, 52)
CORNER_AT = (0, 17, 18, 35)


def edge_picker():
    out = np.zeros((4 * SIDE, PIX), np.float32)
    for i in range(SIDE):
        out[i, i] = 1
        out[SIDE + i, (SIDE - 1) * SIDE + i] = 1
        out[2 * SIDE + i, i * SIDE] = 1
        out[3 * SIDE + i, i * SIDE + SIDE - 1] = 1
    return out.astype(ml_dtypes.bfloat16)


def rim_matrix():
    whole = np.zeros((TAPS, PIX + CH, PIX), np.float32)
    for t in range(TAPS):
        for y in range(SIDE):
            for x in range(SIDE):
                u, v = y + t // 3, x + t % 3
                if u == 0:
                    k = PIX + v
                elif u == SIDE + 1:
                    k = PIX + SIDE + 2 + v
                elif v == 0:
                    k = PIX + 2 * SIDE + 4 + u - 1
                elif v == SIDE + 1:
                    k = PIX + 3 * SIDE + 4 + u - 1
                else:
                    k = (u - 1) * SIDE + v - 1
                whole[t, k, y * SIDE + x] = 1
    rim = [p for p in range(PIX) if p // SIDE in (0, SIDE - 1) or p % SIDE in (0, SIDE - 1)]
    outer = np.zeros((PIX + CH, 640), np.float32)
    for t in range(TAPS):
        outer[:, t * RIM : t * RIM + len(rim)] = whole[t][:, rim]
    return outer.astype(ml_dtypes.bfloat16)


def edges_kernel(index_ref, fields_ref, pick_ref, copies_ref):
    subs = fields_ref.shape[1]
    for s in range(2):
        for f in range(subs):
            x = fields_ref[index_ref[s], f]
            u = s * subs + f
            edges = lax.dot_general(pick_ref[...], x, NT, preferred_element_type=jnp.float32)
            edges = edges.astype(jnp.bfloat16)
            for d in range(copies_ref.shape[0]):
                copies_ref[d, u * 4 * SIDE : (u + 1) * 4 * SIDE, :] = edges


def row_blocks():
    return [slice(t * CH, (t + 3) * CH) for t in range(0, TAPS, 3)]


def inner_kernel(core_ref, index_ref, own_ref, other_ref, gram_ref, done_ref, patches, gram, sems):
    subs = own_ref.shape[1]
    done_ref[...] = jnp.zeros_like(done_ref)
    pixel = lax.broadcasted_iota(jnp.int32, (PIX, PIX), 1)
    ahead = lax.broadcasted_iota(jnp.int32, (PIX, PIX), 0) - pixel
    y, x = pixel // SIDE, pixel % SIDE
    inside = (y > 0) & (y < SIDE - 1) & (x > 0) & (x < SIDE - 1)
    ahead = jnp.where(inside, ahead, PIX)
    for t in range(TAPS):
        shift = (t // 3 - 1) * SIDE + t % 3 - 1
        tap = jnp.where(ahead == shift, 1.0, 0.0).astype(jnp.bfloat16)
        for n, ref in enumerate((own_ref, other_ref)):
            for s in range(2):
                x = ref[index_ref[s]].reshape(subs * CH, PIX)
                values = jnp.dot(x, tap, preferred_element_type=jnp.float32)
                values = values.astype(jnp.bfloat16)
                for f in range(subs):
                    u = (n * 2 + s) * subs + f
                    patches[t * CH : (t + 1) * CH, u * PIX : (u + 1) * PIX] = values[f * CH : (f + 1) * CH, :]
    right = patches[pl.ds(pl.multiple_of(core_ref[0] * HALF, HALF), HALF), :]
    copies = []
    for n, rows in enumerate(row_blocks()):
        block = lax.dot_general(patches[rows, :], right, NT, preferred_element_type=jnp.float32)
        for l in range(4):
            gram[l, rows, :] = block[:, l * CH : (l + 1) * CH]
        gram[4, rows, : CH // 2] = block[:, 4 * CH :]
        gram[4, rows, CH // 2 :] = jnp.zeros((3 * CH, CH // 2), jnp.float32)
        copies.append(pltpu.make_async_copy(gram.at[:, rows, :], gram_ref.at[:, rows, :], sems.at[n]))
        copies[-1].start()
    for copy in copies:
        copy.wait()


def gather_kernel(subs, core_ref, halo_own_ref, halo_other_ref, table_ref, after_ref, tiles_ref):
    core = core_ref[0]
    for side, halo_ref in enumerate((halo_own_ref, halo_other_ref)):
        for f in range(subs):
            for n, at in enumerate(SIDE_AT + CORNER_AT):
                index = halo_ref[f, at]
                sub = index // (4 * SIDE)
                edge = lax.rem(index // SIDE, 4)
                device = sub // subs
                local = sub - device * subs
                near = lax.rem(device, 2) == core
                for s in range(2):
                    row = pl.multiple_of((s * subs + local) * 4 * SIDE + edge * SIDE, SIDE)
                    tile = table_ref[device // 2, pl.ds(row, SIDE), :]
                    u = (side * 2 + s) * subs + f
                    tiles_ref[u * CH + n * SIDE : u * CH + (n + 1) * SIDE, :] = jnp.where(near, tile, jnp.zeros_like(tile))


def outer_kernel(
    subs,
    core_ref,
    index_ref,
    own_ref,
    other_ref,
    tiles_own_ref,
    tiles_other_ref,
    halo_rows_own_ref,
    halo_rows_other_ref,
    taps_ref,
    mask_ref,
    inner_ref,
    message_ref,
    grid,
    patches,
    gram,
    position,
    stage,
    inner,
    sems,
):
    core = core_ref[0]
    units = 4 * subs
    half = units // 2
    copies = []
    for n, rows in enumerate(row_blocks()):
        copies.append(pltpu.make_async_copy(inner_ref.at[:, rows, :], inner.at[:, rows, :], sems.at[n]))
        copies[-1].start()

    lane = lax.broadcasted_iota(jnp.int32, (8, CH), 1)
    base = jnp.full((8, CH), -1000, jnp.int32)
    for e, at in enumerate(SIDE_AT):
        base = jnp.where((lane >= at) & (lane < at + SIDE), e * SIDE, base)
    for e, at in enumerate(CORNER_AT):
        base = jnp.where(lane == at, (4 + e) * SIDE, base)
    position[...] = jnp.zeros((8, CH), jnp.int32)
    position[0:subs, 0:CYCLE] = lax.rem(halo_rows_own_ref[...], SIDE)
    position[subs : 2 * subs, 0:CYCLE] = lax.rem(halo_rows_other_ref[...], SIDE)
    source = position[...] + base

    row_at = lax.broadcasted_iota(jnp.int32, (CH, CH), 0)
    col_at = lax.broadcasted_iota(jnp.int32, (CH, CH), 1)
    diagonal = row_at == col_at
    eye = jnp.where(diagonal, 1.0, 0.0).astype(jnp.bfloat16)
    split = units * CH // 2
    turned = []
    for mine, theirs in ((0, split), (split, 0)):
        tiles = tiles_own_ref[mine : mine + split, :] + tiles_other_ref[theirs : theirs + split, :]
        tiles = lax.dot_general(eye, tiles, NT, preferred_element_type=jnp.float32)
        turned.append(tiles.astype(jnp.bfloat16))
    energy = jnp.zeros((CH, CH), jnp.float32)
    for u in range(units):
        side, f = u // half, u % half % subs
        at = side * subs + f
        pick = jnp.where(row_at == source[at : at + 1, :], 1.0, 0.0).astype(jnp.bfloat16)
        cycle = jnp.dot(turned[side][:, u % half * CH : (u % half + 1) * CH], pick, preferred_element_type=jnp.float32)
        x = (own_ref if side == 0 else other_ref)[index_ref[u % half // subs], f]
        grid[u * CH : (u + 1) * CH, :PIX] = x
        grid[u * CH : (u + 1) * CH, PIX:] = cycle.astype(jnp.bfloat16)
        x = x.astype(jnp.float32)
        energy += x[:, :CH] * x[:, :CH] + x[:, CH:] * x[:, CH:] + cycle * cycle
    kept = mask_ref[...].astype(jnp.float32)
    kept_row = jnp.sum(jnp.where(diagonal, kept, 0.0), axis=1, keepdims=True)
    turned_kept = pltpu.roll(jnp.broadcast_to(kept, (8, CH)), CH // 2, 1)
    kept = jnp.broadcast_to(kept, (8, CH))
    first, second = jnp.where(core == 0, kept, turned_kept), jnp.where(core == 0, turned_kept, kept)
    folded = jnp.where(lane < CH // 2, first, second)
    kept_lane = jnp.where(lax.broadcasted_iota(jnp.int32, (8, CH), 0) == 0, first, folded)

    energy = jnp.sum(energy, axis=1, keepdims=True)

    def exponent(values):
        top = jnp.full((8, CH), jnp.maximum(jnp.max(values), 2.0**-120), jnp.float32)
        return jnp.ceil(jnp.log2(top) * (STEPS / 2) + 0.1)

    kept_exp = exponent(jnp.where(kept_row > 0, energy, 0.0))
    any_exp = exponent(energy)
    row_scale = jnp.where(kept_row > 0, jnp.exp2(kept_exp[0:1, :] * (-1 / STEPS)), 0.0)
    lane_exps = jnp.where(kept_lane > 0, kept_exp, any_exp)
    lane_scale = jnp.exp2(lane_exps * (-1 / STEPS))

    def coded(values):
        return jnp.round(TOP * values * lax.rsqrt(jnp.maximum(jnp.abs(values), 1e-30)))

    chunk = units * CH // 3
    for m in range(0, units * CH, chunk):
        values = jnp.dot(grid[m : m + chunk, :], taps_ref[...], preferred_element_type=jnp.float32)
        values = values.astype(jnp.bfloat16)
        for n in range(chunk // CH):
            u = m // CH + n
            for t in range(TAPS):
                part = values[n * CH : (n + 1) * CH, t * RIM : (t + 1) * RIM]
                patches[t * CH : (t + 1) * CH, u * RIM : (u + 1) * RIM] = part

    right = patches[pl.ds(pl.multiple_of(core * HALF, HALF), HALF), :]
    for t in range(0, TAPS, 3):
        block = lax.dot_general(
            patches[t * CH : (t + 3) * CH, :], right, NT, preferred_element_type=jnp.float32
        )
        copies[t // 3].wait()
        for n in range(3):
            rows = block[n * CH : (n + 1) * CH, :]
            at = slice((t + n) * CH, (t + n + 1) * CH)
            for l in range(4):
                part = rows[:, l * CH : (l + 1) * CH] + inner[l, at, :]
                gram[l, at, :] = coded(part * row_scale * lane_scale[0:1, :])
            part = rows[:, 4 * CH :] + inner[4, at, : CH // 2]
            gram[4, at, : CH // 2] = coded(part * row_scale[:, : CH // 2] * lane_scale[1:2, : CH // 2])

    for j in range(64):
        at = j // 8 * 144 + j % 8 * 9
        block = stage.at[j % 4]
        for c in range(2):
            rows = slice(at + c * 72, at + c * 72 + 9)
            for l in range(4):
                to = (c * 4 + l) * 9
                block[to : to + 9, :] = gram[l, rows, :]
            block[72:81, c * 64 : (c + 1) * 64] = gram[4, rows, : CH // 2]
        block[81:88, :] = (lane_exps + kept_exp)[0:7, :]
        message_ref[j] = block[...].astype(jnp.int32).astype(jnp.int16)


def sum_kernel(landed_ref, sum_ref):
    whole = jnp.zeros((72, CH), jnp.float32)
    folded = jnp.zeros((ROWS - 72, CH), jnp.float32)
    for j in range(landed_ref.shape[0]):
        codes = landed_ref[j].astype(jnp.int32).astype(jnp.float32)
        scale = jnp.exp2(codes[80:88, :] * (1 / STEPS))
        whole += codes[:72, :] * jnp.abs(codes[:72, :]) * scale[1:2, :]
        folded += codes[72:, :] * jnp.abs(codes[72:, :]) * scale[2:3, :]
    sum_ref[:72, :] = whole * TOP**-2
    sum_ref[72:, :] = folded * TOP**-2


def rows_kernel(place_ref, mask_ref, near_ref, far_ref, weight_ref, kept_ref, out_ref, rows, split):
    core, owner = place_ref[0], place_ref[1]
    near, far = near_ref[...], far_ref[...]
    low = jnp.where(core == 0, near, far)
    high = jnp.where(core == 0, far, near)

    def mine(values, l):
        return jnp.where(core == 0, values[l * 9 : l * 9 + 9, :], values[(4 + l) * 9 : (4 + l) * 9 + 9, :])

    def middle(values):
        return jnp.where(core == 0, values[72:81, : CH // 2], values[72:81, CH // 2 :])

    rows[...] = jnp.zeros_like(rows)
    for l in range(4):
        rows[0:9, l * CH : (l + 1) * CH] = mine(low, l)
        rows[0:9, HALF + l * CH : HALF + (l + 1) * CH] = mine(high, l)
    rows[0:9, 4 * CH : HALF] = middle(low)
    rows[0:9, HALF + 4 * CH :] = middle(high)

    at = lax.broadcasted_iota(jnp.int32, (16, CH), 0)
    keep = jnp.zeros((16, CH), jnp.float32)
    for k in range(9):
        bit = mask_ref[lax.rem(owner * 9 + k, CH)]
        keep = jnp.where(at == k, bit.astype(jnp.float32), keep)
    whole = rows[...]
    head = whole.astype(jnp.bfloat16)
    left = whole - head.astype(jnp.float32)
    tail = left.astype(jnp.bfloat16)
    split[0:16, :] = head
    split[16:32, :] = tail
    split[32:48, :] = (left - tail.astype(jnp.float32)).astype(jnp.bfloat16)
    product = jnp.dot(split[...], weight_ref[...], preferred_element_type=jnp.float32)
    product = product[32:48, :] + product[16:32, :] + product[0:16, :]
    count = place_ref[2].astype(jnp.float32)
    kept = kept_ref[...] > 0
    for t in range(TAPS):
        part = whole[:, t * CH : (t + 1) * CH]
        part = jnp.where((keep > 0) & kept, part / count, 0.0)
        out_ref[:, t * CH : (t + 1) * CH] = part[0:9, :]
    for n in range(2):
        part = product[:, n * CH : (n + 1) * CH]
        part = jnp.where(keep > 0, part / count, 0.0)
        out_ref[:, K + n * CH : K + (n + 1) * CH] = part[0:9, :]


VMEM = pl.BlockSpec(memory_space=pltpu.VMEM)
SMEM = pl.BlockSpec(memory_space=pltpu.SMEM)
HBM = pl.BlockSpec(memory_space=pltpu.HBM)


def shape(dims, kind):
    return jax.ShapeDtypeStruct(dims, kind)


def per_device(fields, sample_index, halo_index, channel_mask, weight):
    faces, samples = lax.axis_size("face"), lax.axis_size("sample")
    face, sample = lax.axis_index("face"), lax.axis_index("sample")
    core = lax.rem(face, 2)
    subs = fields.shape[1]
    units = 4 * subs
    swap = [(f, f ^ 1) for f in range(faces)]
    bf16, f32 = jnp.bfloat16, jnp.float32

    other = lax.ppermute(fields, "face", swap)
    halo_other = lax.ppermute(halo_index, "face", swap)
    copies = pl.pallas_call(
        edges_kernel,
        out_shape=shape((faces // 2, 8 * subs * SIDE, CH), bf16),
        in_specs=[SMEM, VMEM, VMEM],
        out_specs=VMEM,
        name="edges",
    )(sample_index, fields, jnp.asarray(edge_picker()))

    copies, other, halo_other = lax.optimization_barrier((copies, other, halo_other))
    same_core = [[f for f in range(c, faces, 2)] for c in range(2)]
    table = lax.all_to_all(copies, "face", 0, 0, axis_index_groups=same_core)

    mask_row = channel_mask[None]
    place = jnp.stack([core, face * samples + sample, jnp.int32(2 * subs * PIX * faces * samples)])

    inner, done = pl.pallas_call(
        inner_kernel,
        out_shape=(pltpu.HBM((5, K, CH), f32), shape((8, CH), f32)),
        in_specs=[SMEM] * 2 + [VMEM] * 2,
        out_specs=(HBM, VMEM),
        scratch_shapes=[
            pltpu.VMEM((K, units * PIX), bf16),
            pltpu.VMEM((5, K, CH), f32),
            pltpu.SemaphoreType.DMA((3,)),
        ],
        compiler_params=pltpu.CompilerParams(vmem_limit_bytes=28 * 2**20),
        cost_estimate=pl.CostEstimate(flops=6 * 10**9, bytes_accessed=5 * 10**6, transcendentals=0),
        name="inner",
    )(place, sample_index, fields, other)

    tiles = pl.pallas_call(
        functools.partial(gather_kernel, subs),
        out_shape=shape((units * CH, CH), bf16),
        in_specs=[SMEM] * 3 + [VMEM] * 2,
        out_specs=VMEM,
        compiler_params=pltpu.CompilerParams(vmem_limit_bytes=4 * 2**20),
        name="gather",
    )(place, halo_index, halo_other, table, done)
    tiles_other = lax.ppermute(tiles, "face", swap)

    message = pl.pallas_call(
        functools.partial(outer_kernel, subs),
        out_shape=shape((64, ROWS, CH), jnp.int16),
        in_specs=[SMEM] * 2 + [VMEM] * 8 + [HBM],
        out_specs=VMEM,
        scratch_shapes=[
            pltpu.VMEM((units * CH, PIX + CH), bf16),
            pltpu.VMEM((K, units * RIM), bf16),
            pltpu.VMEM((5, K, CH), f32),
            pltpu.VMEM((8, CH), jnp.int32),
            pltpu.VMEM((4, ROWS, CH), f32),
            pltpu.VMEM((5, K, CH), f32),
            pltpu.SemaphoreType.DMA((3,)),
        ],
        compiler_params=pltpu.CompilerParams(vmem_limit_bytes=28 * 2**20),
        name="outer",
    )(
        place,
        sample_index,
        fields,
        other,
        tiles,
        tiles_other,
        halo_index,
        halo_other,
        jnp.asarray(rim_matrix()),
        mask_row,
        pltpu.with_memory_space_constraint(inner, pltpu.HBM),
    )

    groups = [[f * samples + s for f in range(c, faces, 2) for s in range(samples)] for c in range(2)]
    landed = lax.all_to_all(message, AXES, 0, 0, axis_index_groups=groups)
    near = pl.pallas_call(
        sum_kernel,
        out_shape=shape((ROWS, CH), f32),
        in_specs=[VMEM],
        out_specs=VMEM,
        compiler_params=pltpu.CompilerParams(vmem_limit_bytes=8 * 2**20),
        name="total",
    )(landed)
    far = lax.ppermute(near, "face", swap)

    return pl.pallas_call(
        rows_kernel,
        out_shape=shape((TAPS, K + weight.shape[1]), f32),
        in_specs=[SMEM] * 2 + [VMEM] * 4,
        out_specs=VMEM,
        scratch_shapes=[pltpu.VMEM((16, K), f32), pltpu.VMEM((48, K), bf16)],
        compiler_params=pltpu.CompilerParams(vmem_limit_bytes=8 * 2**20),
        name="rows",
    )(place, channel_mask, near, far, weight, mask_row)


def solution(mesh):
    placed = (P("sample", "face", None, None), P("sample"), P("face", None), P(), P())
    return jax.shard_map(
        per_device,
        mesh=mesh,
        in_specs=placed,
        out_specs=P(("face", "sample"), None),
        check_vma=False,
    )
```

```python
import functools

import jax
import jax.numpy as jnp
import ml_dtypes
import numpy as np
from jax import lax
from jax.experimental import pallas as pl
from jax.experimental.pallas import tpu as pltpu
from jax.sharding import PartitionSpec as P

SIDE = 16
PIX = SIDE * SIDE
CH = 128
TAPS = 9
K = TAPS * CH
HALF = K // 2
CYCLE = 4 * SIDE + 4
RIM = 64
ROWS = 88
STEPS = 16
TOP = 32700.0
AXES = ("face", "sample")
NT = (((1,), (1,)), ((), ()))
SIDE_AT = (1, 19, 36, 52)
CORNER_AT = (0, 17, 18, 35)


def edge_picker():
    out = np.zeros((4 * SIDE, PIX), np.float32)
    for i in range(SIDE):
        out[i, i] = 1
        out[SIDE + i, (SIDE - 1) * SIDE + i] = 1
        out[2 * SIDE + i, i * SIDE] = 1
        out[3 * SIDE + i, i * SIDE + SIDE - 1] = 1
    return out.astype(ml_dtypes.bfloat16)


def rim_matrix():
    whole = np.zeros((TAPS, PIX + CH, PIX), np.float32)
    for t in range(TAPS):
        for y in range(SIDE):
            for x in range(SIDE):
                u, v = y + t // 3, x + t % 3
                if u == 0:
                    k = PIX + v
                elif u == SIDE + 1:
                    k = PIX + SIDE + 2 + v
                elif v == 0:
                    k = PIX + 2 * SIDE + 4 + u - 1
                elif v == SIDE + 1:
                    k = PIX + 3 * SIDE + 4 + u - 1
                else:
                    k = (u - 1) * SIDE + v - 1
                whole[t, k, y * SIDE + x] = 1
    rim = [p for p in range(PIX) if p // SIDE in (0, SIDE - 1) or p % SIDE in (0, SIDE - 1)]
    outer = np.zeros((PIX + CH, 640), np.float32)
    for t in range(TAPS):
        outer[:, t * RIM : t * RIM + len(rim)] = whole[t][:, rim]
    return outer.astype(ml_dtypes.bfloat16)


def edges_kernel(index_ref, fields_ref, pick_ref, copies_ref):
    subs = fields_ref.shape[1]
    for s in range(2):
        for f in range(subs):
            x = fields_ref[index_ref[s], f]
            u = s * subs + f
            edges = lax.dot_general(pick_ref[...], x, NT, preferred_element_type=jnp.float32)
            edges = edges.astype(jnp.bfloat16)
            for d in range(copies_ref.shape[0]):
                copies_ref[d, u * 4 * SIDE : (u + 1) * 4 * SIDE, :] = edges


def owned_rows(core, patches, owned):
    for c in range(2):

        @pl.when(core == c)
        def _():
            for g in range(K // 144):
                owned[g * 72 : (g + 1) * 72, :] = patches[g * 144 + c * 72 : g * 144 + c * 72 + 72, :]


def tap_blocks():
    return [slice(t, t + 3) for t in range(0, TAPS, 3)]


def inner_kernel(core_ref, index_ref, own_ref, other_ref, gram_ref, done_ref, patches, owned, gram, sems):
    subs = own_ref.shape[1]
    done_ref[...] = jnp.zeros_like(done_ref)
    pixel = lax.broadcasted_iota(jnp.int32, (PIX, PIX), 1)
    ahead = lax.broadcasted_iota(jnp.int32, (PIX, PIX), 0) - pixel
    y, x = pixel // SIDE, pixel % SIDE
    inside = (y > 0) & (y < SIDE - 1) & (x > 0) & (x < SIDE - 1)
    ahead = jnp.where(inside, ahead, PIX)
    for t in range(TAPS):
        shift = (t // 3 - 1) * SIDE + t % 3 - 1
        tap = jnp.where(ahead == shift, 1.0, 0.0).astype(jnp.bfloat16)
        for n, ref in enumerate((own_ref, other_ref)):
            for s in range(2):
                x = ref[index_ref[s]].reshape(subs * CH, PIX)
                values = jnp.dot(x, tap, preferred_element_type=jnp.float32)
                values = values.astype(jnp.bfloat16)
                for f in range(subs):
                    u = (n * 2 + s) * subs + f
                    patches[t * CH : (t + 1) * CH, u * PIX : (u + 1) * PIX] = values[f * CH : (f + 1) * CH, :]
    owned_rows(core_ref[0], patches, owned)
    copies = []
    for n, taps in enumerate(tap_blocks()):
        right = patches[taps.start * CH : taps.stop * CH, :]
        block = lax.dot_general(owned[...], right, NT, preferred_element_type=jnp.float32)
        for l in range(3):
            gram[taps.start + l, :, :] = block[:, l * CH : (l + 1) * CH]
        copies.append(pltpu.make_async_copy(gram.at[taps], gram_ref.at[taps], sems.at[n]))
        copies[-1].start()
    for copy in copies:
        copy.wait()


def gather_kernel(subs, core_ref, halo_own_ref, halo_other_ref, table_ref, after_ref, tiles_ref):
    core = core_ref[0]
    for side, halo_ref in enumerate((halo_own_ref, halo_other_ref)):
        for f in range(subs):
            for n, at in enumerate(SIDE_AT + CORNER_AT):
                index = halo_ref[f, at]
                sub = index // (4 * SIDE)
                edge = lax.rem(index // SIDE, 4)
                device = sub // subs
                local = sub - device * subs
                near = lax.rem(device, 2) == core
                for s in range(2):
                    row = pl.multiple_of((s * subs + local) * 4 * SIDE + edge * SIDE, SIDE)
                    tile = table_ref[device // 2, pl.ds(row, SIDE), :]
                    u = (side * 2 + s) * subs + f
                    tiles_ref[u * CH + n * SIDE : u * CH + (n + 1) * SIDE, :] = jnp.where(near, tile, jnp.zeros_like(tile))


def outer_kernel(
    subs,
    core_ref,
    index_ref,
    own_ref,
    other_ref,
    tiles_own_ref,
    tiles_other_ref,
    halo_rows_own_ref,
    halo_rows_other_ref,
    taps_ref,
    mask_ref,
    inner_ref,
    message_ref,
    grid,
    patches,
    owned,
    gram,
    position,
    stage,
    inner,
    sems,
):
    core = core_ref[0]
    units = 4 * subs
    half = units // 2
    copies = []
    for n, taps in enumerate(tap_blocks()):
        copies.append(pltpu.make_async_copy(inner_ref.at[taps], inner.at[taps], sems.at[n]))
        copies[-1].start()

    lane = lax.broadcasted_iota(jnp.int32, (8, CH), 1)
    base = jnp.full((8, CH), -1000, jnp.int32)
    for e, at in enumerate(SIDE_AT):
        base = jnp.where((lane >= at) & (lane < at + SIDE), e * SIDE, base)
    for e, at in enumerate(CORNER_AT):
        base = jnp.where(lane == at, (4 + e) * SIDE, base)
    position[...] = jnp.zeros((8, CH), jnp.int32)
    position[0:subs, 0:CYCLE] = lax.rem(halo_rows_own_ref[...], SIDE)
    position[subs : 2 * subs, 0:CYCLE] = lax.rem(halo_rows_other_ref[...], SIDE)
    source = position[...] + base

    row_at = lax.broadcasted_iota(jnp.int32, (CH, CH), 0)
    col_at = lax.broadcasted_iota(jnp.int32, (CH, CH), 1)
    diagonal = row_at == col_at
    eye = jnp.where(diagonal, 1.0, 0.0).astype(jnp.bfloat16)
    split = units * CH // 2
    turned = []
    for mine, theirs in ((0, split), (split, 0)):
        tiles = tiles_own_ref[mine : mine + split, :] + tiles_other_ref[theirs : theirs + split, :]
        tiles = lax.dot_general(eye, tiles, NT, preferred_element_type=jnp.float32)
        turned.append(tiles.astype(jnp.bfloat16))
    energy = jnp.zeros((CH, CH), jnp.float32)
    for u in range(units):
        side, f = u // half, u % half % subs
        at = side * subs + f
        pick = jnp.where(row_at == source[at : at + 1, :], 1.0, 0.0).astype(jnp.bfloat16)
        cycle = jnp.dot(turned[side][:, u % half * CH : (u % half + 1) * CH], pick, preferred_element_type=jnp.float32)
        x = (own_ref if side == 0 else other_ref)[index_ref[u % half // subs], f]
        grid[u * CH : (u + 1) * CH, :PIX] = x
        grid[u * CH : (u + 1) * CH, PIX:] = cycle.astype(jnp.bfloat16)
        x = x.astype(jnp.float32)
        energy += x[:, :CH] * x[:, :CH] + x[:, CH:] * x[:, CH:] + cycle * cycle
    kept = mask_ref[...].astype(jnp.float32)
    kept_row = jnp.sum(jnp.where(diagonal, kept, 0.0), axis=1, keepdims=True)
    energy = jnp.sum(energy, axis=1, keepdims=True)

    def exponent(values):
        top = jnp.full((8, CH), jnp.maximum(jnp.max(values), 2.0**-120), jnp.float32)
        return jnp.ceil(jnp.log2(top) * (STEPS / 2) + 0.1)

    kept_exp = exponent(jnp.where(kept_row > 0, energy, 0.0))
    any_exp = exponent(energy)
    lane_exps = jnp.where(kept > 0, kept_exp, any_exp) + kept_exp
    scale = jnp.exp2(lane_exps * (-1 / STEPS))

    def coded(values):
        return jnp.round(TOP * values * lax.rsqrt(jnp.maximum(jnp.abs(values), 1e-30)))

    chunk = units * CH // 3
    for m in range(0, units * CH, chunk):
        values = jnp.dot(grid[m : m + chunk, :], taps_ref[...], preferred_element_type=jnp.float32)
        values = values.astype(jnp.bfloat16)
        for n in range(chunk // CH):
            u = m // CH + n
            for t in range(TAPS):
                part = values[n * CH : (n + 1) * CH, t * RIM : (t + 1) * RIM]
                patches[t * CH : (t + 1) * CH, u * RIM : (u + 1) * RIM] = part

    owned_rows(core, patches, owned)
    for n, taps in enumerate(tap_blocks()):
        right = patches[taps.start * CH : taps.stop * CH, :]
        block = lax.dot_general(owned[...], right, NT, preferred_element_type=jnp.float32)
        copies[n].wait()
        for l in range(3):
            part = block[:, l * CH : (l + 1) * CH] + inner[taps.start + l, :, :]
            gram[taps.start + l, :, :] = coded(part * scale[0:1, :])

    for j in range(message_ref.shape[0]):
        block = stage.at[j % 4]
        for l in range(TAPS):
            block[l * 9 : (l + 1) * 9, :] = gram[l, j * 9 : (j + 1) * 9, :]
        block[81:88, :] = lane_exps[0:7, :]
        message_ref[j] = block[...].astype(jnp.int32).astype(jnp.int16)


def rows_kernel(place_ref, mask_ref, landed_ref, weight_ref, kept_ref, out_ref, rows, split):
    owner = place_ref[1]
    total = jnp.zeros((ROWS, CH), jnp.float32)
    for j in range(landed_ref.shape[0]):
        codes = landed_ref[j].astype(jnp.int32).astype(jnp.float32)
        scale = jnp.exp2(codes[80:88, :] * (1 / STEPS))
        total += codes * jnp.abs(codes) * scale[1:2, :]
    total = total * TOP**-2
    rows[...] = jnp.zeros_like(rows)
    for l in range(TAPS):
        rows[0:9, l * CH : (l + 1) * CH] = total[l * 9 : (l + 1) * 9, :]

    at = lax.broadcasted_iota(jnp.int32, (16, CH), 0)
    keep = jnp.zeros((16, CH), jnp.float32)
    for k in range(9):
        bit = mask_ref[lax.rem(owner * 9 + k, CH)]
        keep = jnp.where(at == k, bit.astype(jnp.float32), keep)
    whole = rows[...]
    head = whole.astype(jnp.bfloat16)
    left = whole - head.astype(jnp.float32)
    tail = left.astype(jnp.bfloat16)
    split[0:16, :] = head
    split[16:32, :] = tail
    split[32:48, :] = (left - tail.astype(jnp.float32)).astype(jnp.bfloat16)
    product = jnp.dot(split[...], weight_ref[...], preferred_element_type=jnp.float32)
    product = product[32:48, :] + product[16:32, :] + product[0:16, :]
    count = place_ref[2].astype(jnp.float32)
    kept = kept_ref[...] > 0
    for t in range(TAPS):
        part = whole[:, t * CH : (t + 1) * CH]
        part = jnp.where((keep > 0) & kept, part / count, 0.0)
        out_ref[:, t * CH : (t + 1) * CH] = part[0:9, :]
    for n in range(2):
        part = product[:, n * CH : (n + 1) * CH]
        part = jnp.where(keep > 0, part / count, 0.0)
        out_ref[:, K + n * CH : K + (n + 1) * CH] = part[0:9, :]


VMEM = pl.BlockSpec(memory_space=pltpu.VMEM)
SMEM = pl.BlockSpec(memory_space=pltpu.SMEM)
HBM = pl.BlockSpec(memory_space=pltpu.HBM)


def shape(dims, kind):
    return jax.ShapeDtypeStruct(dims, kind)


def per_device(fields, sample_index, halo_index, channel_mask, weight):
    faces, samples = lax.axis_size("face"), lax.axis_size("sample")
    face, sample = lax.axis_index("face"), lax.axis_index("sample")
    core = lax.rem(face, 2)
    subs = fields.shape[1]
    units = 4 * subs
    swap = [(f, f ^ 1) for f in range(faces)]
    bf16, f32 = jnp.bfloat16, jnp.float32

    other = lax.ppermute(fields, "face", swap)
    halo_other = lax.ppermute(halo_index, "face", swap)
    copies = pl.pallas_call(
        edges_kernel,
        out_shape=shape((faces // 2, 8 * subs * SIDE, CH), bf16),
        in_specs=[SMEM, VMEM, VMEM],
        out_specs=VMEM,
        name="edges",
    )(sample_index, fields, jnp.asarray(edge_picker()))

    copies, other, halo_other = lax.optimization_barrier((copies, other, halo_other))
    same_core = [[f for f in range(c, faces, 2)] for c in range(2)]
    table = lax.all_to_all(copies, "face", 0, 0, axis_index_groups=same_core)

    mask_row = channel_mask[None]
    place = jnp.stack([core, face * samples + sample, jnp.int32(2 * subs * PIX * faces * samples)])

    inner, done = pl.pallas_call(
        inner_kernel,
        out_shape=(pltpu.HBM((TAPS, HALF, CH), f32), shape((8, CH), f32)),
        in_specs=[SMEM] * 2 + [VMEM] * 2,
        out_specs=(HBM, VMEM),
        scratch_shapes=[
            pltpu.VMEM((K, units * PIX), bf16),
            pltpu.VMEM((HALF, units * PIX), bf16),
            pltpu.VMEM((TAPS, HALF, CH), f32),
            pltpu.SemaphoreType.DMA((3,)),
        ],
        compiler_params=pltpu.CompilerParams(vmem_limit_bytes=28 * 2**20),
        cost_estimate=pl.CostEstimate(flops=6 * 10**9, bytes_accessed=5 * 10**6, transcendentals=0),
        name="inner",
    )(place, sample_index, fields, other)

    tiles = pl.pallas_call(
        functools.partial(gather_kernel, subs),
        out_shape=shape((units * CH, CH), bf16),
        in_specs=[SMEM] * 3 + [VMEM] * 2,
        out_specs=VMEM,
        compiler_params=pltpu.CompilerParams(vmem_limit_bytes=4 * 2**20),
        name="gather",
    )(place, halo_index, halo_other, table, done)
    tiles_other = lax.ppermute(tiles, "face", swap)

    message = pl.pallas_call(
        functools.partial(outer_kernel, subs),
        out_shape=shape((64, ROWS, CH), jnp.int16),
        in_specs=[SMEM] * 2 + [VMEM] * 8 + [HBM],
        out_specs=VMEM,
        scratch_shapes=[
            pltpu.VMEM((units * CH, PIX + CH), bf16),
            pltpu.VMEM((K, units * RIM), bf16),
            pltpu.VMEM((HALF, units * RIM), bf16),
            pltpu.VMEM((TAPS, HALF, CH), f32),
            pltpu.VMEM((8, CH), jnp.int32),
            pltpu.VMEM((4, ROWS, CH), f32),
            pltpu.VMEM((TAPS, HALF, CH), f32),
            pltpu.SemaphoreType.DMA((3,)),
        ],
        compiler_params=pltpu.CompilerParams(vmem_limit_bytes=28 * 2**20),
        name="outer",
    )(
        place,
        sample_index,
        fields,
        other,
        tiles,
        tiles_other,
        halo_index,
        halo_other,
        jnp.asarray(rim_matrix()),
        mask_row,
        pltpu.with_memory_space_constraint(inner, pltpu.HBM),
    )

    groups = [[f * samples + s for f in range(c, faces, 2) for s in range(samples)] for c in range(2)]
    landed = lax.all_to_all(message, AXES, 0, 0, axis_index_groups=groups)
    return pl.pallas_call(
        rows_kernel,
        out_shape=shape((TAPS, K + weight.shape[1]), f32),
        in_specs=[SMEM] * 2 + [VMEM] * 3,
        out_specs=VMEM,
        scratch_shapes=[pltpu.VMEM((16, K), f32), pltpu.VMEM((48, K), bf16)],
        compiler_params=pltpu.CompilerParams(vmem_limit_bytes=8 * 2**20),
        name="rows",
    )(place, channel_mask, landed, weight, mask_row)


def solution(mesh):
    placed = (P("sample", "face", None, None), P("sample"), P("face", None), P(), P())
    return jax.shard_map(
        per_device,
        mesh=mesh,
        in_specs=placed,
        out_specs=P(("face", "sample"), None),
        check_vma=False,
    )
```

```python
import functools

import jax
import jax.numpy as jnp
import ml_dtypes
import numpy as np
from jax import lax
from jax.experimental import pallas as pl
from jax.experimental.pallas import tpu as pltpu
from jax.sharding import PartitionSpec as P

SIDE = 16
PIX = SIDE * SIDE
CH = 128
TAPS = 9
K = TAPS * CH
HALF = K // 2
CYCLE = 4 * SIDE + 4
RIM = 64
INNER = PIX - RIM
ROWS = 88
STEPS = 16
TOP = 32700.0
THIRD = 43
AXES = ("face", "sample")
NT = (((1,), (1,)), ((), ()))
SIDE_AT = (1, 19, 36, 52)
CORNER_AT = (0, 17, 18, 35)


def edge_picker():
    out = np.zeros((4 * SIDE, PIX), np.float32)
    for i in range(SIDE):
        out[i, i] = 1
        out[SIDE + i, (SIDE - 1) * SIDE + i] = 1
        out[2 * SIDE + i, i * SIDE] = 1
        out[3 * SIDE + i, i * SIDE + SIDE - 1] = 1
    return out.astype(ml_dtypes.bfloat16)


def rim_sources(tap):
    lane = lax.broadcasted_iota(jnp.int32, (8, CH), 1)
    second = lane >= RIM
    place = lax.rem(lane, RIM)
    along = lax.rem(place, SIDE)
    side = place // SIDE
    y = jnp.where(side == 0, 0, jnp.where(side == 1, SIDE - 1, along))
    x = jnp.where(side == 2, 0, jnp.where(side == 3, SIDE - 1, along))
    corner = (side >= 2) & ((along == 0) | (along == SIDE - 1))
    y = jnp.where(corner, jnp.clip(along, 1, SIDE - 2), y)
    x = jnp.where(corner, jnp.where(side == 2, 1, SIDE - 2), x)
    u, v = y + tap // 3 - 1, x + tap % 3 - 1
    inside = (u >= 0) & (u < SIDE) & (v >= 0) & (v < SIDE)
    entry = jnp.where(v < 0, 2 * SIDE + 4 + u, 3 * SIDE + 4 + u)
    entry = jnp.where(u < 0, v + 1, jnp.where(u >= SIDE, SIDE + 3 + v, entry))
    pixel = jnp.where(inside, u * SIDE + v + jnp.where(second, PIX, 0), -1)
    cycle = jnp.where(inside, -1, entry + jnp.where(second, CH, 0))
    return pixel[0:1, :], cycle[0:1, :]


def inner_pixels(place):
    rest = place - 2 * (SIDE - 4)
    row = lax.shift_right_logical(jnp.maximum(rest, 0) * 147, 11)
    y = jnp.where(place < SIDE - 4, 1, jnp.where(rest < 0, SIDE - 2, row + 2))
    x = jnp.where(place < SIDE - 4, place + 2, jnp.where(rest < 0, place - SIDE + 6, rest - row * (SIDE - 2) + 1))
    return jnp.where((place >= 0) & (place < INNER), y * SIDE + x, -PIX)


def one_hot(rows, source):
    at = lax.broadcasted_iota(jnp.int32, (rows, CH), 0)
    return jnp.where(at == source, 1.0, 0.0).astype(jnp.bfloat16)


def edges_kernel(index_ref, fields_ref, pick_ref, copies_ref):
    subs = fields_ref.shape[1]
    for s in range(2):
        for f in range(subs):
            x = fields_ref[index_ref[s], f]
            u = s * subs + f
            edges = lax.dot_general(pick_ref[...], x, NT, preferred_element_type=jnp.float32)
            edges = edges.astype(jnp.bfloat16)
            for d in range(copies_ref.shape[0]):
                copies_ref[d, u * 4 * SIDE : (u + 1) * 4 * SIDE, :] = edges


def owned_rows(core, patches, owned):
    for c in range(2):

        @pl.when(core == c)
        def _():
            for g in range(K // 144):
                owned[g * 72 : (g + 1) * 72, :] = patches[g * 144 + c * 72 : g * 144 + c * 72 + 72, :]


def tap_blocks():
    return [slice(0, 4), slice(4, 8), slice(8, TAPS)]


def core_index():
    return lax.axis_index("face") & 1


def inner_kernel(
    index_ref,
    halo_own_ref,
    halo_other_ref,
    own_ref,
    other_ref,
    gram_ref,
    pairs_ref,
    plan_ref,
    patches,
    owned,
    gram,
    sems,
):
    subs = own_ref.shape[1]
    core = core_index()

    for side, halo_ref in enumerate((halo_own_ref, halo_other_ref)):
        for f in range(subs):
            for n, at in enumerate(SIDE_AT + CORNER_AT):
                index = halo_ref[f, at]
                sub = lax.shift_right_logical(index, 6)
                device = lax.shift_right_logical(sub * THIRD, 7)
                row = (lax.shift_right_logical(device, 1) * 2 * subs + sub - device * subs) * 4 * SIDE
                row += index & (3 * SIDE)
                plan_ref[(side * subs + f) * 8 + n] = jnp.where((device & 1) == core, row, -SIDE)

    for s in range(2):
        for n, ref in enumerate((own_ref, other_ref)):
            rows = slice(s * subs * CH, (s + 1) * subs * CH)
            pairs_ref[rows, n * PIX : (n + 1) * PIX] = ref[index_ref[s]].reshape(subs * CH, PIX)

    row_at = lax.broadcasted_iota(jnp.int32, (PIX, PIX), 0)
    place = lax.broadcasted_iota(jnp.int32, (8, PIX), 1)
    ahead = [row_at - inner_pixels(place + d)[0:1, :] for d in (0, INNER - PIX)]
    for t in range(TAPS):
        shift = (t // 3 - 1) * SIDE + t % 3 - 1
        taps = [jnp.where(d == shift, 1.0, 0.0).astype(jnp.bfloat16) for d in ahead]
        for s in range(2):
            first, second = (
                jnp.dot(ref[index_ref[s]].reshape(subs * CH, PIX), tap, preferred_element_type=jnp.float32)
                for ref, tap in zip((own_ref, other_ref), taps)
            )
            columns = (first[:, :CH], first[:, CH:] + second[:, :CH], second[:, CH:])
            for n, values in enumerate(columns):
                values = values.astype(jnp.bfloat16)
                for f in range(subs):
                    at = (s * subs + f) * 2 * INNER + n * CH
                    patches[t * CH : (t + 1) * CH, at : at + CH] = values[f * CH : (f + 1) * CH, :]
    owned_rows(core, patches, owned)
    copies = []
    for n, taps in enumerate(tap_blocks()):
        right = patches[taps.start * CH : taps.stop * CH, :]
        block = lax.dot_general(owned[...], right, NT, preferred_element_type=jnp.float32)
        for l in range(taps.stop - taps.start):
            gram[taps.start + l, :, :] = block[:, l * CH : (l + 1) * CH]
        copies.append(pltpu.make_async_copy(gram.at[taps], gram_ref.at[taps], sems.at[n]))
        copies[-1].start()
    for copy in copies:
        copy.wait()


def gather_kernel(subs, plan_ref, table_ref, tiles_ref):
    zero = jnp.zeros((SIDE, CH), jnp.bfloat16)
    for f in range(2 * subs):
        for n in range(8):
            row = plan_ref[f * 8 + n]
            near = row >= 0
            row = jnp.maximum(row, 0)
            for s in range(2):
                at = pl.multiple_of(row + s * subs * 4 * SIDE, SIDE)
                u = (f // subs * 2 + s) * subs + f % subs
                tiles_ref[u * CH + n * SIDE : u * CH + (n + 1) * SIDE, :] = jnp.where(near, table_ref[pl.ds(at, SIDE), :], zero)


def rim_kernel(subs, pairs_ref, after_ref, inner_ref, rim_ref, matrix_ref, energy_ref, gram_ref, pixels, sems):
    copies = []
    for n, taps in enumerate(tap_blocks()):
        copies.append(pltpu.make_async_copy(inner_ref.at[taps], gram_ref.at[taps], sems.at[n]))
        copies[-1].start()
    for t in range(TAPS):
        pixel, cycle = rim_sources(t)
        pixels[:, t * CH : (t + 1) * CH] = one_hot(2 * PIX, pixel)
        matrix_ref[:, t * CH : (t + 1) * CH] = one_hot(2 * CH, cycle)
    energy = jnp.zeros((CH, CH), jnp.float32)
    for p in range(2 * subs):
        x = pairs_ref[p * CH : (p + 1) * CH, :].astype(jnp.float32)
        for n in range(4):
            energy += x[:, n * CH : (n + 1) * CH] * x[:, n * CH : (n + 1) * CH]
    energy_ref[...] = energy
    values = jnp.dot(pairs_ref[...], pixels[...], preferred_element_type=jnp.float32).astype(jnp.bfloat16)
    for p in range(2 * subs):
        for t in range(TAPS):
            part = values[p * CH : (p + 1) * CH, t * CH : (t + 1) * CH]
            rim_ref[t * CH : (t + 1) * CH, p * CH : (p + 1) * CH] = part
    for copy in copies:
        copy.wait()


def outer_kernel(
    subs,
    tiles_own_ref,
    tiles_other_ref,
    halo_rows_own_ref,
    halo_rows_other_ref,
    matrix_ref,
    energy_ref,
    mask_ref,
    rim_ref,
    inner_ref,
    message_ref,
    patches,
    owned,
    gram,
    stage,
    position,
    cycles,
):
    core = core_index()
    units = 4 * subs
    half = units // 2
    lane = lax.broadcasted_iota(jnp.int32, (8, CH), 1)
    base = jnp.full((8, CH), -1000, jnp.int32)
    for e, at in enumerate(SIDE_AT):
        base = jnp.where((lane >= at) & (lane < at + SIDE), e * SIDE, base)
    for e, at in enumerate(CORNER_AT):
        base = jnp.where(lane == at, (4 + e) * SIDE, base)
    position[...] = jnp.zeros((8, CH), jnp.int32)
    position[0:subs, 0:CYCLE] = lax.rem(halo_rows_own_ref[...], SIDE)
    position[subs : 2 * subs, 0:CYCLE] = lax.rem(halo_rows_other_ref[...], SIDE)
    source = position[...] + base

    row_at = lax.broadcasted_iota(jnp.int32, (CH, CH), 0)
    col_at = lax.broadcasted_iota(jnp.int32, (CH, CH), 1)
    diagonal = row_at == col_at
    eye = jnp.where(diagonal, 1.0, 0.0).astype(jnp.bfloat16)
    split = units * CH // 2
    energy = energy_ref[...]
    for side, (mine, theirs) in enumerate(((0, split), (split, 0))):
        tiles = tiles_own_ref[mine : mine + split, :] + tiles_other_ref[theirs : theirs + split, :]
        tiles = lax.dot_general(eye, tiles, NT, preferred_element_type=jnp.float32).astype(jnp.bfloat16)
        for p in range(half):
            at = side * subs + p % subs
            pick = jnp.where(row_at == source[at : at + 1, :], 1.0, 0.0).astype(jnp.bfloat16)
            cycle = jnp.dot(tiles[:, p * CH : (p + 1) * CH], pick, preferred_element_type=jnp.float32)
            energy += cycle * cycle
            cycles[p * CH : (p + 1) * CH, side * CH : (side + 1) * CH] = cycle.astype(jnp.bfloat16)

    values = jnp.dot(cycles[...], matrix_ref[...], preferred_element_type=jnp.float32).astype(jnp.bfloat16)
    for p in range(half):
        for t in range(TAPS):
            part = values[p * CH : (p + 1) * CH, t * CH : (t + 1) * CH]
            place = (slice(t * CH, (t + 1) * CH), slice(p * CH, (p + 1) * CH))
            patches[place] = rim_ref[place] + part

    kept = mask_ref[...].astype(jnp.float32)
    kept_row = jnp.sum(jnp.where(diagonal, kept, 0.0), axis=1, keepdims=True)
    energy = jnp.sum(energy, axis=1, keepdims=True)

    def exponent(values):
        top = jnp.full((8, CH), jnp.maximum(jnp.max(values), 2.0**-120), jnp.float32)
        return jnp.ceil(jnp.log2(top) * (STEPS / 2) + 0.1)

    kept_exp = exponent(jnp.where(kept_row > 0, energy, 0.0))
    any_exp = exponent(energy)
    lane_exps = jnp.where(kept > 0, kept_exp, any_exp) + kept_exp
    scale = jnp.exp2(lane_exps * (-1 / STEPS))

    def coded(values):
        return jnp.round(TOP * values * lax.rsqrt(jnp.maximum(jnp.abs(values), 1e-30)))

    owned_rows(core, patches, owned)
    for n, taps in enumerate(tap_blocks()):
        right = patches[taps.start * CH : taps.stop * CH, :]
        block = lax.dot_general(owned[...], right, NT, preferred_element_type=jnp.float32)
        for l in range(taps.stop - taps.start):
            part = block[:, l * CH : (l + 1) * CH] + inner_ref[taps.start + l, :, :]
            gram[taps.start + l, :, :] = coded(part * scale[0:1, :])

    for j in range(message_ref.shape[0]):
        block = stage.at[j % 4]
        for l in range(TAPS):
            block[l * 9 : (l + 1) * 9, :] = gram[l, j * 9 : (j + 1) * 9, :]
        block[81:88, :] = lane_exps[0:7, :]
        message_ref[j] = block[...].astype(jnp.int32).astype(jnp.int16)


def rows_kernel(count, landed_ref, weight_ref, kept_ref, out_ref, rows, split):
    owner = lax.axis_index("face") * lax.axis_size("sample") + lax.axis_index("sample")
    total = jnp.zeros((ROWS, CH), jnp.float32)
    for j in range(landed_ref.shape[0]):
        codes = landed_ref[j].astype(jnp.int32).astype(jnp.float32)
        scale = jnp.exp2(codes[80:88, :] * (1 / STEPS))
        total += codes * jnp.abs(codes) * scale[1:2, :]
    total = total * TOP**-2
    rows[...] = jnp.zeros_like(rows)
    for l in range(TAPS):
        rows[0:9, l * CH : (l + 1) * CH] = total[l * 9 : (l + 1) * 9, :]

    channel = lax.rem(owner * 9 + lax.broadcasted_iota(jnp.int32, (16, CH), 0), CH)
    own = lax.broadcasted_iota(jnp.int32, (16, CH), 1) == channel
    keep = jnp.sum(jnp.where(own, kept_ref[...].astype(jnp.float32), 0.0), axis=1, keepdims=True)
    whole = rows[...]
    head = whole.astype(jnp.bfloat16)
    left = whole - head.astype(jnp.float32)
    tail = left.astype(jnp.bfloat16)
    split[0:16, :] = head
    split[16:32, :] = tail
    split[32:48, :] = (left - tail.astype(jnp.float32)).astype(jnp.bfloat16)
    product = jnp.dot(split[...], weight_ref[...], preferred_element_type=jnp.float32)
    product = product[32:48, :] + product[16:32, :] + product[0:16, :]
    kept = kept_ref[...] > 0
    for t in range(TAPS):
        part = whole[:, t * CH : (t + 1) * CH]
        part = jnp.where((keep > 0) & kept, part / count, 0.0)
        out_ref[:, t * CH : (t + 1) * CH] = part[0:9, :]
    for n in range(2):
        part = product[:, n * CH : (n + 1) * CH]
        part = jnp.where(keep > 0, part / count, 0.0)
        out_ref[:, K + n * CH : K + (n + 1) * CH] = part[0:9, :]


VMEM = pl.BlockSpec(memory_space=pltpu.VMEM)
SMEM = pl.BlockSpec(memory_space=pltpu.SMEM)
HBM = pl.BlockSpec(memory_space=pltpu.HBM)


def shape(dims, kind):
    return jax.ShapeDtypeStruct(dims, kind)


def per_device(fields, sample_index, halo_index, channel_mask, weight):
    faces, samples = lax.axis_size("face"), lax.axis_size("sample")
    subs = fields.shape[1]
    units = 4 * subs
    swap = [(f, f ^ 1) for f in range(faces)]
    bf16, f32 = jnp.bfloat16, jnp.float32

    other = lax.ppermute(fields, "face", swap)
    halo_other = lax.ppermute(halo_index, "face", swap)
    copies = pl.pallas_call(
        edges_kernel,
        out_shape=shape((faces // 2, 8 * subs * SIDE, CH), bf16),
        in_specs=[SMEM, VMEM, VMEM],
        out_specs=VMEM,
        name="edges",
    )(sample_index, fields, jnp.asarray(edge_picker()))

    copies, other, halo_other = lax.optimization_barrier((copies, other, halo_other))
    same_core = [[f for f in range(c, faces, 2)] for c in range(2)]
    table = lax.all_to_all(copies, "face", 0, 0, axis_index_groups=same_core)

    mask_row = channel_mask[None]
    inner, pairs, plan = pl.pallas_call(
        inner_kernel,
        out_shape=(
            pltpu.HBM((TAPS, HALF, CH), f32),
            shape((units * CH // 2, 2 * PIX), bf16),
            shape((2 * subs * 8,), jnp.int32),
        ),
        in_specs=[SMEM] * 3 + [VMEM] * 2,
        out_specs=(HBM, VMEM, SMEM),
        scratch_shapes=[
            pltpu.VMEM((K, units * INNER), bf16),
            pltpu.VMEM((HALF, units * INNER), bf16),
            pltpu.VMEM((TAPS, HALF, CH), f32),
            pltpu.SemaphoreType.DMA((3,)),
        ],
        compiler_params=pltpu.CompilerParams(vmem_limit_bytes=32 * 2**20),
        cost_estimate=pl.CostEstimate(flops=6 * 10**9, bytes_accessed=5 * 10**6, transcendentals=0),
        name="inner",
    )(sample_index, halo_index, halo_other, fields, other)

    tiles = pl.pallas_call(
        functools.partial(gather_kernel, subs),
        out_shape=shape((units * CH, CH), bf16),
        in_specs=[SMEM, VMEM],
        out_specs=VMEM,
        compiler_params=pltpu.CompilerParams(vmem_limit_bytes=4 * 2**20),
        name="gather",
    )(plan, table.reshape(-1, CH))
    tiles_other = lax.ppermute(tiles, "face", swap)

    rim, matrix, energy, inner = pl.pallas_call(
        functools.partial(rim_kernel, subs),
        out_shape=(
            shape((K, units * RIM), bf16),
            shape((2 * CH, K), bf16),
            shape((CH, CH), f32),
            shape((TAPS, HALF, CH), f32),
        ),
        in_specs=[VMEM, pl.BlockSpec(memory_space=pl.ANY), HBM],
        out_specs=(VMEM, VMEM, VMEM, VMEM),
        scratch_shapes=[pltpu.VMEM((2 * PIX, K), bf16), pltpu.SemaphoreType.DMA((3,))],
        compiler_params=pltpu.CompilerParams(vmem_limit_bytes=16 * 2**20),
        cost_estimate=pl.CostEstimate(flops=10**9, bytes_accessed=6 * 10**6, transcendentals=0),
        name="rim",
    )(pairs, tiles, pltpu.with_memory_space_constraint(inner, pltpu.HBM))

    message = pl.pallas_call(
        functools.partial(outer_kernel, subs),
        out_shape=shape((64, ROWS, CH), jnp.int16),
        in_specs=[VMEM] * 9,
        out_specs=VMEM,
        scratch_shapes=[
            pltpu.VMEM((K, units * RIM), bf16),
            pltpu.VMEM((HALF, units * RIM), bf16),
            pltpu.VMEM((TAPS, HALF, CH), f32),
            pltpu.VMEM((4, ROWS, CH), f32),
            pltpu.VMEM((8, CH), jnp.int32),
            pltpu.VMEM((units * CH // 2, 2 * CH), bf16),
        ],
        compiler_params=pltpu.CompilerParams(vmem_limit_bytes=28 * 2**20),
        name="outer",
    )(
        tiles,
        tiles_other,
        halo_index,
        halo_other,
        matrix,
        energy,
        mask_row,
        rim,
        inner,
    )

    groups = [[f * samples + s for f in range(c, faces, 2) for s in range(samples)] for c in range(2)]
    landed = lax.all_to_all(message, AXES, 0, 0, axis_index_groups=groups)
    count = 2 * subs * PIX * faces * samples
    return pl.pallas_call(
        functools.partial(rows_kernel, count),
        out_shape=shape((9, K + weight.shape[1]), f32),
        in_specs=[VMEM] * 3,
        out_specs=VMEM,
        scratch_shapes=[pltpu.VMEM((16, K), f32), pltpu.VMEM((48, K), bf16)],
        compiler_params=pltpu.CompilerParams(vmem_limit_bytes=8 * 2**20),
        name="rows",
    )(landed, weight, mask_row)


def solution(mesh):
    placed = (P("sample", "face", None, None), P("sample"), P("face", None), P(), P())
    return jax.shard_map(
        per_device,
        mesh=mesh,
        in_specs=placed,
        out_specs=P(("face", "sample"), None),
        check_vma=False,
    )
```

```python
import functools

import jax
import jax.numpy as jnp
import ml_dtypes
import numpy as np
from jax import lax
from jax.experimental import pallas as pl
from jax.experimental.pallas import tpu as pltpu
from jax.sharding import PartitionSpec as P

SIDE = 16
PIX = SIDE * SIDE
CH = 128
TAPS = 9
K = TAPS * CH
HALF = K // 2
CYCLE = 4 * SIDE + 4
RIM = 64
INNER = PIX - RIM
ROWS = 88
STEPS = 16
TOP = 32700.0
THIRD = 43
AXES = ("face", "sample")
NT = (((1,), (1,)), ((), ()))
SIDE_AT = (1, 19, 36, 52)
CORNER_AT = (0, 17, 18, 35)


def rim_sources(tap):
    lane = lax.broadcasted_iota(jnp.int32, (8, CH), 1)
    second = lane >= RIM
    place = lax.rem(lane, RIM)
    along = lax.rem(place, SIDE)
    side = place // SIDE
    y = jnp.where(side == 0, 0, jnp.where(side == 1, SIDE - 1, along))
    x = jnp.where(side == 2, 0, jnp.where(side == 3, SIDE - 1, along))
    corner = (side >= 2) & ((along == 0) | (along == SIDE - 1))
    y = jnp.where(corner, jnp.clip(along, 1, SIDE - 2), y)
    x = jnp.where(corner, jnp.where(side == 2, 1, SIDE - 2), x)
    u, v = y + tap // 3 - 1, x + tap % 3 - 1
    inside = (u >= 0) & (u < SIDE) & (v >= 0) & (v < SIDE)
    entry = jnp.where(v < 0, 2 * SIDE + 4 + u, 3 * SIDE + 4 + u)
    entry = jnp.where(u < 0, v + 1, jnp.where(u >= SIDE, SIDE + 3 + v, entry))
    pixel = jnp.where(inside, u * SIDE + v + jnp.where(second, PIX, 0), -1)
    cycle = jnp.where(inside, -1, entry + jnp.where(second, CH, 0))
    return pixel[0:1, :], cycle[0:1, :]


def inner_pixels(place):
    rest = place - 2 * (SIDE - 4)
    row = lax.shift_right_logical(jnp.maximum(rest, 0) * 147, 11)
    y = jnp.where(place < SIDE - 4, 1, jnp.where(rest < 0, SIDE - 2, row + 2))
    x = jnp.where(place < SIDE - 4, place + 2, jnp.where(rest < 0, place - SIDE + 6, rest - row * (SIDE - 2) + 1))
    return jnp.where((place >= 0) & (place < INNER), y * SIDE + x, -PIX)


def one_hot(rows, source):
    at = lax.broadcasted_iota(jnp.int32, (rows, CH), 0)
    return jnp.where(at == source, 1.0, 0.0).astype(jnp.bfloat16)


def edges_kernel(index_ref, fields_ref, copies_ref):
    subs = fields_ref.shape[1]
    row = lax.broadcasted_iota(jnp.int32, (4 * SIDE, PIX), 0)
    pixel = lax.broadcasted_iota(jnp.int32, (4 * SIDE, PIX), 1)
    along = row & (SIDE - 1)
    wanted = jnp.where(row < SIDE, along, (SIDE - 1) * SIDE + along)
    wanted = jnp.where(row >= 2 * SIDE, along * SIDE, wanted)
    wanted = jnp.where(row >= 3 * SIDE, along * SIDE + SIDE - 1, wanted)
    pick = jnp.where(pixel == wanted, 1.0, 0.0).astype(jnp.bfloat16)
    for s in range(2):
        for f in range(subs):
            x = fields_ref[index_ref[s], f]
            u = s * subs + f
            edges = lax.dot_general(pick, x, NT, preferred_element_type=jnp.float32)
            edges = edges.astype(jnp.bfloat16)
            for d in range(copies_ref.shape[0]):
                copies_ref[d, u * 4 * SIDE : (u + 1) * 4 * SIDE, :] = edges


def owned_rows(core, patches, owned):
    for c in range(2):

        @pl.when(core == c)
        def _():
            for g in range(K // 144):
                owned[g * 72 : (g + 1) * 72, :] = patches[g * 144 + c * 72 : g * 144 + c * 72 + 72, :]


def tap_blocks():
    return [slice(0, 4), slice(4, 8), slice(8, TAPS)]


def core_index():
    return lax.axis_index("face") & 1


def inner_kernel(
    index_ref,
    halo_own_ref,
    halo_other_ref,
    own_ref,
    other_ref,
    gram_ref,
    pairs_ref,
    plan_ref,
    patches,
    owned,
    gram,
    sems,
):
    subs = own_ref.shape[1]
    core = core_index()

    for side, halo_ref in enumerate((halo_own_ref, halo_other_ref)):
        for f in range(subs):
            for n, at in enumerate(SIDE_AT + CORNER_AT):
                index = halo_ref[f, at]
                sub = lax.shift_right_logical(index, 6)
                device = lax.shift_right_logical(sub * THIRD, 7)
                row = (lax.shift_right_logical(device, 1) * 2 * subs + sub - device * subs) * 4 * SIDE
                row += index & (3 * SIDE)
                plan_ref[(side * subs + f) * 8 + n] = jnp.where((device & 1) == core, row, -SIDE)

    for s in range(2):
        for n, ref in enumerate((own_ref, other_ref)):
            rows = slice(s * subs * CH, (s + 1) * subs * CH)
            pairs_ref[rows, n * PIX : (n + 1) * PIX] = ref[index_ref[s]].reshape(subs * CH, PIX)

    row_at = lax.broadcasted_iota(jnp.int32, (PIX, PIX), 0)
    place = lax.broadcasted_iota(jnp.int32, (8, PIX), 1)
    ahead = [row_at - inner_pixels(place + d)[0:1, :] for d in (0, INNER - PIX)]
    for t in range(TAPS):
        shift = (t // 3 - 1) * SIDE + t % 3 - 1
        taps = [jnp.where(d == shift, 1.0, 0.0).astype(jnp.bfloat16) for d in ahead]
        for s in range(2):
            first, second = (
                jnp.dot(ref[index_ref[s]].reshape(subs * CH, PIX), tap, preferred_element_type=jnp.float32)
                for ref, tap in zip((own_ref, other_ref), taps)
            )
            columns = (first[:, :CH], first[:, CH:] + second[:, :CH], second[:, CH:])
            for n, values in enumerate(columns):
                values = values.astype(jnp.bfloat16)
                for f in range(subs):
                    at = (s * subs + f) * 2 * INNER + n * CH
                    patches[t * CH : (t + 1) * CH, at : at + CH] = values[f * CH : (f + 1) * CH, :]
    owned_rows(core, patches, owned)
    copies = []
    for n, taps in enumerate(tap_blocks()):
        right = patches[taps.start * CH : taps.stop * CH, :]
        block = lax.dot_general(owned[...], right, NT, preferred_element_type=jnp.float32)
        for l in range(taps.stop - taps.start):
            gram[taps.start + l, :, :] = block[:, l * CH : (l + 1) * CH]
        copies.append(pltpu.make_async_copy(gram.at[taps], gram_ref.at[taps], sems.at[n]))
        copies[-1].start()
    for copy in copies:
        copy.wait()


def gather_kernel(subs, plan_ref, table_ref, tiles_ref):
    zero = jnp.zeros((SIDE, CH), jnp.bfloat16)
    for f in range(2 * subs):
        for n in range(8):
            row = plan_ref[f * 8 + n]
            near = row >= 0
            row = jnp.maximum(row, 0)
            for s in range(2):
                at = pl.multiple_of(row + s * subs * 4 * SIDE, SIDE)
                u = (f // subs * 2 + s) * subs + f % subs
                tiles_ref[u * CH + n * SIDE : u * CH + (n + 1) * SIDE, :] = jnp.where(near, table_ref[pl.ds(at, SIDE), :], zero)


def rim_kernel(subs, pairs_ref, after_ref, inner_ref, rim_ref, matrix_ref, energy_ref, gram_ref, pixels, sem):
    copy = pltpu.make_async_copy(inner_ref.at[tap_blocks()[0]], gram_ref, sem)
    copy.start()
    for t in range(TAPS):
        pixel, cycle = rim_sources(t)
        pixels[:, t * CH : (t + 1) * CH] = one_hot(2 * PIX, pixel)
        matrix_ref[:, t * CH : (t + 1) * CH] = one_hot(2 * CH, cycle)
    energy = jnp.zeros((CH, CH), jnp.float32)
    for p in range(2 * subs):
        x = pairs_ref[p * CH : (p + 1) * CH, :].astype(jnp.float32)
        for n in range(4):
            energy += x[:, n * CH : (n + 1) * CH] * x[:, n * CH : (n + 1) * CH]
    energy_ref[...] = energy
    values = jnp.dot(pairs_ref[...], pixels[...], preferred_element_type=jnp.float32).astype(jnp.bfloat16)
    for p in range(2 * subs):
        for t in range(TAPS):
            part = values[p * CH : (p + 1) * CH, t * CH : (t + 1) * CH]
            rim_ref[t * CH : (t + 1) * CH, p * CH : (p + 1) * CH] = part
    copy.wait()


def outer_kernel(
    subs,
    tiles_own_ref,
    tiles_other_ref,
    halo_rows_own_ref,
    halo_rows_other_ref,
    matrix_ref,
    energy_ref,
    mask_ref,
    rim_ref,
    first_ref,
    inner_ref,
    message_ref,
    patches,
    owned,
    gram,
    stage,
    position,
    cycles,
    inner,
    sems,
):
    core = core_index()
    units = 4 * subs
    half = units // 2
    copies = []
    for n, taps in enumerate(tap_blocks()[1:]):
        copies.append(pltpu.make_async_copy(inner_ref.at[taps], inner.at[taps], sems.at[n]))
        copies[-1].start()

    lane = lax.broadcasted_iota(jnp.int32, (8, CH), 1)
    base = jnp.full((8, CH), -1000, jnp.int32)
    for e, at in enumerate(SIDE_AT):
        base = jnp.where((lane >= at) & (lane < at + SIDE), e * SIDE, base)
    for e, at in enumerate(CORNER_AT):
        base = jnp.where(lane == at, (4 + e) * SIDE, base)
    position[...] = jnp.zeros((8, CH), jnp.int32)
    position[0:subs, 0:CYCLE] = lax.rem(halo_rows_own_ref[...], SIDE)
    position[subs : 2 * subs, 0:CYCLE] = lax.rem(halo_rows_other_ref[...], SIDE)
    source = position[...] + base

    row_at = lax.broadcasted_iota(jnp.int32, (CH, CH), 0)
    col_at = lax.broadcasted_iota(jnp.int32, (CH, CH), 1)
    diagonal = row_at == col_at
    eye = jnp.where(diagonal, 1.0, 0.0).astype(jnp.bfloat16)
    split = units * CH // 2
    energy = energy_ref[...]
    for side, (mine, theirs) in enumerate(((0, split), (split, 0))):
        tiles = tiles_own_ref[mine : mine + split, :] + tiles_other_ref[theirs : theirs + split, :]
        tiles = lax.dot_general(eye, tiles, NT, preferred_element_type=jnp.float32).astype(jnp.bfloat16)
        for p in range(half):
            at = side * subs + p % subs
            pick = jnp.where(row_at == source[at : at + 1, :], 1.0, 0.0).astype(jnp.bfloat16)
            cycle = jnp.dot(tiles[:, p * CH : (p + 1) * CH], pick, preferred_element_type=jnp.float32)
            energy += cycle * cycle
            cycles[p * CH : (p + 1) * CH, side * CH : (side + 1) * CH] = cycle.astype(jnp.bfloat16)

    values = jnp.dot(cycles[...], matrix_ref[...], preferred_element_type=jnp.float32).astype(jnp.bfloat16)
    for p in range(half):
        for t in range(TAPS):
            part = values[p * CH : (p + 1) * CH, t * CH : (t + 1) * CH]
            place = (slice(t * CH, (t + 1) * CH), slice(p * CH, (p + 1) * CH))
            patches[place] = rim_ref[place] + part

    kept = mask_ref[...].astype(jnp.float32)
    kept_row = jnp.sum(jnp.where(diagonal, kept, 0.0), axis=1, keepdims=True)
    energy = jnp.sum(energy, axis=1, keepdims=True)

    def exponent(values):
        top = jnp.full((8, CH), jnp.maximum(jnp.max(values), 2.0**-120), jnp.float32)
        return jnp.ceil(jnp.log2(top) * (STEPS / 2) + 0.1)

    kept_exp = exponent(jnp.where(kept_row > 0, energy, 0.0))
    any_exp = exponent(energy)
    lane_exps = jnp.where(kept > 0, kept_exp, any_exp) + kept_exp
    scale = jnp.exp2(lane_exps * (-1 / STEPS))

    def coded(values):
        return jnp.round(TOP * values * lax.rsqrt(jnp.maximum(jnp.abs(values), 1e-30)))

    owned_rows(core, patches, owned)
    for n, taps in enumerate(tap_blocks()):
        right = patches[taps.start * CH : taps.stop * CH, :]
        block = lax.dot_general(owned[...], right, NT, preferred_element_type=jnp.float32)
        if n > 0:
            copies[n - 1].wait()
        for l in range(taps.stop - taps.start):
            part = block[:, l * CH : (l + 1) * CH] + (inner if n > 0 else first_ref)[taps.start + l, :, :]
            gram[taps.start + l, :, :] = coded(part * scale[0:1, :])

    for j in range(message_ref.shape[0]):
        block = stage.at[j % 4]
        for l in range(TAPS):
            block[l * 9 : (l + 1) * 9, :] = gram[l, j * 9 : (j + 1) * 9, :]
        block[81:88, :] = lane_exps[0:7, :]
        message_ref[j] = block[...].astype(jnp.int32).astype(jnp.int16)


def rows_kernel(count, landed_ref, weight_ref, kept_ref, out_ref, rows, split):
    owner = lax.axis_index("face") * lax.axis_size("sample") + lax.axis_index("sample")
    total = jnp.zeros((ROWS, CH), jnp.float32)
    for j in range(landed_ref.shape[0]):
        codes = landed_ref[j].astype(jnp.int32).astype(jnp.float32)
        scale = jnp.exp2(codes[80:88, :] * (1 / STEPS))
        total += codes * jnp.abs(codes) * scale[1:2, :]
    total = total * TOP**-2
    rows[...] = jnp.zeros_like(rows)
    for l in range(TAPS):
        rows[0:9, l * CH : (l + 1) * CH] = total[l * 9 : (l + 1) * 9, :]

    channel = lax.rem(owner * 9 + lax.broadcasted_iota(jnp.int32, (16, CH), 0), CH)
    own = lax.broadcasted_iota(jnp.int32, (16, CH), 1) == channel
    keep = jnp.sum(jnp.where(own, kept_ref[...].astype(jnp.float32), 0.0), axis=1, keepdims=True)
    whole = rows[...]
    head = whole.astype(jnp.bfloat16)
    left = whole - head.astype(jnp.float32)
    tail = left.astype(jnp.bfloat16)
    split[0:16, :] = head
    split[16:32, :] = tail
    split[32:48, :] = (left - tail.astype(jnp.float32)).astype(jnp.bfloat16)
    product = jnp.dot(split[...], weight_ref[...], preferred_element_type=jnp.float32)
    product = product[32:48, :] + product[16:32, :] + product[0:16, :]
    kept = kept_ref[...] > 0
    for t in range(TAPS):
        part = whole[:, t * CH : (t + 1) * CH]
        part = jnp.where((keep > 0) & kept, part / count, 0.0)
        out_ref[:, t * CH : (t + 1) * CH] = part[0:9, :]
    for n in range(2):
        part = product[:, n * CH : (n + 1) * CH]
        part = jnp.where(keep > 0, part / count, 0.0)
        out_ref[:, K + n * CH : K + (n + 1) * CH] = part[0:9, :]


VMEM = pl.BlockSpec(memory_space=pltpu.VMEM)
SMEM = pl.BlockSpec(memory_space=pltpu.SMEM)
HBM = pl.BlockSpec(memory_space=pltpu.HBM)


def shape(dims, kind):
    return jax.ShapeDtypeStruct(dims, kind)


def per_device(fields, sample_index, halo_index, channel_mask, weight):
    faces, samples = lax.axis_size("face"), lax.axis_size("sample")
    subs = fields.shape[1]
    units = 4 * subs
    swap = [(f, f ^ 1) for f in range(faces)]
    bf16, f32 = jnp.bfloat16, jnp.float32

    other = lax.ppermute(fields, "face", swap)
    halo_other = lax.ppermute(halo_index, "face", swap)
    copies = pl.pallas_call(
        edges_kernel,
        out_shape=shape((faces // 2, 8 * subs * SIDE, CH), bf16),
        in_specs=[SMEM, VMEM],
        out_specs=VMEM,
        compiler_params=pltpu.CompilerParams(vmem_limit_bytes=8 * 2**20),
        name="edges",
    )(*(pltpu.with_memory_space_constraint(a, pltpu.HBM) for a in (sample_index, fields)))

    same_core = [[f for f in range(c, faces, 2)] for c in range(2)]
    table = lax.all_to_all(copies, "face", 0, 0, axis_index_groups=same_core)

    mask_row = channel_mask[None]
    inner, pairs, plan = pl.pallas_call(
        inner_kernel,
        out_shape=(
            pltpu.HBM((TAPS, HALF, CH), f32),
            shape((units * CH // 2, 2 * PIX), bf16),
            shape((2 * subs * 8,), jnp.int32),
        ),
        in_specs=[SMEM] * 3 + [VMEM] * 2,
        out_specs=(HBM, VMEM, SMEM),
        scratch_shapes=[
            pltpu.VMEM((K, units * INNER), bf16),
            pltpu.VMEM((HALF, units * INNER), bf16),
            pltpu.VMEM((TAPS, HALF, CH), f32),
            pltpu.SemaphoreType.DMA((3,)),
        ],
        compiler_params=pltpu.CompilerParams(vmem_limit_bytes=32 * 2**20),
        cost_estimate=pl.CostEstimate(flops=6 * 10**9, bytes_accessed=5 * 10**6, transcendentals=0),
        name="inner",
    )(sample_index, halo_index, halo_other, fields, other)

    tiles = pl.pallas_call(
        functools.partial(gather_kernel, subs),
        out_shape=shape((units * CH, CH), bf16),
        in_specs=[SMEM, VMEM],
        out_specs=VMEM,
        compiler_params=pltpu.CompilerParams(vmem_limit_bytes=4 * 2**20),
        name="gather",
    )(plan, table.reshape(-1, CH))
    tiles_other = lax.ppermute(tiles, "face", swap)

    inner = pltpu.with_memory_space_constraint(inner, pltpu.HBM)
    rim, matrix, energy, first = pl.pallas_call(
        functools.partial(rim_kernel, subs),
        out_shape=(
            shape((K, units * RIM), bf16),
            shape((2 * CH, K), bf16),
            shape((CH, CH), f32),
            shape((tap_blocks()[0].stop, HALF, CH), f32),
        ),
        in_specs=[VMEM, pl.BlockSpec(memory_space=pl.ANY), HBM],
        out_specs=(VMEM, VMEM, VMEM, VMEM),
        scratch_shapes=[pltpu.VMEM((2 * PIX, K), bf16), pltpu.SemaphoreType.DMA],
        compiler_params=pltpu.CompilerParams(vmem_limit_bytes=16 * 2**20),
        cost_estimate=pl.CostEstimate(flops=10**9, bytes_accessed=6 * 10**6, transcendentals=0),
        name="rim",
    )(pairs, tiles, inner)

    message = pl.pallas_call(
        functools.partial(outer_kernel, subs),
        out_shape=shape((64, ROWS, CH), jnp.int16),
        in_specs=[VMEM] * 9 + [HBM],
        out_specs=VMEM,
        scratch_shapes=[
            pltpu.VMEM((K, units * RIM), bf16),
            pltpu.VMEM((HALF, units * RIM), bf16),
            pltpu.VMEM((TAPS, HALF, CH), f32),
            pltpu.VMEM((4, ROWS, CH), f32),
            pltpu.VMEM((8, CH), jnp.int32),
            pltpu.VMEM((units * CH // 2, 2 * CH), bf16),
            pltpu.VMEM((TAPS, HALF, CH), f32),
            pltpu.SemaphoreType.DMA((2,)),
        ],
        compiler_params=pltpu.CompilerParams(vmem_limit_bytes=28 * 2**20),
        name="outer",
    )(
        tiles,
        tiles_other,
        halo_index,
        halo_other,
        matrix,
        energy,
        mask_row,
        rim,
        first,
        inner,
    )

    groups = [[f * samples + s for f in range(c, faces, 2) for s in range(samples)] for c in range(2)]
    landed = lax.all_to_all(message, AXES, 0, 0, axis_index_groups=groups)
    count = 2 * subs * PIX * faces * samples
    return pl.pallas_call(
        functools.partial(rows_kernel, count),
        out_shape=shape((9, K + weight.shape[1]), f32),
        in_specs=[VMEM] * 3,
        out_specs=VMEM,
        scratch_shapes=[pltpu.VMEM((16, K), f32), pltpu.VMEM((48, K), bf16)],
        compiler_params=pltpu.CompilerParams(vmem_limit_bytes=8 * 2**20),
        name="rows",
    )(landed, weight, mask_row)


def solution(mesh):
    placed = (P("sample", "face", None, None), P("sample"), P("face", None), P(), P())
    return jax.shard_map(
        per_device,
        mesh=mesh,
        in_specs=placed,
        out_specs=P(("face", "sample"), None),
        check_vma=False,
    )
```

```python
import functools

import jax
import jax.numpy as jnp
import ml_dtypes
import numpy as np
from jax import lax
from jax.experimental import pallas as pl
from jax.experimental.pallas import tpu as pltpu
from jax.sharding import PartitionSpec as P

SIDE = 16
PIX = SIDE * SIDE
CH = 128
TAPS = 9
K = TAPS * CH
HALF = K // 2
CYCLE = 4 * SIDE + 4
RIM = 64
INNER = PIX - RIM
ROWS = 82
STEPS = 16
TOP = 32700.0
THIRD = 43
AXES = ("face", "sample")
NT = (((1,), (1,)), ((), ()))
SIDE_AT = (1, 19, 36, 52)
CORNER_AT = (0, 17, 18, 35)


def rim_sources(tap):
    lane = lax.broadcasted_iota(jnp.int32, (8, CH), 1)
    second = lane >= RIM
    place = lax.rem(lane, RIM)
    along = lax.rem(place, SIDE)
    side = place // SIDE
    y = jnp.where(side == 0, 0, jnp.where(side == 1, SIDE - 1, along))
    x = jnp.where(side == 2, 0, jnp.where(side == 3, SIDE - 1, along))
    corner = (side >= 2) & ((along == 0) | (along == SIDE - 1))
    y = jnp.where(corner, jnp.clip(along, 1, SIDE - 2), y)
    x = jnp.where(corner, jnp.where(side == 2, 1, SIDE - 2), x)
    u, v = y + tap // 3 - 1, x + tap % 3 - 1
    inside = (u >= 0) & (u < SIDE) & (v >= 0) & (v < SIDE)
    entry = jnp.where(v < 0, 2 * SIDE + 4 + u, 3 * SIDE + 4 + u)
    entry = jnp.where(u < 0, v + 1, jnp.where(u >= SIDE, SIDE + 3 + v, entry))
    pixel = jnp.where(inside, u * SIDE + v + jnp.where(second, PIX, 0), -1)
    cycle = jnp.where(inside, -1, entry + jnp.where(second, CH, 0))
    return pixel[0:1, :], cycle[0:1, :]


def inner_pixels(place):
    rest = place - 2 * (SIDE - 4)
    row = lax.shift_right_logical(jnp.maximum(rest, 0) * 147, 11)
    y = jnp.where(place < SIDE - 4, 1, jnp.where(rest < 0, SIDE - 2, row + 2))
    x = jnp.where(place < SIDE - 4, place + 2, jnp.where(rest < 0, place - SIDE + 6, rest - row * (SIDE - 2) + 1))
    return jnp.where((place >= 0) & (place < INNER), y * SIDE + x, -PIX)


def one_hot(rows, source):
    at = lax.broadcasted_iota(jnp.int32, (rows, CH), 0)
    return jnp.where(at == source, 1.0, 0.0).astype(jnp.bfloat16)


def edges_kernel(index_ref, fields_ref, copies_ref):
    subs = fields_ref.shape[1]
    row = lax.broadcasted_iota(jnp.int32, (4 * SIDE, PIX), 0)
    pixel = lax.broadcasted_iota(jnp.int32, (4 * SIDE, PIX), 1)
    along = row & (SIDE - 1)
    wanted = jnp.where(row < SIDE, along, (SIDE - 1) * SIDE + along)
    wanted = jnp.where(row >= 2 * SIDE, along * SIDE, wanted)
    wanted = jnp.where(row >= 3 * SIDE, along * SIDE + SIDE - 1, wanted)
    pick = jnp.where(pixel == wanted, 1.0, 0.0).astype(jnp.bfloat16)
    for s in range(2):
        for f in range(subs):
            x = fields_ref[index_ref[s], f]
            u = s * subs + f
            edges = lax.dot_general(pick, x, NT, preferred_element_type=jnp.float32)
            edges = edges.astype(jnp.bfloat16)
            for d in range(copies_ref.shape[0]):
                copies_ref[d, u * 4 * SIDE : (u + 1) * 4 * SIDE, :] = edges


def owned_rows(core, patches, owned):
    for c in range(2):

        @pl.when(core == c)
        def _():
            for g in range(K // 144):
                owned[g * 72 : (g + 1) * 72, :] = patches[g * 144 + c * 72 : g * 144 + c * 72 + 72, :]


def tap_blocks():
    return [slice(0, 4), slice(4, 8), slice(8, TAPS)]


def core_index():
    return lax.axis_index("face") & 1


def inner_kernel(
    index_ref,
    halo_own_ref,
    halo_other_ref,
    own_ref,
    other_ref,
    gram_ref,
    pairs_ref,
    plan_ref,
    patches,
    owned,
    gram,
    sems,
):
    subs = own_ref.shape[1]
    core = core_index()

    for side, halo_ref in enumerate((halo_own_ref, halo_other_ref)):
        for f in range(subs):
            for n, at in enumerate(SIDE_AT + CORNER_AT):
                index = halo_ref[f, at]
                sub = lax.shift_right_logical(index, 6)
                device = lax.shift_right_logical(sub * THIRD, 7)
                row = (lax.shift_right_logical(device, 1) * 2 * subs + sub - device * subs) * 4 * SIDE
                row += index & (3 * SIDE)
                plan_ref[(side * subs + f) * 8 + n] = jnp.where((device & 1) == core, row, -SIDE)

    for s in range(2):
        for n, ref in enumerate((own_ref, other_ref)):
            rows = slice(s * subs * CH, (s + 1) * subs * CH)
            pairs_ref[rows, n * PIX : (n + 1) * PIX] = ref[index_ref[s]].reshape(subs * CH, PIX)

    row_at = lax.broadcasted_iota(jnp.int32, (PIX, PIX), 0)
    place = lax.broadcasted_iota(jnp.int32, (8, PIX), 1)
    ahead = [row_at - inner_pixels(place + d)[0:1, :] for d in (0, INNER - PIX)]
    for t in range(TAPS):
        shift = (t // 3 - 1) * SIDE + t % 3 - 1
        taps = [jnp.where(d == shift, 1.0, 0.0).astype(jnp.bfloat16) for d in ahead]
        for s in range(2):
            first, second = (
                jnp.dot(ref[index_ref[s]].reshape(subs * CH, PIX), tap, preferred_element_type=jnp.float32)
                for ref, tap in zip((own_ref, other_ref), taps)
            )
            columns = (first[:, :CH], first[:, CH:] + second[:, :CH], second[:, CH:])
            for n, values in enumerate(columns):
                values = values.astype(jnp.bfloat16)
                for f in range(subs):
                    at = (s * subs + f) * 2 * INNER + n * CH
                    patches[t * CH : (t + 1) * CH, at : at + CH] = values[f * CH : (f + 1) * CH, :]
    owned_rows(core, patches, owned)
    copies = []
    for n, taps in enumerate(tap_blocks()):
        right = patches[taps.start * CH : taps.stop * CH, :]
        block = lax.dot_general(owned[...], right, NT, preferred_element_type=jnp.float32)
        for l in range(taps.stop - taps.start):
            gram[taps.start + l, :, :] = block[:, l * CH : (l + 1) * CH]
        copies.append(pltpu.make_async_copy(gram.at[taps], gram_ref.at[taps], sems.at[n]))
        copies[-1].start()
    for copy in copies:
        copy.wait()


def gather_kernel(subs, plan_ref, table_ref, tiles_ref):
    zero = jnp.zeros((SIDE, CH), jnp.bfloat16)
    for f in range(2 * subs):
        for n in range(8):
            row = plan_ref[f * 8 + n]
            near = row >= 0
            row = jnp.maximum(row, 0)
            for s in range(2):
                at = pl.multiple_of(row + s * subs * 4 * SIDE, SIDE)
                u = (f // subs * 2 + s) * subs + f % subs
                tiles_ref[u * CH + n * SIDE : u * CH + (n + 1) * SIDE, :] = jnp.where(near, table_ref[pl.ds(at, SIDE), :], zero)


def rim_kernel(subs, pairs_ref, after_ref, inner_ref, rim_ref, matrix_ref, energy_ref, gram_ref, pixels, sem):
    copy = pltpu.make_async_copy(inner_ref.at[tap_blocks()[0]], gram_ref, sem)
    copy.start()
    for t in range(TAPS):
        pixel, cycle = rim_sources(t)
        pixels[:, t * CH : (t + 1) * CH] = one_hot(2 * PIX, pixel)
        matrix_ref[:, t * CH : (t + 1) * CH] = one_hot(2 * CH, cycle)
    energy = jnp.zeros((CH, CH), jnp.float32)
    for p in range(2 * subs):
        x = pairs_ref[p * CH : (p + 1) * CH, :].astype(jnp.float32)
        for n in range(4):
            energy += x[:, n * CH : (n + 1) * CH] * x[:, n * CH : (n + 1) * CH]
    energy_ref[...] = energy
    values = jnp.dot(pairs_ref[...], pixels[...], preferred_element_type=jnp.float32).astype(jnp.bfloat16)
    for p in range(2 * subs):
        for t in range(TAPS):
            part = values[p * CH : (p + 1) * CH, t * CH : (t + 1) * CH]
            rim_ref[t * CH : (t + 1) * CH, p * CH : (p + 1) * CH] = part
    copy.wait()


def outer_kernel(
    subs,
    tiles_own_ref,
    tiles_other_ref,
    halo_rows_own_ref,
    halo_rows_other_ref,
    matrix_ref,
    energy_ref,
    mask_ref,
    rim_ref,
    first_ref,
    inner_ref,
    message_ref,
    patches,
    owned,
    gram,
    stage,
    position,
    cycles,
    inner,
    sems,
):
    core = core_index()
    units = 4 * subs
    half = units // 2
    copies = []
    for n, taps in enumerate(tap_blocks()[1:]):
        copies.append(pltpu.make_async_copy(inner_ref.at[taps], inner.at[taps], sems.at[n]))
        copies[-1].start()

    lane = lax.broadcasted_iota(jnp.int32, (8, CH), 1)
    base = jnp.full((8, CH), -1000, jnp.int32)
    for e, at in enumerate(SIDE_AT):
        base = jnp.where((lane >= at) & (lane < at + SIDE), e * SIDE, base)
    for e, at in enumerate(CORNER_AT):
        base = jnp.where(lane == at, (4 + e) * SIDE, base)
    position[...] = jnp.zeros((8, CH), jnp.int32)
    position[0:subs, 0:CYCLE] = lax.rem(halo_rows_own_ref[...], SIDE)
    position[subs : 2 * subs, 0:CYCLE] = lax.rem(halo_rows_other_ref[...], SIDE)
    source = position[...] + base

    row_at = lax.broadcasted_iota(jnp.int32, (CH, CH), 0)
    col_at = lax.broadcasted_iota(jnp.int32, (CH, CH), 1)
    diagonal = row_at == col_at
    eye = jnp.where(diagonal, 1.0, 0.0).astype(jnp.bfloat16)
    split = units * CH // 2
    energy = energy_ref[...]
    for side, (mine, theirs) in enumerate(((0, split), (split, 0))):
        tiles = tiles_own_ref[mine : mine + split, :] + tiles_other_ref[theirs : theirs + split, :]
        tiles = lax.dot_general(eye, tiles, NT, preferred_element_type=jnp.float32).astype(jnp.bfloat16)
        for p in range(half):
            at = side * subs + p % subs
            pick = jnp.where(row_at == source[at : at + 1, :], 1.0, 0.0).astype(jnp.bfloat16)
            cycle = jnp.dot(tiles[:, p * CH : (p + 1) * CH], pick, preferred_element_type=jnp.float32)
            energy += cycle * cycle
            cycles[p * CH : (p + 1) * CH, side * CH : (side + 1) * CH] = cycle.astype(jnp.bfloat16)

    values = jnp.dot(cycles[...], matrix_ref[...], preferred_element_type=jnp.float32).astype(jnp.bfloat16)
    for p in range(half):
        for t in range(TAPS):
            part = values[p * CH : (p + 1) * CH, t * CH : (t + 1) * CH]
            place = (slice(t * CH, (t + 1) * CH), slice(p * CH, (p + 1) * CH))
            patches[place] = rim_ref[place] + part

    kept = mask_ref[...].astype(jnp.float32)
    kept_row = jnp.sum(jnp.where(diagonal, kept, 0.0), axis=1, keepdims=True)
    energy = jnp.sum(energy, axis=1, keepdims=True)

    def exponent(values):
        top = jnp.full((8, CH), jnp.maximum(jnp.max(values), 2.0**-120), jnp.float32)
        return jnp.ceil(jnp.log2(top) * (STEPS / 2) + 0.1)

    kept_exp = exponent(jnp.where(kept_row > 0, energy, 0.0))
    any_exp = exponent(energy)
    lane_exps = jnp.where(kept > 0, kept_exp, any_exp) + kept_exp
    scale = jnp.exp2(lane_exps * (-1 / STEPS))

    def coded(values):
        return jnp.round(TOP * values * lax.rsqrt(jnp.maximum(jnp.abs(values), 1e-30)))

    owned_rows(core, patches, owned)
    for n, taps in enumerate(tap_blocks()):
        right = patches[taps.start * CH : taps.stop * CH, :]
        block = lax.dot_general(owned[...], right, NT, preferred_element_type=jnp.float32)
        if n > 0:
            copies[n - 1].wait()
        for l in range(taps.stop - taps.start):
            part = block[:, l * CH : (l + 1) * CH] + (inner if n > 0 else first_ref)[taps.start + l, :, :]
            gram[taps.start + l, :, :] = coded(part * scale[0:1, :])

    for j in range(message_ref.shape[0] // ROWS):
        block = stage.at[j % 4]
        for l in range(TAPS):
            block[l * 9 : (l + 1) * 9, :] = gram[l, j * 9 : (j + 1) * 9, :]
        block[81:88, :] = lane_exps[0:7, :]
        message_ref[j * ROWS : (j + 1) * ROWS, :] = block[:ROWS, :].astype(jnp.int32).astype(jnp.int16)


def rows_kernel(count, landed_ref, weight_ref, kept_ref, out_ref, rows, split):
    owner = lax.axis_index("face") * lax.axis_size("sample") + lax.axis_index("sample")
    total = jnp.zeros((ROWS, CH), jnp.float32)
    for j in range(landed_ref.shape[0] // ROWS):
        codes = landed_ref[j * ROWS : (j + 1) * ROWS, :].astype(jnp.int32).astype(jnp.float32)
        scale = jnp.exp2(codes[80:82, :] * (1 / STEPS))
        total += codes * jnp.abs(codes) * scale[1:2, :]
    total = total * TOP**-2
    rows[...] = jnp.zeros_like(rows)
    for l in range(TAPS):
        rows[0:9, l * CH : (l + 1) * CH] = total[l * 9 : (l + 1) * 9, :]

    channel = lax.rem(owner * 9 + lax.broadcasted_iota(jnp.int32, (16, CH), 0), CH)
    own = lax.broadcasted_iota(jnp.int32, (16, CH), 1) == channel
    keep = jnp.sum(jnp.where(own, kept_ref[...].astype(jnp.float32), 0.0), axis=1, keepdims=True)
    whole = rows[...]
    head = whole.astype(jnp.bfloat16)
    left = whole - head.astype(jnp.float32)
    tail = left.astype(jnp.bfloat16)
    split[0:16, :] = head
    split[16:32, :] = tail
    split[32:48, :] = (left - tail.astype(jnp.float32)).astype(jnp.bfloat16)
    product = jnp.dot(split[...], weight_ref[...], preferred_element_type=jnp.float32)
    product = product[32:48, :] + product[16:32, :] + product[0:16, :]
    kept = kept_ref[...] > 0
    for t in range(TAPS):
        part = whole[:, t * CH : (t + 1) * CH]
        part = jnp.where((keep > 0) & kept, part / count, 0.0)
        out_ref[:, t * CH : (t + 1) * CH] = part[0:9, :]
    for n in range(2):
        part = product[:, n * CH : (n + 1) * CH]
        part = jnp.where(keep > 0, part / count, 0.0)
        out_ref[:, K + n * CH : K + (n + 1) * CH] = part[0:9, :]


VMEM = pl.BlockSpec(memory_space=pltpu.VMEM)
SMEM = pl.BlockSpec(memory_space=pltpu.SMEM)
HBM = pl.BlockSpec(memory_space=pltpu.HBM)


def shape(dims, kind):
    return jax.ShapeDtypeStruct(dims, kind)


def per_device(fields, sample_index, halo_index, channel_mask, weight):
    faces, samples = lax.axis_size("face"), lax.axis_size("sample")
    subs = fields.shape[1]
    units = 4 * subs
    swap = [(f, f ^ 1) for f in range(faces)]
    bf16, f32 = jnp.bfloat16, jnp.float32

    other = lax.ppermute(fields, "face", swap)
    halo_other = lax.ppermute(halo_index, "face", swap)
    copies = pl.pallas_call(
        edges_kernel,
        out_shape=shape((faces // 2, 8 * subs * SIDE, CH), bf16),
        in_specs=[SMEM, VMEM],
        out_specs=VMEM,
        compiler_params=pltpu.CompilerParams(vmem_limit_bytes=8 * 2**20),
        name="edges",
    )(*(pltpu.with_memory_space_constraint(a, pltpu.HBM) for a in (sample_index, fields)))

    same_core = [[f for f in range(c, faces, 2)] for c in range(2)]
    table = lax.all_to_all(copies, "face", 0, 0, axis_index_groups=same_core)

    mask_row = channel_mask[None]
    inner, pairs, plan = pl.pallas_call(
        inner_kernel,
        out_shape=(
            pltpu.HBM((TAPS, HALF, CH), f32),
            shape((units * CH // 2, 2 * PIX), bf16),
            shape((2 * subs * 8,), jnp.int32),
        ),
        in_specs=[SMEM] * 3 + [VMEM] * 2,
        out_specs=(HBM, VMEM, SMEM),
        scratch_shapes=[
            pltpu.VMEM((K, units * INNER), bf16),
            pltpu.VMEM((HALF, units * INNER), bf16),
            pltpu.VMEM((TAPS, HALF, CH), f32),
            pltpu.SemaphoreType.DMA((3,)),
        ],
        compiler_params=pltpu.CompilerParams(vmem_limit_bytes=32 * 2**20),
        cost_estimate=pl.CostEstimate(flops=6 * 10**9, bytes_accessed=5 * 10**6, transcendentals=0),
        name="inner",
    )(sample_index, halo_index, halo_other, fields, other)

    tiles = pl.pallas_call(
        functools.partial(gather_kernel, subs),
        out_shape=shape((units * CH, CH), bf16),
        in_specs=[SMEM, VMEM],
        out_specs=VMEM,
        compiler_params=pltpu.CompilerParams(vmem_limit_bytes=4 * 2**20),
        name="gather",
    )(plan, table.reshape(-1, CH))
    tiles_other = lax.ppermute(tiles, "face", swap)

    inner = pltpu.with_memory_space_constraint(inner, pltpu.HBM)
    rim, matrix, energy, first = pl.pallas_call(
        functools.partial(rim_kernel, subs),
        out_shape=(
            shape((K, units * RIM), bf16),
            shape((2 * CH, K), bf16),
            shape((CH, CH), f32),
            shape((tap_blocks()[0].stop, HALF, CH), f32),
        ),
        in_specs=[VMEM, pl.BlockSpec(memory_space=pl.ANY), HBM],
        out_specs=(VMEM, VMEM, VMEM, VMEM),
        scratch_shapes=[pltpu.VMEM((2 * PIX, K), bf16), pltpu.SemaphoreType.DMA],
        compiler_params=pltpu.CompilerParams(vmem_limit_bytes=16 * 2**20),
        cost_estimate=pl.CostEstimate(flops=10**9, bytes_accessed=6 * 10**6, transcendentals=0),
        name="rim",
    )(pairs, tiles, inner)

    message = pl.pallas_call(
        functools.partial(outer_kernel, subs),
        out_shape=shape((64 * ROWS, CH), jnp.int16),
        in_specs=[VMEM] * 9 + [HBM],
        out_specs=VMEM,
        scratch_shapes=[
            pltpu.VMEM((K, units * RIM), bf16),
            pltpu.VMEM((HALF, units * RIM), bf16),
            pltpu.VMEM((TAPS, HALF, CH), f32),
            pltpu.VMEM((4, 88, CH), f32),
            pltpu.VMEM((8, CH), jnp.int32),
            pltpu.VMEM((units * CH // 2, 2 * CH), bf16),
            pltpu.VMEM((TAPS, HALF, CH), f32),
            pltpu.SemaphoreType.DMA((2,)),
        ],
        compiler_params=pltpu.CompilerParams(vmem_limit_bytes=28 * 2**20),
        name="outer",
    )(
        tiles,
        tiles_other,
        halo_index,
        halo_other,
        matrix,
        energy,
        mask_row,
        rim,
        first,
        inner,
    )

    groups = [[f * samples + s for f in range(c, faces, 2) for s in range(samples)] for c in range(2)]
    landed = lax.all_to_all(message.reshape(64, -1, 2, CH), AXES, 0, 0, axis_index_groups=groups).reshape(-1, CH)
    count = 2 * subs * PIX * faces * samples
    return pl.pallas_call(
        functools.partial(rows_kernel, count),
        out_shape=shape((9, K + weight.shape[1]), f32),
        in_specs=[VMEM] * 3,
        out_specs=VMEM,
        scratch_shapes=[pltpu.VMEM((16, K), f32), pltpu.VMEM((48, K), bf16)],
        compiler_params=pltpu.CompilerParams(vmem_limit_bytes=8 * 2**20),
        name="rows",
    )(landed, weight, mask_row)


def solution(mesh):
    placed = (P("sample", "face", None, None), P("sample"), P("face", None), P(), P())
    return jax.shard_map(
        per_device,
        mesh=mesh,
        in_specs=placed,
        out_specs=P(("face", "sample"), None),
        check_vma=False,
    )
```

```python
import functools

import jax
import jax.numpy as jnp
import ml_dtypes
import numpy as np
from jax import lax
from jax.experimental import pallas as pl
from jax.experimental.pallas import tpu as pltpu
from jax.sharding import PartitionSpec as P

SIDE = 16
PIX = SIDE * SIDE
CH = 128
TAPS = 9
K = TAPS * CH
HALF = K // 2
CYCLE = 4 * SIDE + 4
RIM = 64
INNER = PIX - RIM
ROWS = 82
STEPS = 16
TOP = 32700.0
THIRD = 43
GROUP = 4
AXES = ("face", "sample")
NT = (((1,), (1,)), ((), ()))
SIDE_AT = (1, 19, 36, 52)
CORNER_AT = (0, 17, 18, 35)


def rim_sources(tap):
    lane = lax.broadcasted_iota(jnp.int32, (8, CH), 1)
    second = lane >= RIM
    place = lax.rem(lane, RIM)
    along = lax.rem(place, SIDE)
    side = place // SIDE
    y = jnp.where(side == 0, 0, jnp.where(side == 1, SIDE - 1, along))
    x = jnp.where(side == 2, 0, jnp.where(side == 3, SIDE - 1, along))
    corner = (side >= 2) & ((along == 0) | (along == SIDE - 1))
    y = jnp.where(corner, jnp.clip(along, 1, SIDE - 2), y)
    x = jnp.where(corner, jnp.where(side == 2, 1, SIDE - 2), x)
    u, v = y + tap // 3 - 1, x + tap % 3 - 1
    inside = (u >= 0) & (u < SIDE) & (v >= 0) & (v < SIDE)
    entry = jnp.where(v < 0, 2 * SIDE + 4 + u, 3 * SIDE + 4 + u)
    entry = jnp.where(u < 0, v + 1, jnp.where(u >= SIDE, SIDE + 3 + v, entry))
    pixel = jnp.where(inside, u * SIDE + v + jnp.where(second, PIX, 0), -1)
    cycle = jnp.where(inside, -1, entry + jnp.where(second, CH, 0))
    return pixel[0:1, :], cycle[0:1, :]


def inner_pixels(place):
    rest = place - 2 * (SIDE - 4)
    row = lax.shift_right_logical(jnp.maximum(rest, 0) * 147, 11)
    y = jnp.where(place < SIDE - 4, 1, jnp.where(rest < 0, SIDE - 2, row + 2))
    x = jnp.where(place < SIDE - 4, place + 2, jnp.where(rest < 0, place - SIDE + 6, rest - row * (SIDE - 2) + 1))
    return jnp.where((place >= 0) & (place < INNER), y * SIDE + x, -PIX)


def one_hot(rows, source):
    at = lax.broadcasted_iota(jnp.int32, (rows, CH), 0)
    return jnp.where(at == source, 1.0, 0.0).astype(jnp.bfloat16)


def edges_kernel(index_ref, fields_ref, copies_ref):
    subs = fields_ref.shape[1]
    row = lax.broadcasted_iota(jnp.int32, (4 * SIDE, PIX), 0)
    pixel = lax.broadcasted_iota(jnp.int32, (4 * SIDE, PIX), 1)
    along = row & (SIDE - 1)
    wanted = jnp.where(row < SIDE, along, (SIDE - 1) * SIDE + along)
    wanted = jnp.where(row >= 2 * SIDE, along * SIDE, wanted)
    wanted = jnp.where(row >= 3 * SIDE, along * SIDE + SIDE - 1, wanted)
    pick = jnp.where(pixel == wanted, 1.0, 0.0).astype(jnp.bfloat16)
    for s in range(2):
        for f in range(subs):
            x = fields_ref[index_ref[s], f]
            u = s * subs + f
            edges = lax.dot_general(pick, x, NT, preferred_element_type=jnp.float32)
            edges = edges.astype(jnp.bfloat16)
            for d in range(copies_ref.shape[0]):
                copies_ref[d, u * 4 * SIDE : (u + 1) * 4 * SIDE, :] = edges


def owned_rows(core, patches, owned):
    for c in range(2):

        @pl.when(core == c)
        def _():
            for g in range(K // 144):
                owned[g * 72 : (g + 1) * 72, :] = patches[g * 144 + c * 72 : g * 144 + c * 72 + 72, :]


def tap_blocks():
    return [slice(0, 4), slice(4, 8), slice(8, TAPS)]


def core_index():
    return lax.axis_index("face") & 1


def inner_kernel(
    index_ref,
    own_ref,
    other_ref,
    gram_ref,
    pairs_ref,
    patches,
    owned,
    gram,
    sems,
):
    subs = own_ref.shape[1]
    core = core_index()

    index = index_ref[...]
    for s in range(2):
        rows = slice(s * subs * CH, (s + 1) * subs * CH)
        chosen = [(index[:, s : s + 1] == n).astype(jnp.float32).astype(jnp.bfloat16) for n in range(own_ref.shape[0])]
        for n, ref in enumerate((own_ref, other_ref)):
            parts = [ref[k].reshape(subs * CH, PIX) * one for k, one in enumerate(chosen)]
            pairs_ref[rows, n * PIX : (n + 1) * PIX] = sum(parts[1:], parts[0])

    row_at = lax.broadcasted_iota(jnp.int32, (PIX, PIX), 0)
    place = lax.broadcasted_iota(jnp.int32, (8, PIX), 1)
    ahead = [row_at - inner_pixels(place + d)[0:1, :] for d in (0, INNER - PIX)]
    for t in range(TAPS):
        shift = (t // 3 - 1) * SIDE + t % 3 - 1
        taps = [jnp.where(d == shift, 1.0, 0.0).astype(jnp.bfloat16) for d in ahead]
        for s in range(2):
            first, second = (
                jnp.dot(
                    pairs_ref[s * subs * CH : (s + 1) * subs * CH, n * PIX : (n + 1) * PIX],
                    tap,
                    preferred_element_type=jnp.float32,
                )
                for n, tap in enumerate(taps)
            )
            columns = (first[:, :CH], first[:, CH:] + second[:, :CH], second[:, CH:])
            for n, values in enumerate(columns):
                values = values.astype(jnp.bfloat16)
                for f in range(subs):
                    at = (s * subs + f) * 2 * INNER + n * CH
                    patches[t * CH : (t + 1) * CH, at : at + CH] = values[f * CH : (f + 1) * CH, :]
    owned_rows(core, patches, owned)
    copies = []
    for n, taps in enumerate(tap_blocks()):
        right = patches[taps.start * CH : taps.stop * CH, :]
        block = lax.dot_general(owned[...], right, NT, preferred_element_type=jnp.float32)
        for l in range(taps.stop - taps.start):
            gram[taps.start + l, :, :] = block[:, l * CH : (l + 1) * CH]
        copies.append(pltpu.make_async_copy(gram.at[taps], gram_ref.at[taps], sems.at[n]))
        copies[-1].start()
    for copy in copies:
        copy.wait()


def gather_kernel(subs, halo_own_ref, halo_other_ref, table_ref, after_ref, tiles_ref):
    core = core_index()
    zero = jnp.zeros((SIDE, CH), jnp.bfloat16)
    for side, halo_ref in enumerate((halo_own_ref, halo_other_ref)):
        for f in range(subs):
            for n, at in enumerate(SIDE_AT + CORNER_AT):
                index = halo_ref[f, at]
                sub = lax.shift_right_logical(index, 6)
                device = lax.shift_right_logical(sub * THIRD, 7)
                row = (lax.shift_right_logical(device, 1) * 2 * subs + sub - device * subs) * 4 * SIDE
                row = pl.multiple_of(row + (index & (3 * SIDE)), SIDE)
                for s in range(2):
                    u = (side * 2 + s) * subs + f
                    tile = table_ref[pl.ds(pl.multiple_of(row + s * subs * 4 * SIDE, SIDE), SIDE), :]
                    tiles_ref[u * CH + n * SIDE : u * CH + (n + 1) * SIDE, :] = jnp.where((device & 1) == core, tile, zero)


def rim_kernel(subs, pairs_ref, after_ref, inner_ref, rim_ref, matrix_ref, energy_ref, gram_ref, pixels, sem):
    copy = pltpu.make_async_copy(inner_ref.at[tap_blocks()[0]], gram_ref, sem)
    copy.start()
    for t in range(TAPS):
        pixel, cycle = rim_sources(t)
        pixels[:, t * CH : (t + 1) * CH] = one_hot(2 * PIX, pixel)
        matrix_ref[:, t * CH : (t + 1) * CH] = one_hot(2 * CH, cycle)
    energy = jnp.zeros((CH, CH), jnp.float32)
    for p in range(2 * subs):
        x = pairs_ref[p * CH : (p + 1) * CH, :].astype(jnp.float32)
        for n in range(4):
            energy += x[:, n * CH : (n + 1) * CH] * x[:, n * CH : (n + 1) * CH]
    energy_ref[...] = energy
    values = jnp.dot(pairs_ref[...], pixels[...], preferred_element_type=jnp.float32).astype(jnp.bfloat16)
    for p in range(2 * subs):
        for t in range(TAPS):
            part = values[p * CH : (p + 1) * CH, t * CH : (t + 1) * CH]
            rim_ref[t * CH : (t + 1) * CH, p * CH : (p + 1) * CH] = part
    copy.wait()


def outer_kernel(
    subs,
    tiles_own_ref,
    tiles_other_ref,
    halo_rows_own_ref,
    halo_rows_other_ref,
    matrix_ref,
    energy_ref,
    mask_ref,
    rim_ref,
    first_ref,
    inner_ref,
    message_ref,
    patches,
    owned,
    gram,
    stage,
    position,
    cycles,
    inner,
    sems,
):
    core = core_index()
    units = 4 * subs
    half = units // 2
    copies = []
    for n, taps in enumerate(tap_blocks()[1:]):
        copies.append(pltpu.make_async_copy(inner_ref.at[taps], inner.at[taps], sems.at[n]))
        copies[-1].start()

    lane = lax.broadcasted_iota(jnp.int32, (8, CH), 1)
    base = jnp.full((8, CH), -1000, jnp.int32)
    for e, at in enumerate(SIDE_AT):
        base = jnp.where((lane >= at) & (lane < at + SIDE), e * SIDE, base)
    for e, at in enumerate(CORNER_AT):
        base = jnp.where(lane == at, (4 + e) * SIDE, base)
    position[...] = jnp.zeros((8, CH), jnp.int32)
    position[0:subs, 0:CYCLE] = lax.rem(halo_rows_own_ref[...], SIDE)
    position[subs : 2 * subs, 0:CYCLE] = lax.rem(halo_rows_other_ref[...], SIDE)
    source = position[...] + base

    row_at = lax.broadcasted_iota(jnp.int32, (CH, CH), 0)
    col_at = lax.broadcasted_iota(jnp.int32, (CH, CH), 1)
    diagonal = row_at == col_at
    eye = jnp.where(diagonal, 1.0, 0.0).astype(jnp.bfloat16)
    split = units * CH // 2
    energy = energy_ref[...]
    for side, (mine, theirs) in enumerate(((0, split), (split, 0))):
        tiles = tiles_own_ref[mine : mine + split, :] + tiles_other_ref[theirs : theirs + split, :]
        tiles = lax.dot_general(eye, tiles, NT, preferred_element_type=jnp.float32).astype(jnp.bfloat16)
        for p in range(half):
            at = side * subs + p % subs
            pick = jnp.where(row_at == source[at : at + 1, :], 1.0, 0.0).astype(jnp.bfloat16)
            cycle = jnp.dot(tiles[:, p * CH : (p + 1) * CH], pick, preferred_element_type=jnp.float32)
            energy += cycle * cycle
            cycles[p * CH : (p + 1) * CH, side * CH : (side + 1) * CH] = cycle.astype(jnp.bfloat16)

    values = jnp.dot(cycles[...], matrix_ref[...], preferred_element_type=jnp.float32).astype(jnp.bfloat16)
    for p in range(half):
        for t in range(TAPS):
            part = values[p * CH : (p + 1) * CH, t * CH : (t + 1) * CH]
            place = (slice(t * CH, (t + 1) * CH), slice(p * CH, (p + 1) * CH))
            patches[place] = rim_ref[place] + part

    kept = mask_ref[...].astype(jnp.float32)
    kept_row = jnp.sum(jnp.where(diagonal, kept, 0.0), axis=1, keepdims=True)
    energy = jnp.sum(energy, axis=1, keepdims=True)

    def exponent(values):
        top = jnp.full((8, CH), jnp.maximum(jnp.max(values), 2.0**-120), jnp.float32)
        return jnp.ceil(jnp.log2(top) * (STEPS / 2) + 0.1)

    kept_exp = exponent(jnp.where(kept_row > 0, energy, 0.0))
    any_exp = exponent(energy)
    lane_exps = jnp.where(kept > 0, kept_exp, any_exp) + kept_exp
    scale = jnp.exp2(lane_exps * (-1 / STEPS)) * TOP**2

    def coded(values):
        return jnp.round(values * lax.rsqrt(jnp.maximum(jnp.abs(values), 1e-30)))

    owned_rows(core, patches, owned)
    for m in range(0, HALF, HALF // 2):
        at = slice(m, m + HALF // 2)
        for n, taps in enumerate(tap_blocks()):
            right = patches[taps.start * CH : taps.stop * CH, :]
            block = lax.dot_general(owned[at, :], right, NT, preferred_element_type=jnp.float32)
            if n > 0 and m == 0:
                copies[n - 1].wait()
            for l in range(taps.stop - taps.start):
                part = block[:, l * CH : (l + 1) * CH] + (inner if n > 0 else first_ref)[taps.start + l, at, :]
                gram[taps.start + l, at, :] = coded(part * scale[0:1, :])

        for j in range(m // 9, (m + HALF // 2) // 9, GROUP):
            block = stage.at[j // GROUP % 4]
            for i in range(GROUP):
                for l in range(TAPS):
                    to = i * ROWS + l * 9
                    block[to : to + 9, :] = gram[l, (j + i) * 9 : (j + i + 1) * 9, :]
                block[i * ROWS + 81 : (i + 1) * ROWS, :] = lane_exps[0:1, :]
            message_ref[j * ROWS : (j + GROUP) * ROWS, :] = block[...].astype(jnp.int32).astype(jnp.int16)


def rows_kernel(count, landed_ref, weight_ref, kept_ref, out_ref, rows, split, stage):
    owner = lax.axis_index("face") * lax.axis_size("sample") + lax.axis_index("sample")
    total = jnp.zeros((ROWS, CH), jnp.float32)
    for j in range(0, landed_ref.shape[0] // ROWS, 2 * GROUP):
        block = stage.at[j // (2 * GROUP) % 4]
        block[...] = landed_ref[j * ROWS : (j + 2 * GROUP) * ROWS, :].astype(jnp.int32).astype(jnp.float32)
        for i in range(2 * GROUP):
            codes = block[i * ROWS : (i + 1) * ROWS, :]
            total += codes * jnp.abs(codes) * jnp.exp2(block[i * ROWS + 81 : (i + 1) * ROWS, :] * (1 / STEPS))
    total = total * TOP**-2
    rows[...] = jnp.zeros_like(rows)
    for l in range(TAPS):
        rows[0:9, l * CH : (l + 1) * CH] = total[l * 9 : (l + 1) * 9, :]

    channel = lax.rem(owner * 9 + lax.broadcasted_iota(jnp.int32, (16, CH), 0), CH)
    own = lax.broadcasted_iota(jnp.int32, (16, CH), 1) == channel
    keep = jnp.sum(jnp.where(own, kept_ref[...].astype(jnp.float32), 0.0), axis=1, keepdims=True)
    whole = rows[...]
    head = whole.astype(jnp.bfloat16)
    left = whole - head.astype(jnp.float32)
    tail = left.astype(jnp.bfloat16)
    split[0:16, :] = head
    split[16:32, :] = tail
    split[32:48, :] = (left - tail.astype(jnp.float32)).astype(jnp.bfloat16)
    product = jnp.dot(split[...], weight_ref[...], preferred_element_type=jnp.float32)
    product = product[32:48, :] + product[16:32, :] + product[0:16, :]
    kept = kept_ref[...] > 0
    for t in range(TAPS):
        part = whole[:, t * CH : (t + 1) * CH]
        part = jnp.where((keep > 0) & kept, part / count, 0.0)
        out_ref[:, t * CH : (t + 1) * CH] = part[0:9, :]
    for n in range(2):
        part = product[:, n * CH : (n + 1) * CH]
        part = jnp.where(keep > 0, part / count, 0.0)
        out_ref[:, K + n * CH : K + (n + 1) * CH] = part[0:9, :]


VMEM = pl.BlockSpec(memory_space=pltpu.VMEM)
SMEM = pl.BlockSpec(memory_space=pltpu.SMEM)
HBM = pl.BlockSpec(memory_space=pltpu.HBM)
ANY = pl.BlockSpec(memory_space=pl.ANY)


def shape(dims, kind):
    return jax.ShapeDtypeStruct(dims, kind)


def per_device(fields, sample_index, halo_index, channel_mask, weight):
    faces, samples = lax.axis_size("face"), lax.axis_size("sample")
    subs = fields.shape[1]
    units = 4 * subs
    swap = [(f, f ^ 1) for f in range(faces)]
    bf16, f32 = jnp.bfloat16, jnp.float32

    other = lax.ppermute(fields, "face", swap)
    halo_other = lax.ppermute(halo_index, "face", swap)
    copies = pl.pallas_call(
        edges_kernel,
        out_shape=shape((faces // 2, 8 * subs * SIDE, CH), bf16),
        in_specs=[SMEM, VMEM],
        out_specs=VMEM,
        compiler_params=pltpu.CompilerParams(vmem_limit_bytes=8 * 2**20),
        name="edges",
    )(*(pltpu.with_memory_space_constraint(a, pltpu.HBM) for a in (sample_index, fields)))

    same_core = [[f for f in range(c, faces, 2)] for c in range(2)]
    table = lax.all_to_all(copies, "face", 0, 0, axis_index_groups=same_core)

    mask_row = channel_mask[None]
    inner, pairs = pl.pallas_call(
        inner_kernel,
        out_shape=(
            pltpu.HBM((TAPS, HALF, CH), f32),
            shape((units * CH // 2, 2 * PIX), bf16),
        ),
        in_specs=[VMEM] * 3,
        out_specs=(HBM, VMEM),
        scratch_shapes=[
            pltpu.VMEM((K, units * INNER), bf16),
            pltpu.VMEM((HALF, units * INNER), bf16),
            pltpu.VMEM((TAPS, HALF, CH), f32),
            pltpu.SemaphoreType.DMA((3,)),
        ],
        compiler_params=pltpu.CompilerParams(vmem_limit_bytes=32 * 2**20),
        cost_estimate=pl.CostEstimate(flops=6 * 10**9, bytes_accessed=5 * 10**6, transcendentals=0),
        name="inner",
    )(sample_index[None], fields, other)

    tiles = pl.pallas_call(
        functools.partial(gather_kernel, subs),
        out_shape=shape((units * CH, CH), bf16),
        in_specs=[SMEM, SMEM, VMEM, ANY],
        out_specs=VMEM,
        compiler_params=pltpu.CompilerParams(vmem_limit_bytes=4 * 2**20),
        name="gather",
    )(halo_index, halo_other, table.reshape(-1, CH), pairs)
    tiles_other = lax.ppermute(tiles, "face", swap)

    inner = pltpu.with_memory_space_constraint(inner, pltpu.HBM)
    rim, matrix, energy, first = pl.pallas_call(
        functools.partial(rim_kernel, subs),
        out_shape=(
            shape((K, units * RIM), bf16),
            shape((2 * CH, K), bf16),
            shape((CH, CH), f32),
            shape((tap_blocks()[0].stop, HALF, CH), f32),
        ),
        in_specs=[VMEM, ANY, HBM],
        out_specs=(VMEM, VMEM, VMEM, VMEM),
        scratch_shapes=[pltpu.VMEM((2 * PIX, K), bf16), pltpu.SemaphoreType.DMA],
        compiler_params=pltpu.CompilerParams(vmem_limit_bytes=16 * 2**20),
        cost_estimate=pl.CostEstimate(flops=10**9, bytes_accessed=6 * 10**6, transcendentals=0),
        name="rim",
    )(pairs, tiles, inner)

    message = pl.pallas_call(
        functools.partial(outer_kernel, subs),
        out_shape=shape((64 * ROWS, CH), jnp.int16),
        in_specs=[VMEM] * 9 + [HBM],
        out_specs=VMEM,
        scratch_shapes=[
            pltpu.VMEM((K, units * RIM), bf16),
            pltpu.VMEM((HALF, units * RIM), bf16),
            pltpu.VMEM((TAPS, HALF, CH), f32),
            pltpu.VMEM((4, GROUP * ROWS, CH), f32),
            pltpu.VMEM((8, CH), jnp.int32),
            pltpu.VMEM((units * CH // 2, 2 * CH), bf16),
            pltpu.VMEM((TAPS, HALF, CH), f32),
            pltpu.SemaphoreType.DMA((2,)),
        ],
        compiler_params=pltpu.CompilerParams(vmem_limit_bytes=28 * 2**20),
        name="outer",
    )(
        tiles,
        tiles_other,
        halo_index,
        halo_other,
        matrix,
        energy,
        mask_row,
        rim,
        first,
        inner,
    )

    groups = [[f * samples + s for f in range(c, faces, 2) for s in range(samples)] for c in range(2)]
    landed = lax.all_to_all(message.reshape(64, -1, 2, CH), AXES, 0, 0, axis_index_groups=groups).reshape(-1, CH)
    count = 2 * subs * PIX * faces * samples
    return pl.pallas_call(
        functools.partial(rows_kernel, count),
        out_shape=shape((9, K + weight.shape[1]), f32),
        in_specs=[VMEM] * 3,
        out_specs=VMEM,
        scratch_shapes=[pltpu.VMEM((16, K), f32), pltpu.VMEM((48, K), bf16), pltpu.VMEM((4, 2 * GROUP * ROWS, CH), f32)],
        compiler_params=pltpu.CompilerParams(vmem_limit_bytes=8 * 2**20),
        name="rows",
    )(landed, weight, mask_row)


def solution(mesh):
    placed = (P("sample", "face", None, None), P("sample"), P("face", None), P(), P())
    return jax.shard_map(
        per_device,
        mesh=mesh,
        in_specs=placed,
        out_specs=P(("face", "sample"), None),
        check_vma=False,
    )
```

```python
import functools

import jax
import jax.numpy as jnp
import ml_dtypes
import numpy as np
from jax import lax
from jax.experimental import pallas as pl
from jax.experimental.pallas import tpu as pltpu
from jax.sharding import PartitionSpec as P

SIDE = 16
PIX = SIDE * SIDE
CH = 128
TAPS = 9
K = TAPS * CH
HALF = K // 2
CYCLE = 4 * SIDE + 4
RIM = 64
INNER = PIX - RIM
ROWS = 82
STEPS = 16
TOP = 32700.0
THIRD = 43
GROUP = 4
AXES = ("face", "sample")
NT = (((1,), (1,)), ((), ()))
SIDE_AT = (1, 19, 36, 52)
CORNER_AT = (0, 17, 18, 35)


def rim_sources(tap):
    lane = lax.broadcasted_iota(jnp.int32, (8, CH), 1)
    second = lane >= RIM
    place = lax.rem(lane, RIM)
    along = lax.rem(place, SIDE)
    side = place // SIDE
    y = jnp.where(side == 0, 0, jnp.where(side == 1, SIDE - 1, along))
    x = jnp.where(side == 2, 0, jnp.where(side == 3, SIDE - 1, along))
    corner = (side >= 2) & ((along == 0) | (along == SIDE - 1))
    y = jnp.where(corner, jnp.clip(along, 1, SIDE - 2), y)
    x = jnp.where(corner, jnp.where(side == 2, 1, SIDE - 2), x)
    u, v = y + tap // 3 - 1, x + tap % 3 - 1
    inside = (u >= 0) & (u < SIDE) & (v >= 0) & (v < SIDE)
    entry = jnp.where(v < 0, 2 * SIDE + 4 + u, 3 * SIDE + 4 + u)
    entry = jnp.where(u < 0, v + 1, jnp.where(u >= SIDE, SIDE + 3 + v, entry))
    pixel = jnp.where(inside, u * SIDE + v + jnp.where(second, PIX, 0), -1)
    cycle = jnp.where(inside, -1, entry + jnp.where(second, CH, 0))
    return pixel[0:1, :], cycle[0:1, :]


def inner_pixels(place):
    rest = place - 2 * (SIDE - 4)
    row = lax.shift_right_logical(jnp.maximum(rest, 0) * 147, 11)
    y = jnp.where(place < SIDE - 4, 1, jnp.where(rest < 0, SIDE - 2, row + 2))
    x = jnp.where(place < SIDE - 4, place + 2, jnp.where(rest < 0, place - SIDE + 6, rest - row * (SIDE - 2) + 1))
    return jnp.where((place >= 0) & (place < INNER), y * SIDE + x, -PIX)


def one_hot(rows, source):
    at = lax.broadcasted_iota(jnp.int32, (rows, CH), 0)
    return jnp.where(at == source, 1.0, 0.0).astype(jnp.bfloat16)


def edges_kernel(index_ref, fields_ref, copies_ref):
    subs = fields_ref.shape[1]
    row = lax.broadcasted_iota(jnp.int32, (4 * SIDE, PIX), 0)
    pixel = lax.broadcasted_iota(jnp.int32, (4 * SIDE, PIX), 1)
    along = row & (SIDE - 1)
    wanted = jnp.where(row < SIDE, along, (SIDE - 1) * SIDE + along)
    wanted = jnp.where(row >= 2 * SIDE, along * SIDE, wanted)
    wanted = jnp.where(row >= 3 * SIDE, along * SIDE + SIDE - 1, wanted)
    pick = jnp.where(pixel == wanted, 1.0, 0.0).astype(jnp.bfloat16)
    for s in range(2):
        for f in range(subs):
            x = fields_ref[index_ref[s], f]
            u = s * subs + f
            edges = lax.dot_general(pick, x, NT, preferred_element_type=jnp.float32)
            edges = edges.astype(jnp.bfloat16)
            for d in range(copies_ref.shape[0]):
                copies_ref[d, u * 4 * SIDE : (u + 1) * 4 * SIDE, :] = edges


def owned_rows(core, patches, owned):
    for c in range(2):

        @pl.when(core == c)
        def _():
            for g in range(K // 144):
                owned[g * 72 : (g + 1) * 72, :] = patches[g * 144 + c * 72 : g * 144 + c * 72 + 72, :]


def tap_blocks():
    return [slice(0, 4), slice(4, 8), slice(8, TAPS)]


def core_index():
    return lax.axis_index("face") & 1


def inner_kernel(
    index_ref,
    own_ref,
    other_ref,
    gram_ref,
    pairs_ref,
    patches,
    owned,
    gram,
    sems,
):
    subs = own_ref.shape[1]
    core = core_index()

    index = index_ref[...]
    for s in range(2):
        rows = slice(s * subs * CH, (s + 1) * subs * CH)
        chosen = [(index[:, s : s + 1] == n).astype(jnp.float32).astype(jnp.bfloat16) for n in range(own_ref.shape[0])]
        for n, ref in enumerate((own_ref, other_ref)):
            parts = [ref[k].reshape(subs * CH, PIX) * one for k, one in enumerate(chosen)]
            pairs_ref[rows, n * PIX : (n + 1) * PIX] = sum(parts[1:], parts[0])

    row_at = lax.broadcasted_iota(jnp.int32, (PIX, PIX), 0)
    place = lax.broadcasted_iota(jnp.int32, (8, PIX), 1)
    ahead = [row_at - inner_pixels(place + d)[0:1, :] for d in (0, INNER - PIX)]
    for t in range(TAPS):
        shift = (t // 3 - 1) * SIDE + t % 3 - 1
        taps = [jnp.where(d == shift, 1.0, 0.0).astype(jnp.bfloat16) for d in ahead]
        for s in range(2):
            first, second = (
                jnp.dot(
                    pairs_ref[s * subs * CH : (s + 1) * subs * CH, n * PIX : (n + 1) * PIX],
                    tap,
                    preferred_element_type=jnp.float32,
                )
                for n, tap in enumerate(taps)
            )
            columns = (first[:, :CH], first[:, CH:] + second[:, :CH], second[:, CH:])
            for n, values in enumerate(columns):
                values = values.astype(jnp.bfloat16)
                for f in range(subs):
                    at = (s * subs + f) * 2 * INNER + n * CH
                    patches[t * CH : (t + 1) * CH, at : at + CH] = values[f * CH : (f + 1) * CH, :]
    owned_rows(core, patches, owned)
    copies = []
    for n, taps in enumerate(tap_blocks()):
        right = patches[taps.start * CH : taps.stop * CH, :]
        block = lax.dot_general(owned[...], right, NT, preferred_element_type=jnp.float32)
        for l in range(taps.stop - taps.start):
            gram[taps.start + l, :, :] = block[:, l * CH : (l + 1) * CH]
        copies.append(pltpu.make_async_copy(gram.at[taps], gram_ref.at[taps], sems.at[n]))
        copies[-1].start()
    for copy in copies:
        copy.wait()


def gather_kernel(subs, halo_own_ref, halo_other_ref, table_ref, after_ref, tiles_ref):
    core = core_index()
    zero = jnp.zeros((SIDE, CH), jnp.bfloat16)
    for side, halo_ref in enumerate((halo_own_ref, halo_other_ref)):
        for f in range(subs):
            for n, at in enumerate(SIDE_AT + CORNER_AT):
                index = halo_ref[f, at]
                sub = lax.shift_right_logical(index, 6)
                device = lax.shift_right_logical(sub * THIRD, 7)
                row = (lax.shift_right_logical(device, 1) * 2 * subs + sub - device * subs) * 4 * SIDE
                row = pl.multiple_of(row + (index & (3 * SIDE)), SIDE)
                for s in range(2):
                    u = (side * 2 + s) * subs + f
                    tile = table_ref[pl.ds(pl.multiple_of(row + s * subs * 4 * SIDE, SIDE), SIDE), :]
                    tiles_ref[u * CH + n * SIDE : u * CH + (n + 1) * SIDE, :] = jnp.where((device & 1) == core, tile, zero)


def rim_kernel(subs, pairs_ref, after_ref, inner_ref, rim_ref, matrix_ref, energy_ref, gram_ref, pixels, sem):
    copy = pltpu.make_async_copy(inner_ref.at[tap_blocks()[0]], gram_ref, sem)
    copy.start()
    for t in range(TAPS):
        pixel, cycle = rim_sources(t)
        pixels[:, t * CH : (t + 1) * CH] = one_hot(2 * PIX, pixel)
        matrix_ref[:, t * CH : (t + 1) * CH] = one_hot(2 * CH, cycle)
    energy = jnp.zeros((CH, CH), jnp.float32)
    for p in range(2 * subs):
        x = pairs_ref[p * CH : (p + 1) * CH, :].astype(jnp.float32)
        for n in range(4):
            energy += x[:, n * CH : (n + 1) * CH] * x[:, n * CH : (n + 1) * CH]
    energy_ref[...] = energy
    values = jnp.dot(pairs_ref[...], pixels[...], preferred_element_type=jnp.float32).astype(jnp.bfloat16)
    for p in range(2 * subs):
        for t in range(TAPS):
            part = values[p * CH : (p + 1) * CH, t * CH : (t + 1) * CH]
            rim_ref[t * CH : (t + 1) * CH, p * CH : (p + 1) * CH] = part
    copy.wait()


def outer_kernel(
    subs,
    tiles_own_ref,
    tiles_other_ref,
    halo_rows_own_ref,
    halo_rows_other_ref,
    matrix_ref,
    energy_ref,
    mask_ref,
    rim_ref,
    first_ref,
    inner_ref,
    message_ref,
    patches,
    owned,
    gram,
    stage,
    position,
    cycles,
    inner,
    sems,
):
    core = core_index()
    units = 4 * subs
    half = units // 2
    copies = []
    for n, taps in enumerate(tap_blocks()[1:]):
        copies.append(pltpu.make_async_copy(inner_ref.at[taps], inner.at[taps], sems.at[n]))
        copies[-1].start()

    lane = lax.broadcasted_iota(jnp.int32, (8, CH), 1)
    base = jnp.full((8, CH), -1000, jnp.int32)
    for e, at in enumerate(SIDE_AT):
        base = jnp.where((lane >= at) & (lane < at + SIDE), e * SIDE, base)
    for e, at in enumerate(CORNER_AT):
        base = jnp.where(lane == at, (4 + e) * SIDE, base)
    position[...] = jnp.zeros((8, CH), jnp.int32)
    position[0:subs, 0:CYCLE] = lax.rem(halo_rows_own_ref[...], SIDE)
    position[subs : 2 * subs, 0:CYCLE] = lax.rem(halo_rows_other_ref[...], SIDE)
    source = position[...] + base

    row_at = lax.broadcasted_iota(jnp.int32, (CH, CH), 0)
    col_at = lax.broadcasted_iota(jnp.int32, (CH, CH), 1)
    diagonal = row_at == col_at
    eye = jnp.where(diagonal, 1.0, 0.0).astype(jnp.bfloat16)
    split = units * CH // 2
    energy = energy_ref[...]
    for side, (mine, theirs) in enumerate(((0, split), (split, 0))):
        tiles = tiles_own_ref[mine : mine + split, :] + tiles_other_ref[theirs : theirs + split, :]
        tiles = lax.dot_general(eye, tiles, NT, preferred_element_type=jnp.float32).astype(jnp.bfloat16)
        for p in range(half):
            at = side * subs + p % subs
            pick = jnp.where(row_at == source[at : at + 1, :], 1.0, 0.0).astype(jnp.bfloat16)
            cycle = jnp.dot(tiles[:, p * CH : (p + 1) * CH], pick, preferred_element_type=jnp.float32)
            energy += cycle * cycle
            cycles[p * CH : (p + 1) * CH, side * CH : (side + 1) * CH] = cycle.astype(jnp.bfloat16)

    values = jnp.dot(cycles[...], matrix_ref[...], preferred_element_type=jnp.float32).astype(jnp.bfloat16)
    for p in range(half):
        for t in range(TAPS):
            part = values[p * CH : (p + 1) * CH, t * CH : (t + 1) * CH]
            place = (slice(t * CH, (t + 1) * CH), slice(p * CH, (p + 1) * CH))
            patches[place] = rim_ref[place] + part

    kept = mask_ref[...].astype(jnp.float32)
    kept_row = jnp.sum(jnp.where(diagonal, kept, 0.0), axis=1, keepdims=True)
    energy = jnp.sum(energy, axis=1, keepdims=True)

    def exponent(values):
        top = jnp.full((8, CH), jnp.maximum(jnp.max(values), 2.0**-120), jnp.float32)
        return jnp.ceil(jnp.log2(top) * (STEPS / 2) + 0.1)

    kept_exp = exponent(jnp.where(kept_row > 0, energy, 0.0))
    any_exp = exponent(energy)
    lane_exps = jnp.where(kept > 0, kept_exp, any_exp) + kept_exp
    scale = jnp.exp2(lane_exps * (-1 / STEPS)) * TOP**2

    def coded(values):
        return jnp.round(values * lax.rsqrt(jnp.maximum(jnp.abs(values), 1e-30)))

    owned_rows(core, patches, owned)

    def add_block(n, at):
        taps = tap_blocks()[n]
        right = patches[taps.start * CH : taps.stop * CH, :]
        block = lax.dot_general(owned[at, :], right, NT, preferred_element_type=jnp.float32)
        if n > 0 and at.start == 0:
            copies[n - 1].wait()
        for l in range(taps.stop - taps.start):
            part = block[:, l * CH : (l + 1) * CH] + (inner if n > 0 else first_ref)[taps.start + l, at, :]
            gram[taps.start + l, at, :] = coded(part * scale[0:1, :])

    add_block(0, slice(0, HALF))
    for m in range(0, HALF, HALF // 2):
        add_block(1, slice(m, m + HALF // 2))
        add_block(2, slice(m, m + HALF // 2))

        for j in range(m // 9, (m + HALF // 2) // 9, GROUP):
            block = stage.at[j // GROUP % 4]
            for i in range(GROUP):
                for l in range(TAPS):
                    to = i * ROWS + l * 9
                    block[to : to + 9, :] = gram[l, (j + i) * 9 : (j + i + 1) * 9, :]
                block[i * ROWS + 81 : (i + 1) * ROWS, :] = lane_exps[0:1, :]
            message_ref[j * ROWS : (j + GROUP) * ROWS, :] = block[...].astype(jnp.int32).astype(jnp.int16)


def rows_kernel(count, landed_ref, weight_ref, kept_ref, out_ref, rows, split, stage):
    owner = lax.axis_index("face") * lax.axis_size("sample") + lax.axis_index("sample")
    total = jnp.zeros((ROWS, CH), jnp.float32)
    for j in range(0, landed_ref.shape[0] // ROWS, 2 * GROUP):
        block = stage.at[j // (2 * GROUP) % 4]
        block[...] = landed_ref[j * ROWS : (j + 2 * GROUP) * ROWS, :].astype(jnp.int32).astype(jnp.float32)
        for i in range(2 * GROUP):
            codes = block[i * ROWS : (i + 1) * ROWS, :]
            total += codes * jnp.abs(codes) * jnp.exp2(block[i * ROWS + 81 : (i + 1) * ROWS, :] * (1 / STEPS))
    total = total * TOP**-2
    rows[...] = jnp.zeros_like(rows)
    for l in range(TAPS):
        rows[0:9, l * CH : (l + 1) * CH] = total[l * 9 : (l + 1) * 9, :]

    channel = lax.rem(owner * 9 + lax.broadcasted_iota(jnp.int32, (16, CH), 0), CH)
    own = lax.broadcasted_iota(jnp.int32, (16, CH), 1) == channel
    keep = jnp.sum(jnp.where(own, kept_ref[...].astype(jnp.float32), 0.0), axis=1, keepdims=True)
    whole = rows[...]
    head = whole.astype(jnp.bfloat16)
    left = whole - head.astype(jnp.float32)
    tail = left.astype(jnp.bfloat16)
    split[0:16, :] = head
    split[16:32, :] = tail
    split[32:48, :] = (left - tail.astype(jnp.float32)).astype(jnp.bfloat16)
    product = jnp.dot(split[...], weight_ref[...], preferred_element_type=jnp.float32)
    product = product[32:48, :] + product[16:32, :] + product[0:16, :]
    kept = kept_ref[...] > 0
    for t in range(TAPS):
        part = whole[:, t * CH : (t + 1) * CH]
        part = jnp.where((keep > 0) & kept, part / count, 0.0)
        out_ref[:, t * CH : (t + 1) * CH] = part[0:9, :]
    for n in range(2):
        part = product[:, n * CH : (n + 1) * CH]
        part = jnp.where(keep > 0, part / count, 0.0)
        out_ref[:, K + n * CH : K + (n + 1) * CH] = part[0:9, :]


VMEM = pl.BlockSpec(memory_space=pltpu.VMEM)
SMEM = pl.BlockSpec(memory_space=pltpu.SMEM)
HBM = pl.BlockSpec(memory_space=pltpu.HBM)
ANY = pl.BlockSpec(memory_space=pl.ANY)


def shape(dims, kind):
    return jax.ShapeDtypeStruct(dims, kind)


def per_device(fields, sample_index, halo_index, channel_mask, weight):
    faces, samples = lax.axis_size("face"), lax.axis_size("sample")
    subs = fields.shape[1]
    units = 4 * subs
    swap = [(f, f ^ 1) for f in range(faces)]
    bf16, f32 = jnp.bfloat16, jnp.float32

    other = lax.ppermute(fields, "face", swap)
    halo_other = lax.ppermute(halo_index, "face", swap)
    copies = pl.pallas_call(
        edges_kernel,
        out_shape=shape((faces // 2, 8 * subs * SIDE, CH), bf16),
        in_specs=[SMEM, VMEM],
        out_specs=VMEM,
        compiler_params=pltpu.CompilerParams(vmem_limit_bytes=8 * 2**20),
        name="edges",
    )(*(pltpu.with_memory_space_constraint(a, pltpu.HBM) for a in (sample_index, fields)))

    same_core = [[f for f in range(c, faces, 2)] for c in range(2)]
    table = lax.all_to_all(copies, "face", 0, 0, axis_index_groups=same_core)

    mask_row = channel_mask[None]
    inner, pairs = pl.pallas_call(
        inner_kernel,
        out_shape=(
            pltpu.HBM((TAPS, HALF, CH), f32),
            shape((units * CH // 2, 2 * PIX), bf16),
        ),
        in_specs=[VMEM] * 3,
        out_specs=(HBM, VMEM),
        scratch_shapes=[
            pltpu.VMEM((K, units * INNER), bf16),
            pltpu.VMEM((HALF, units * INNER), bf16),
            pltpu.VMEM((TAPS, HALF, CH), f32),
            pltpu.SemaphoreType.DMA((3,)),
        ],
        compiler_params=pltpu.CompilerParams(vmem_limit_bytes=32 * 2**20),
        cost_estimate=pl.CostEstimate(flops=6 * 10**9, bytes_accessed=5 * 10**6, transcendentals=0),
        name="inner",
    )(sample_index[None], fields, other)

    tiles = pl.pallas_call(
        functools.partial(gather_kernel, subs),
        out_shape=shape((units * CH, CH), bf16),
        in_specs=[SMEM, SMEM, VMEM, ANY],
        out_specs=VMEM,
        compiler_params=pltpu.CompilerParams(vmem_limit_bytes=4 * 2**20),
        name="gather",
    )(halo_index, halo_other, table.reshape(-1, CH), pairs)
    tiles_other = lax.ppermute(tiles, "face", swap)

    inner = pltpu.with_memory_space_constraint(inner, pltpu.HBM)
    rim, matrix, energy, first = pl.pallas_call(
        functools.partial(rim_kernel, subs),
        out_shape=(
            shape((K, units * RIM), bf16),
            shape((2 * CH, K), bf16),
            shape((CH, CH), f32),
            shape((tap_blocks()[0].stop, HALF, CH), f32),
        ),
        in_specs=[VMEM, ANY, HBM],
        out_specs=(VMEM, VMEM, VMEM, VMEM),
        scratch_shapes=[pltpu.VMEM((2 * PIX, K), bf16), pltpu.SemaphoreType.DMA],
        compiler_params=pltpu.CompilerParams(vmem_limit_bytes=16 * 2**20),
        cost_estimate=pl.CostEstimate(flops=10**9, bytes_accessed=6 * 10**6, transcendentals=0),
        name="rim",
    )(pairs, tiles, inner)

    message = pl.pallas_call(
        functools.partial(outer_kernel, subs),
        out_shape=shape((64 * ROWS, CH), jnp.int16),
        in_specs=[VMEM] * 9 + [HBM],
        out_specs=VMEM,
        scratch_shapes=[
            pltpu.VMEM((K, units * RIM), bf16),
            pltpu.VMEM((HALF, units * RIM), bf16),
            pltpu.VMEM((TAPS, HALF, CH), f32),
            pltpu.VMEM((4, GROUP * ROWS, CH), f32),
            pltpu.VMEM((8, CH), jnp.int32),
            pltpu.VMEM((units * CH // 2, 2 * CH), bf16),
            pltpu.VMEM((TAPS, HALF, CH), f32),
            pltpu.SemaphoreType.DMA((2,)),
        ],
        compiler_params=pltpu.CompilerParams(vmem_limit_bytes=28 * 2**20),
        name="outer",
    )(
        tiles,
        tiles_other,
        halo_index,
        halo_other,
        matrix,
        energy,
        mask_row,
        rim,
        first,
        inner,
    )

    groups = [[f * samples + s for f in range(c, faces, 2) for s in range(samples)] for c in range(2)]
    landed = lax.all_to_all(message.reshape(64, -1, 2, CH), AXES, 0, 0, axis_index_groups=groups).reshape(-1, CH)
    count = 2 * subs * PIX * faces * samples
    return pl.pallas_call(
        functools.partial(rows_kernel, count),
        out_shape=shape((9, K + weight.shape[1]), f32),
        in_specs=[VMEM] * 3,
        out_specs=VMEM,
        scratch_shapes=[pltpu.VMEM((16, K), f32), pltpu.VMEM((48, K), bf16), pltpu.VMEM((4, 2 * GROUP * ROWS, CH), f32)],
        compiler_params=pltpu.CompilerParams(vmem_limit_bytes=8 * 2**20),
        name="rows",
    )(landed, weight, mask_row)


def solution(mesh):
    placed = (P("sample", "face", None, None), P("sample"), P("face", None), P(), P())
    return jax.shard_map(
        per_device,
        mesh=mesh,
        in_specs=placed,
        out_specs=P(("face", "sample"), None),
        check_vma=False,
    )
```

```python
import functools

import jax
import jax.numpy as jnp
import ml_dtypes
import numpy as np
from jax import lax
from jax.experimental import pallas as pl
from jax.experimental.pallas import tpu as pltpu
from jax.sharding import PartitionSpec as P

SIDE = 16
PIX = SIDE * SIDE
CH = 128
TAPS = 9
K = TAPS * CH
HALF = K // 2
CYCLE = 4 * SIDE + 4
RIM = 64
INNER = PIX - RIM
ROWS = 82
STEPS = 16
TOP = 32700.0
THIRD = 43
GROUP = 4
AXES = ("face", "sample")
NT = (((1,), (1,)), ((), ()))
SIDE_AT = (1, 19, 36, 52)
CORNER_AT = (0, 17, 18, 35)


def rim_sources(tap):
    lane = lax.broadcasted_iota(jnp.int32, (8, CH), 1)
    second = lane >= RIM
    place = lax.rem(lane, RIM)
    along = lax.rem(place, SIDE)
    side = place // SIDE
    y = jnp.where(side == 0, 0, jnp.where(side == 1, SIDE - 1, along))
    x = jnp.where(side == 2, 0, jnp.where(side == 3, SIDE - 1, along))
    corner = (side >= 2) & ((along == 0) | (along == SIDE - 1))
    y = jnp.where(corner, jnp.clip(along, 1, SIDE - 2), y)
    x = jnp.where(corner, jnp.where(side == 2, 1, SIDE - 2), x)
    u, v = y + tap // 3 - 1, x + tap % 3 - 1
    inside = (u >= 0) & (u < SIDE) & (v >= 0) & (v < SIDE)
    entry = jnp.where(v < 0, 2 * SIDE + 4 + u, 3 * SIDE + 4 + u)
    entry = jnp.where(u < 0, v + 1, jnp.where(u >= SIDE, SIDE + 3 + v, entry))
    pixel = jnp.where(inside, u * SIDE + v + jnp.where(second, PIX, 0), -1)
    cycle = jnp.where(inside, -1, entry + jnp.where(second, CH, 0))
    return pixel[0:1, :], cycle[0:1, :]


def inner_pixels(place):
    rest = place - 2 * (SIDE - 4)
    row = lax.shift_right_logical(jnp.maximum(rest, 0) * 147, 11)
    y = jnp.where(place < SIDE - 4, 1, jnp.where(rest < 0, SIDE - 2, row + 2))
    x = jnp.where(place < SIDE - 4, place + 2, jnp.where(rest < 0, place - SIDE + 6, rest - row * (SIDE - 2) + 1))
    return jnp.where((place >= 0) & (place < INNER), y * SIDE + x, -PIX)


def one_hot(rows, source):
    at = lax.broadcasted_iota(jnp.int32, (rows, CH), 0)
    return jnp.where(at == source, 1.0, 0.0).astype(jnp.bfloat16)


def edges_kernel(index_ref, fields_ref, copies_ref):
    subs = fields_ref.shape[1]
    row = lax.broadcasted_iota(jnp.int32, (4 * SIDE, PIX), 0)
    pixel = lax.broadcasted_iota(jnp.int32, (4 * SIDE, PIX), 1)
    along = row & (SIDE - 1)
    wanted = jnp.where(row < SIDE, along, (SIDE - 1) * SIDE + along)
    wanted = jnp.where(row >= 2 * SIDE, along * SIDE, wanted)
    wanted = jnp.where(row >= 3 * SIDE, along * SIDE + SIDE - 1, wanted)
    pick = jnp.where(pixel == wanted, 1.0, 0.0).astype(jnp.bfloat16)
    for s in range(2):
        for f in range(subs):
            x = fields_ref[index_ref[s], f]
            u = s * subs + f
            edges = lax.dot_general(pick, x, NT, preferred_element_type=jnp.float32)
            edges = edges.astype(jnp.bfloat16)
            for d in range(copies_ref.shape[0]):
                copies_ref[d, u * 4 * SIDE : (u + 1) * 4 * SIDE, :] = edges


def owned_rows(core, patches, owned):
    for c in range(2):

        @pl.when(core == c)
        def _():
            for g in range(K // 144):
                owned[g * 72 : (g + 1) * 72, :] = patches[g * 144 + c * 72 : g * 144 + c * 72 + 72, :]


def tap_blocks():
    return [slice(0, 4), slice(4, 5), slice(5, TAPS)]


def core_index():
    return lax.axis_index("face") & 1


def inner_kernel(
    index_ref,
    own_ref,
    other_ref,
    gram_ref,
    pairs_ref,
    patches,
    owned,
    gram,
    sems,
):
    subs = own_ref.shape[1]
    core = core_index()

    index = index_ref[...]
    for s in range(2):
        rows = slice(s * subs * CH, (s + 1) * subs * CH)
        chosen = [(index[:, s : s + 1] == n).astype(jnp.float32).astype(jnp.bfloat16) for n in range(own_ref.shape[0])]
        for n, ref in enumerate((own_ref, other_ref)):
            parts = [ref[k].reshape(subs * CH, PIX) * one for k, one in enumerate(chosen)]
            pairs_ref[rows, n * PIX : (n + 1) * PIX] = sum(parts[1:], parts[0])

    row_at = lax.broadcasted_iota(jnp.int32, (PIX, PIX), 0)
    place = lax.broadcasted_iota(jnp.int32, (8, PIX), 1)
    ahead = [row_at - inner_pixels(place + d)[0:1, :] for d in (0, INNER - PIX)]
    for t in range(TAPS):
        shift = (t // 3 - 1) * SIDE + t % 3 - 1
        taps = [jnp.where(d == shift, 1.0, 0.0).astype(jnp.bfloat16) for d in ahead]
        for s in range(2):
            first, second = (
                jnp.dot(
                    pairs_ref[s * subs * CH : (s + 1) * subs * CH, n * PIX : (n + 1) * PIX],
                    tap,
                    preferred_element_type=jnp.float32,
                )
                for n, tap in enumerate(taps)
            )
            columns = (first[:, :CH], first[:, CH:] + second[:, :CH], second[:, CH:])
            for n, values in enumerate(columns):
                values = values.astype(jnp.bfloat16)
                for f in range(subs):
                    at = (s * subs + f) * 2 * INNER + n * CH
                    patches[t * CH : (t + 1) * CH, at : at + CH] = values[f * CH : (f + 1) * CH, :]
    owned_rows(core, patches, owned)
    copies = []
    for n, taps in enumerate(tap_blocks()):
        right = patches[taps.start * CH : taps.stop * CH, :]
        block = lax.dot_general(owned[...], right, NT, preferred_element_type=jnp.float32)
        for l in range(taps.stop - taps.start):
            gram[taps.start + l, :, :] = block[:, l * CH : (l + 1) * CH]
        copies.append(pltpu.make_async_copy(gram.at[taps], gram_ref.at[taps], sems.at[n]))
        copies[-1].start()
    for copy in copies:
        copy.wait()


def gather_kernel(subs, halo_own_ref, halo_other_ref, table_ref, after_ref, tiles_ref):
    core = core_index()
    zero = jnp.zeros((SIDE, CH), jnp.bfloat16)
    for side, halo_ref in enumerate((halo_own_ref, halo_other_ref)):
        for f in range(subs):
            for n, at in enumerate(SIDE_AT + CORNER_AT):
                index = halo_ref[f, at]
                sub = lax.shift_right_logical(index, 6)
                device = lax.shift_right_logical(sub * THIRD, 7)
                row = (lax.shift_right_logical(device, 1) * 2 * subs + sub - device * subs) * 4 * SIDE
                row = pl.multiple_of(row + (index & (3 * SIDE)), SIDE)
                for s in range(2):
                    u = (side * 2 + s) * subs + f
                    tile = table_ref[pl.ds(pl.multiple_of(row + s * subs * 4 * SIDE, SIDE), SIDE), :]
                    tiles_ref[u * CH + n * SIDE : u * CH + (n + 1) * SIDE, :] = jnp.where((device & 1) == core, tile, zero)


def rim_kernel(subs, pairs_ref, after_ref, inner_ref, rim_ref, matrix_ref, energy_ref, gram_ref, pixels, sem):
    copy = pltpu.make_async_copy(inner_ref.at[tap_blocks()[0]], gram_ref, sem)
    copy.start()
    for t in range(TAPS):
        pixel, cycle = rim_sources(t)
        pixels[:, t * CH : (t + 1) * CH] = one_hot(2 * PIX, pixel)
        matrix_ref[:, t * CH : (t + 1) * CH] = one_hot(2 * CH, cycle)
    energy = jnp.zeros((CH, CH), jnp.float32)
    for p in range(2 * subs):
        x = pairs_ref[p * CH : (p + 1) * CH, :].astype(jnp.float32)
        for n in range(4):
            energy += x[:, n * CH : (n + 1) * CH] * x[:, n * CH : (n + 1) * CH]
    energy_ref[...] = energy
    values = jnp.dot(pairs_ref[...], pixels[...], preferred_element_type=jnp.float32).astype(jnp.bfloat16)
    for p in range(2 * subs):
        for t in range(TAPS):
            part = values[p * CH : (p + 1) * CH, t * CH : (t + 1) * CH]
            rim_ref[t * CH : (t + 1) * CH, p * CH : (p + 1) * CH] = part
    copy.wait()


def outer_kernel(
    subs,
    tiles_own_ref,
    tiles_other_ref,
    halo_rows_own_ref,
    halo_rows_other_ref,
    matrix_ref,
    energy_ref,
    mask_ref,
    rim_ref,
    first_ref,
    inner_ref,
    message_ref,
    patches,
    owned,
    gram,
    stage,
    position,
    cycles,
    inner,
    sems,
):
    core = core_index()
    units = 4 * subs
    half = units // 2
    copies = []
    for n, taps in enumerate(tap_blocks()[1:]):
        copies.append(pltpu.make_async_copy(inner_ref.at[taps], inner.at[taps], sems.at[n]))
        copies[-1].start()

    lane = lax.broadcasted_iota(jnp.int32, (8, CH), 1)
    base = jnp.full((8, CH), -1000, jnp.int32)
    for e, at in enumerate(SIDE_AT):
        base = jnp.where((lane >= at) & (lane < at + SIDE), e * SIDE, base)
    for e, at in enumerate(CORNER_AT):
        base = jnp.where(lane == at, (4 + e) * SIDE, base)
    position[...] = jnp.zeros((8, CH), jnp.int32)
    position[0:subs, 0:CYCLE] = lax.rem(halo_rows_own_ref[...], SIDE)
    position[subs : 2 * subs, 0:CYCLE] = lax.rem(halo_rows_other_ref[...], SIDE)
    source = position[...] + base

    row_at = lax.broadcasted_iota(jnp.int32, (CH, CH), 0)
    col_at = lax.broadcasted_iota(jnp.int32, (CH, CH), 1)
    diagonal = row_at == col_at
    eye = jnp.where(diagonal, 1.0, 0.0).astype(jnp.bfloat16)
    split = units * CH // 2
    energy = energy_ref[...]
    for side, (mine, theirs) in enumerate(((0, split), (split, 0))):
        tiles = tiles_own_ref[mine : mine + split, :] + tiles_other_ref[theirs : theirs + split, :]
        tiles = lax.dot_general(eye, tiles, NT, preferred_element_type=jnp.float32).astype(jnp.bfloat16)
        for p in range(half):
            at = side * subs + p % subs
            pick = jnp.where(row_at == source[at : at + 1, :], 1.0, 0.0).astype(jnp.bfloat16)
            cycle = jnp.dot(tiles[:, p * CH : (p + 1) * CH], pick, preferred_element_type=jnp.float32)
            energy += cycle * cycle
            cycles[p * CH : (p + 1) * CH, side * CH : (side + 1) * CH] = cycle.astype(jnp.bfloat16)

    values = jnp.dot(cycles[...], matrix_ref[...], preferred_element_type=jnp.float32).astype(jnp.bfloat16)
    for p in range(half):
        for t in range(TAPS):
            part = values[p * CH : (p + 1) * CH, t * CH : (t + 1) * CH]
            place = (slice(t * CH, (t + 1) * CH), slice(p * CH, (p + 1) * CH))
            patches[place] = rim_ref[place] + part

    kept = mask_ref[...].astype(jnp.float32)
    kept_row = jnp.sum(jnp.where(diagonal, kept, 0.0), axis=1, keepdims=True)
    energy = jnp.sum(energy, axis=1, keepdims=True)

    def exponent(values):
        top = jnp.full((8, CH), jnp.maximum(jnp.max(values), 2.0**-120), jnp.float32)
        return jnp.ceil(jnp.log2(top) * (STEPS / 2) + 0.1)

    kept_exp = exponent(jnp.where(kept_row > 0, energy, 0.0))
    any_exp = exponent(energy)
    lane_exps = jnp.where(kept > 0, kept_exp, any_exp) + kept_exp
    scale = jnp.exp2(lane_exps * (-1 / STEPS)) * TOP**2

    def coded(values):
        return jnp.round(values * lax.rsqrt(jnp.maximum(jnp.abs(values), 1e-30)))

    owned_rows(core, patches, owned)

    def add_block(n, at):
        taps = tap_blocks()[n]
        right = patches[taps.start * CH : taps.stop * CH, :]
        block = lax.dot_general(owned[at, :], right, NT, preferred_element_type=jnp.float32)
        if n > 0 and at.start == 0:
            copies[n - 1].wait()
        for l in range(taps.stop - taps.start):
            part = block[:, l * CH : (l + 1) * CH] + (inner if n > 0 else first_ref)[taps.start + l, at, :]
            gram[taps.start + l, at, :] = coded(part * scale[0:1, :])

    add_block(0, slice(0, HALF))
    for m in range(0, HALF, HALF // 2):
        add_block(1, slice(m, m + HALF // 2))
        add_block(2, slice(m, m + HALF // 2))

        for j in range(m // 9, (m + HALF // 2) // 9, GROUP):
            block = stage.at[j // GROUP % 4]
            for i in range(GROUP):
                for l in range(TAPS):
                    to = i * ROWS + l * 9
                    block[to : to + 9, :] = gram[l, (j + i) * 9 : (j + i + 1) * 9, :]
                block[i * ROWS + 81 : (i + 1) * ROWS, :] = lane_exps[0:1, :]
            message_ref[j * ROWS : (j + GROUP) * ROWS, :] = block[...].astype(jnp.int32).astype(jnp.int16)


def rows_kernel(count, landed_ref, weight_ref, kept_ref, out_ref, rows, split, stage):
    owner = lax.axis_index("face") * lax.axis_size("sample") + lax.axis_index("sample")
    total = jnp.zeros((ROWS, CH), jnp.float32)
    for j in range(0, landed_ref.shape[0] // ROWS, 2 * GROUP):
        block = stage.at[j // (2 * GROUP) % 4]
        block[...] = landed_ref[j * ROWS : (j + 2 * GROUP) * ROWS, :].astype(jnp.int32).astype(jnp.float32)
        for i in range(2 * GROUP):
            codes = block[i * ROWS : (i + 1) * ROWS, :]
            total += codes * jnp.abs(codes) * jnp.exp2(block[i * ROWS + 81 : (i + 1) * ROWS, :] * (1 / STEPS))
    total = total * TOP**-2
    rows[...] = jnp.zeros_like(rows)
    for l in range(TAPS):
        rows[0:9, l * CH : (l + 1) * CH] = total[l * 9 : (l + 1) * 9, :]

    channel = lax.rem(owner * 9 + lax.broadcasted_iota(jnp.int32, (16, CH), 0), CH)
    own = lax.broadcasted_iota(jnp.int32, (16, CH), 1) == channel
    keep = jnp.sum(jnp.where(own, kept_ref[...].astype(jnp.float32), 0.0), axis=1, keepdims=True)
    whole = rows[...]
    head = whole.astype(jnp.bfloat16)
    left = whole - head.astype(jnp.float32)
    tail = left.astype(jnp.bfloat16)
    split[0:16, :] = head
    split[16:32, :] = tail
    split[32:48, :] = (left - tail.astype(jnp.float32)).astype(jnp.bfloat16)
    product = jnp.dot(split[...], weight_ref[...], preferred_element_type=jnp.float32)
    product = product[32:48, :] + product[16:32, :] + product[0:16, :]
    kept = kept_ref[...] > 0
    for t in range(TAPS):
        part = whole[:, t * CH : (t + 1) * CH]
        part = jnp.where((keep > 0) & kept, part / count, 0.0)
        out_ref[:, t * CH : (t + 1) * CH] = part[0:9, :]
    for n in range(2):
        part = product[:, n * CH : (n + 1) * CH]
        part = jnp.where(keep > 0, part / count, 0.0)
        out_ref[:, K + n * CH : K + (n + 1) * CH] = part[0:9, :]


VMEM = pl.BlockSpec(memory_space=pltpu.VMEM)
SMEM = pl.BlockSpec(memory_space=pltpu.SMEM)
HBM = pl.BlockSpec(memory_space=pltpu.HBM)
ANY = pl.BlockSpec(memory_space=pl.ANY)


def shape(dims, kind):
    return jax.ShapeDtypeStruct(dims, kind)


def per_device(fields, sample_index, halo_index, channel_mask, weight):
    faces, samples = lax.axis_size("face"), lax.axis_size("sample")
    subs = fields.shape[1]
    units = 4 * subs
    swap = [(f, f ^ 1) for f in range(faces)]
    bf16, f32 = jnp.bfloat16, jnp.float32

    other = lax.ppermute(fields, "face", swap)
    halo_other = lax.ppermute(halo_index, "face", swap)
    copies = pl.pallas_call(
        edges_kernel,
        out_shape=shape((faces // 2, 8 * subs * SIDE, CH), bf16),
        in_specs=[SMEM, VMEM],
        out_specs=VMEM,
        compiler_params=pltpu.CompilerParams(vmem_limit_bytes=8 * 2**20),
        name="edges",
    )(*(pltpu.with_memory_space_constraint(a, pltpu.HBM) for a in (sample_index, fields)))

    same_core = [[f for f in range(c, faces, 2)] for c in range(2)]
    table = lax.all_to_all(copies, "face", 0, 0, axis_index_groups=same_core)

    mask_row = channel_mask[None]
    inner, pairs = pl.pallas_call(
        inner_kernel,
        out_shape=(
            pltpu.HBM((TAPS, HALF, CH), f32),
            shape((units * CH // 2, 2 * PIX), bf16),
        ),
        in_specs=[VMEM] * 3,
        out_specs=(HBM, VMEM),
        scratch_shapes=[
            pltpu.VMEM((K, units * INNER), bf16),
            pltpu.VMEM((HALF, units * INNER), bf16),
            pltpu.VMEM((TAPS, HALF, CH), f32),
            pltpu.SemaphoreType.DMA((3,)),
        ],
        compiler_params=pltpu.CompilerParams(vmem_limit_bytes=32 * 2**20),
        cost_estimate=pl.CostEstimate(flops=6 * 10**9, bytes_accessed=5 * 10**6, transcendentals=0),
        name="inner",
    )(sample_index[None], fields, other)

    tiles = pl.pallas_call(
        functools.partial(gather_kernel, subs),
        out_shape=shape((units * CH, CH), bf16),
        in_specs=[SMEM, SMEM, VMEM, ANY],
        out_specs=VMEM,
        compiler_params=pltpu.CompilerParams(vmem_limit_bytes=4 * 2**20),
        name="gather",
    )(halo_index, halo_other, table.reshape(-1, CH), pairs)
    tiles_other = lax.ppermute(tiles, "face", swap)

    inner = pltpu.with_memory_space_constraint(inner, pltpu.HBM)
    rim, matrix, energy, first = pl.pallas_call(
        functools.partial(rim_kernel, subs),
        out_shape=(
            shape((K, units * RIM), bf16),
            shape((2 * CH, K), bf16),
            shape((CH, CH), f32),
            shape((tap_blocks()[0].stop, HALF, CH), f32),
        ),
        in_specs=[VMEM, ANY, HBM],
        out_specs=(VMEM, VMEM, VMEM, VMEM),
        scratch_shapes=[pltpu.VMEM((2 * PIX, K), bf16), pltpu.SemaphoreType.DMA],
        compiler_params=pltpu.CompilerParams(vmem_limit_bytes=16 * 2**20),
        cost_estimate=pl.CostEstimate(flops=10**9, bytes_accessed=6 * 10**6, transcendentals=0),
        name="rim",
    )(pairs, tiles, inner)

    message = pl.pallas_call(
        functools.partial(outer_kernel, subs),
        out_shape=shape((64 * ROWS, CH), jnp.int16),
        in_specs=[VMEM] * 9 + [HBM],
        out_specs=VMEM,
        scratch_shapes=[
            pltpu.VMEM((K, units * RIM), bf16),
            pltpu.VMEM((HALF, units * RIM), bf16),
            pltpu.VMEM((TAPS, HALF, CH), f32),
            pltpu.VMEM((4, GROUP * ROWS, CH), f32),
            pltpu.VMEM((8, CH), jnp.int32),
            pltpu.VMEM((units * CH // 2, 2 * CH), bf16),
            pltpu.VMEM((TAPS, HALF, CH), f32),
            pltpu.SemaphoreType.DMA((2,)),
        ],
        compiler_params=pltpu.CompilerParams(vmem_limit_bytes=28 * 2**20),
        name="outer",
    )(
        tiles,
        tiles_other,
        halo_index,
        halo_other,
        matrix,
        energy,
        mask_row,
        rim,
        first,
        inner,
    )

    groups = [[f * samples + s for f in range(c, faces, 2) for s in range(samples)] for c in range(2)]
    landed = lax.all_to_all(message.reshape(64, -1, 2, CH), AXES, 0, 0, axis_index_groups=groups).reshape(-1, CH)
    count = 2 * subs * PIX * faces * samples
    return pl.pallas_call(
        functools.partial(rows_kernel, count),
        out_shape=shape((9, K + weight.shape[1]), f32),
        in_specs=[VMEM] * 3,
        out_specs=VMEM,
        scratch_shapes=[pltpu.VMEM((16, K), f32), pltpu.VMEM((48, K), bf16), pltpu.VMEM((4, 2 * GROUP * ROWS, CH), f32)],
        compiler_params=pltpu.CompilerParams(vmem_limit_bytes=8 * 2**20),
        name="rows",
    )(landed, weight, mask_row)


def solution(mesh):
    placed = (P("sample", "face", None, None), P("sample"), P("face", None), P(), P())
    return jax.shard_map(
        per_device,
        mesh=mesh,
        in_specs=placed,
        out_specs=P(("face", "sample"), None),
        check_vma=False,
    )
```

```python
import functools

import jax
import jax.numpy as jnp
import ml_dtypes
import numpy as np
from jax import lax
from jax.experimental import pallas as pl
from jax.experimental.pallas import tpu as pltpu
from jax.sharding import PartitionSpec as P

SIDE = 16
PIX = SIDE * SIDE
CH = 128
TAPS = 9
K = TAPS * CH
HALF = K // 2
CYCLE = 4 * SIDE + 4
RIM = 64
INNER = PIX - RIM
ROWS = 82
STEPS = 16
TOP = 32700.0
THIRD = 43
GROUP = 8
AXES = ("face", "sample")
NT = (((1,), (1,)), ((), ()))
SIDE_AT = (1, 19, 36, 52)
CORNER_AT = (0, 17, 18, 35)


def rim_sources(tap):
    lane = lax.broadcasted_iota(jnp.int32, (8, CH), 1)
    second = lane >= RIM
    place = lax.rem(lane, RIM)
    along = lax.rem(place, SIDE)
    side = place // SIDE
    y = jnp.where(side == 0, 0, jnp.where(side == 1, SIDE - 1, along))
    x = jnp.where(side == 2, 0, jnp.where(side == 3, SIDE - 1, along))
    corner = (side >= 2) & ((along == 0) | (along == SIDE - 1))
    y = jnp.where(corner, jnp.clip(along, 1, SIDE - 2), y)
    x = jnp.where(corner, jnp.where(side == 2, 1, SIDE - 2), x)
    u, v = y + tap // 3 - 1, x + tap % 3 - 1
    inside = (u >= 0) & (u < SIDE) & (v >= 0) & (v < SIDE)
    entry = jnp.where(v < 0, 2 * SIDE + 4 + u, 3 * SIDE + 4 + u)
    entry = jnp.where(u < 0, v + 1, jnp.where(u >= SIDE, SIDE + 3 + v, entry))
    pixel = jnp.where(inside, u * SIDE + v + jnp.where(second, PIX, 0), -1)
    cycle = jnp.where(inside, -1, entry + jnp.where(second, CH, 0))
    return pixel[0:1, :], cycle[0:1, :]


def inner_pixels(place):
    rest = place - 2 * (SIDE - 4)
    row = lax.shift_right_logical(jnp.maximum(rest, 0) * 147, 11)
    y = jnp.where(place < SIDE - 4, 1, jnp.where(rest < 0, SIDE - 2, row + 2))
    x = jnp.where(place < SIDE - 4, place + 2, jnp.where(rest < 0, place - SIDE + 6, rest - row * (SIDE - 2) + 1))
    return jnp.where((place >= 0) & (place < INNER), y * SIDE + x, -PIX)


def one_hot(rows, source):
    at = lax.broadcasted_iota(jnp.int32, (rows, CH), 0)
    return jnp.where(at == source, 1.0, 0.0).astype(jnp.bfloat16)


def edges_kernel(index_ref, fields_ref, copies_ref):
    subs = fields_ref.shape[1]
    row = lax.broadcasted_iota(jnp.int32, (4 * SIDE, PIX), 0)
    pixel = lax.broadcasted_iota(jnp.int32, (4 * SIDE, PIX), 1)
    along = row & (SIDE - 1)
    wanted = jnp.where(row < SIDE, along, (SIDE - 1) * SIDE + along)
    wanted = jnp.where(row >= 2 * SIDE, along * SIDE, wanted)
    wanted = jnp.where(row >= 3 * SIDE, along * SIDE + SIDE - 1, wanted)
    pick = jnp.where(pixel == wanted, 1.0, 0.0).astype(jnp.bfloat16)
    for s in range(2):
        for f in range(subs):
            x = fields_ref[index_ref[s], f]
            u = s * subs + f
            edges = lax.dot_general(pick, x, NT, preferred_element_type=jnp.float32)
            edges = edges.astype(jnp.bfloat16)
            for d in range(copies_ref.shape[0]):
                copies_ref[d, u * 4 * SIDE : (u + 1) * 4 * SIDE, :] = edges


def owned_rows(core, patches, owned):
    for c in range(2):

        @pl.when(core == c)
        def _():
            for g in range(K // 144):
                owned[g * 72 : (g + 1) * 72, :] = patches[g * 144 + c * 72 : g * 144 + c * 72 + 72, :]


def tap_blocks():
    return [slice(0, 4), slice(4, 8), slice(8, TAPS)]


def core_index():
    return lax.axis_index("face") & 1


def inner_kernel(
    index_ref,
    own_ref,
    other_ref,
    gram_ref,
    pairs_ref,
    patches,
    owned,
    gram,
    sems,
):
    subs = own_ref.shape[1]
    core = core_index()

    index = index_ref[...]
    for s in range(2):
        rows = slice(s * subs * CH, (s + 1) * subs * CH)
        chosen = [(index[:, s : s + 1] == n).astype(jnp.float32).astype(jnp.bfloat16) for n in range(own_ref.shape[0])]
        for n, ref in enumerate((own_ref, other_ref)):
            parts = [ref[k].reshape(subs * CH, PIX) * one for k, one in enumerate(chosen)]
            pairs_ref[rows, n * PIX : (n + 1) * PIX] = sum(parts[1:], parts[0])

    row_at = lax.broadcasted_iota(jnp.int32, (PIX, PIX), 0)
    place = lax.broadcasted_iota(jnp.int32, (8, PIX), 1)
    ahead = [row_at - inner_pixels(place + d)[0:1, :] for d in (0, INNER - PIX)]
    for t in range(TAPS):
        shift = (t // 3 - 1) * SIDE + t % 3 - 1
        taps = [jnp.where(d == shift, 1.0, 0.0).astype(jnp.bfloat16) for d in ahead]
        for s in range(2):
            first, second = (
                jnp.dot(
                    pairs_ref[s * subs * CH : (s + 1) * subs * CH, n * PIX : (n + 1) * PIX],
                    tap,
                    preferred_element_type=jnp.float32,
                )
                for n, tap in enumerate(taps)
            )
            columns = (first[:, :CH], first[:, CH:] + second[:, :CH], second[:, CH:])
            for n, values in enumerate(columns):
                values = values.astype(jnp.bfloat16)
                for f in range(subs):
                    at = (s * subs + f) * 2 * INNER + n * CH
                    patches[t * CH : (t + 1) * CH, at : at + CH] = values[f * CH : (f + 1) * CH, :]
    owned_rows(core, patches, owned)
    copies = []
    for n, taps in enumerate(tap_blocks()):
        right = patches[taps.start * CH : taps.stop * CH, :]
        block = lax.dot_general(owned[...], right, NT, preferred_element_type=jnp.float32)
        for l in range(taps.stop - taps.start):
            gram[taps.start + l, :, :] = block[:, l * CH : (l + 1) * CH]
        copies.append(pltpu.make_async_copy(gram.at[taps], gram_ref.at[taps], sems.at[n]))
        copies[-1].start()
    for copy in copies:
        copy.wait()


def gather_kernel(subs, halo_own_ref, halo_other_ref, table_ref, after_ref, tiles_ref):
    core = core_index()
    zero = jnp.zeros((SIDE, CH), jnp.bfloat16)
    for side, halo_ref in enumerate((halo_own_ref, halo_other_ref)):
        for f in range(subs):
            for n, at in enumerate(SIDE_AT + CORNER_AT):
                index = halo_ref[f, at]
                sub = lax.shift_right_logical(index, 6)
                device = lax.shift_right_logical(sub * THIRD, 7)
                row = (lax.shift_right_logical(device, 1) * 2 * subs + sub - device * subs) * 4 * SIDE
                row = pl.multiple_of(row + (index & (3 * SIDE)), SIDE)
                for s in range(2):
                    u = (side * 2 + s) * subs + f
                    tile = table_ref[pl.ds(pl.multiple_of(row + s * subs * 4 * SIDE, SIDE), SIDE), :]
                    tiles_ref[u * CH + n * SIDE : u * CH + (n + 1) * SIDE, :] = jnp.where((device & 1) == core, tile, zero)


def rim_kernel(subs, pairs_ref, after_ref, inner_ref, rim_ref, matrix_ref, energy_ref, gram_ref, pixels, sem):
    copy = pltpu.make_async_copy(inner_ref.at[tap_blocks()[0]], gram_ref, sem)
    copy.start()
    for t in range(TAPS):
        pixel, cycle = rim_sources(t)
        pixels[:, t * CH : (t + 1) * CH] = one_hot(2 * PIX, pixel)
        matrix_ref[:, t * CH : (t + 1) * CH] = one_hot(2 * CH, cycle)
    energy = jnp.zeros((CH, CH), jnp.float32)
    for p in range(2 * subs):
        x = pairs_ref[p * CH : (p + 1) * CH, :].astype(jnp.float32)
        for n in range(4):
            energy += x[:, n * CH : (n + 1) * CH] * x[:, n * CH : (n + 1) * CH]
    energy_ref[...] = energy
    values = jnp.dot(pairs_ref[...], pixels[...], preferred_element_type=jnp.float32).astype(jnp.bfloat16)
    for p in range(2 * subs):
        for t in range(TAPS):
            part = values[p * CH : (p + 1) * CH, t * CH : (t + 1) * CH]
            rim_ref[t * CH : (t + 1) * CH, p * CH : (p + 1) * CH] = part
    copy.wait()


def outer_kernel(
    subs,
    tiles_own_ref,
    tiles_other_ref,
    halo_rows_own_ref,
    halo_rows_other_ref,
    matrix_ref,
    energy_ref,
    mask_ref,
    rim_ref,
    first_ref,
    inner_ref,
    message_ref,
    patches,
    owned,
    gram,
    stage,
    position,
    cycles,
    inner,
    sems,
):
    core = core_index()
    units = 4 * subs
    half = units // 2
    copies = []
    for n, taps in enumerate(tap_blocks()[1:]):
        copies.append(pltpu.make_async_copy(inner_ref.at[taps], inner.at[taps], sems.at[n]))
        copies[-1].start()

    lane = lax.broadcasted_iota(jnp.int32, (8, CH), 1)
    base = jnp.full((8, CH), -1000, jnp.int32)
    for e, at in enumerate(SIDE_AT):
        base = jnp.where((lane >= at) & (lane < at + SIDE), e * SIDE, base)
    for e, at in enumerate(CORNER_AT):
        base = jnp.where(lane == at, (4 + e) * SIDE, base)
    position[...] = jnp.zeros((8, CH), jnp.int32)
    position[0:subs, 0:CYCLE] = lax.rem(halo_rows_own_ref[...], SIDE)
    position[subs : 2 * subs, 0:CYCLE] = lax.rem(halo_rows_other_ref[...], SIDE)
    source = position[...] + base

    row_at = lax.broadcasted_iota(jnp.int32, (CH, CH), 0)
    col_at = lax.broadcasted_iota(jnp.int32, (CH, CH), 1)
    diagonal = row_at == col_at
    eye = jnp.where(diagonal, 1.0, 0.0).astype(jnp.bfloat16)
    split = units * CH // 2
    energy = energy_ref[...]
    for side, (mine, theirs) in enumerate(((0, split), (split, 0))):
        tiles = tiles_own_ref[mine : mine + split, :] + tiles_other_ref[theirs : theirs + split, :]
        tiles = lax.dot_general(eye, tiles, NT, preferred_element_type=jnp.float32).astype(jnp.bfloat16)
        for p in range(half):
            at = side * subs + p % subs
            pick = jnp.where(row_at == source[at : at + 1, :], 1.0, 0.0).astype(jnp.bfloat16)
            cycle = jnp.dot(tiles[:, p * CH : (p + 1) * CH], pick, preferred_element_type=jnp.float32)
            energy += cycle * cycle
            cycles[p * CH : (p + 1) * CH, side * CH : (side + 1) * CH] = cycle.astype(jnp.bfloat16)

    values = jnp.dot(cycles[...], matrix_ref[...], preferred_element_type=jnp.float32).astype(jnp.bfloat16)
    for p in range(half):
        for t in range(TAPS):
            part = values[p * CH : (p + 1) * CH, t * CH : (t + 1) * CH]
            place = (slice(t * CH, (t + 1) * CH), slice(p * CH, (p + 1) * CH))
            patches[place] = rim_ref[place] + part

    kept = mask_ref[...].astype(jnp.float32)
    kept_row = jnp.sum(jnp.where(diagonal, kept, 0.0), axis=1, keepdims=True)
    energy = jnp.sum(energy, axis=1, keepdims=True)

    def exponent(values):
        top = jnp.full((8, CH), jnp.maximum(jnp.max(values), 2.0**-120), jnp.float32)
        return jnp.ceil(jnp.log2(top) * (STEPS / 2) + 0.1)

    kept_exp = exponent(jnp.where(kept_row > 0, energy, 0.0))
    any_exp = exponent(energy)
    lane_exps = jnp.where(kept > 0, kept_exp, any_exp) + kept_exp
    scale = jnp.exp2(lane_exps * (-1 / STEPS)) * TOP**2

    def coded(values):
        return jnp.round(values * lax.rsqrt(jnp.maximum(jnp.abs(values), 1e-30)))

    owned_rows(core, patches, owned)

    def add_block(n, at):
        taps = tap_blocks()[n]
        right = patches[taps.start * CH : taps.stop * CH, :]
        block = lax.dot_general(owned[at, :], right, NT, preferred_element_type=jnp.float32)
        if n > 0 and at.start == 0:
            copies[n - 1].wait()
        for l in range(taps.stop - taps.start):
            part = block[:, l * CH : (l + 1) * CH] + (inner if n > 0 else first_ref)[taps.start + l, at, :]
            gram[taps.start + l, at, :] = coded(part * scale[0:1, :])

    add_block(0, slice(0, HALF))
    for m in range(0, HALF, HALF // 2):
        add_block(1, slice(m, m + HALF // 2))
        add_block(2, slice(m, m + HALF // 2))

        for j in range(m // 9, (m + HALF // 2) // 9, GROUP):
            block = stage.at[j // GROUP % 4]
            for i in range(GROUP):
                for l in range(TAPS):
                    to = i * ROWS + l * 9
                    block[to : to + 9, :] = gram[l, (j + i) * 9 : (j + i + 1) * 9, :]
                block[i * ROWS + 81 : (i + 1) * ROWS, :] = lane_exps[0:1, :]
            message_ref[j * ROWS : (j + GROUP) * ROWS, :] = block[...].astype(jnp.int32).astype(jnp.int16)


def rows_kernel(count, landed_ref, weight_ref, kept_ref, out_ref, rows, split, stage):
    owner = lax.axis_index("face") * lax.axis_size("sample") + lax.axis_index("sample")
    total = jnp.zeros((ROWS, CH), jnp.float32)
    for j in range(0, landed_ref.shape[0] // ROWS, 2 * GROUP):
        block = stage.at[j // (2 * GROUP) % 4]
        block[...] = landed_ref[j * ROWS : (j + 2 * GROUP) * ROWS, :].astype(jnp.int32).astype(jnp.float32)
        for i in range(2 * GROUP):
            codes = block[i * ROWS : (i + 1) * ROWS, :]
            total += codes * jnp.abs(codes) * jnp.exp2(block[i * ROWS + 81 : (i + 1) * ROWS, :] * (1 / STEPS))
    total = total * TOP**-2
    rows[...] = jnp.zeros_like(rows)
    for l in range(TAPS):
        rows[0:9, l * CH : (l + 1) * CH] = total[l * 9 : (l + 1) * 9, :]

    channel = lax.rem(owner * 9 + lax.broadcasted_iota(jnp.int32, (16, CH), 0), CH)
    own = lax.broadcasted_iota(jnp.int32, (16, CH), 1) == channel
    keep = jnp.sum(jnp.where(own, kept_ref[...].astype(jnp.float32), 0.0), axis=1, keepdims=True)
    whole = rows[...]
    head = whole.astype(jnp.bfloat16)
    left = whole - head.astype(jnp.float32)
    tail = left.astype(jnp.bfloat16)
    split[0:16, :] = head
    split[16:32, :] = tail
    split[32:48, :] = (left - tail.astype(jnp.float32)).astype(jnp.bfloat16)
    product = jnp.dot(split[...], weight_ref[...], preferred_element_type=jnp.float32)
    product = product[32:48, :] + product[16:32, :] + product[0:16, :]
    kept = kept_ref[...] > 0
    for t in range(TAPS):
        part = whole[:, t * CH : (t + 1) * CH]
        part = jnp.where((keep > 0) & kept, part / count, 0.0)
        out_ref[:, t * CH : (t + 1) * CH] = part[0:9, :]
    for n in range(2):
        part = product[:, n * CH : (n + 1) * CH]
        part = jnp.where(keep > 0, part / count, 0.0)
        out_ref[:, K + n * CH : K + (n + 1) * CH] = part[0:9, :]


VMEM = pl.BlockSpec(memory_space=pltpu.VMEM)
SMEM = pl.BlockSpec(memory_space=pltpu.SMEM)
HBM = pl.BlockSpec(memory_space=pltpu.HBM)
ANY = pl.BlockSpec(memory_space=pl.ANY)


def shape(dims, kind):
    return jax.ShapeDtypeStruct(dims, kind)


def per_device(fields, sample_index, halo_index, channel_mask, weight):
    faces, samples = lax.axis_size("face"), lax.axis_size("sample")
    subs = fields.shape[1]
    units = 4 * subs
    swap = [(f, f ^ 1) for f in range(faces)]
    bf16, f32 = jnp.bfloat16, jnp.float32

    other = lax.ppermute(fields, "face", swap)
    halo_other = lax.ppermute(halo_index, "face", swap)
    copies = pl.pallas_call(
        edges_kernel,
        out_shape=shape((faces // 2, 8 * subs * SIDE, CH), bf16),
        in_specs=[SMEM, VMEM],
        out_specs=VMEM,
        compiler_params=pltpu.CompilerParams(vmem_limit_bytes=8 * 2**20),
        name="edges",
    )(*(pltpu.with_memory_space_constraint(a, pltpu.HBM) for a in (sample_index, fields)))

    same_core = [[f for f in range(c, faces, 2)] for c in range(2)]
    table = lax.all_to_all(copies, "face", 0, 0, axis_index_groups=same_core)

    mask_row = channel_mask[None]
    inner, pairs = pl.pallas_call(
        inner_kernel,
        out_shape=(
            pltpu.HBM((TAPS, HALF, CH), f32),
            shape((units * CH // 2, 2 * PIX), bf16),
        ),
        in_specs=[VMEM] * 3,
        out_specs=(HBM, VMEM),
        scratch_shapes=[
            pltpu.VMEM((K, units * INNER), bf16),
            pltpu.VMEM((HALF, units * INNER), bf16),
            pltpu.VMEM((TAPS, HALF, CH), f32),
            pltpu.SemaphoreType.DMA((3,)),
        ],
        compiler_params=pltpu.CompilerParams(vmem_limit_bytes=32 * 2**20),
        cost_estimate=pl.CostEstimate(flops=6 * 10**9, bytes_accessed=5 * 10**6, transcendentals=0),
        name="inner",
    )(sample_index[None], fields, other)

    tiles = pl.pallas_call(
        functools.partial(gather_kernel, subs),
        out_shape=shape((units * CH, CH), bf16),
        in_specs=[SMEM, SMEM, VMEM, ANY],
        out_specs=VMEM,
        compiler_params=pltpu.CompilerParams(vmem_limit_bytes=4 * 2**20),
        name="gather",
    )(halo_index, halo_other, table.reshape(-1, CH), pairs)
    tiles_other = lax.ppermute(tiles, "face", swap)

    inner = pltpu.with_memory_space_constraint(inner, pltpu.HBM)
    rim, matrix, energy, first = pl.pallas_call(
        functools.partial(rim_kernel, subs),
        out_shape=(
            shape((K, units * RIM), bf16),
            shape((2 * CH, K), bf16),
            shape((CH, CH), f32),
            shape((tap_blocks()[0].stop, HALF, CH), f32),
        ),
        in_specs=[VMEM, ANY, HBM],
        out_specs=(VMEM, VMEM, VMEM, VMEM),
        scratch_shapes=[pltpu.VMEM((2 * PIX, K), bf16), pltpu.SemaphoreType.DMA],
        compiler_params=pltpu.CompilerParams(vmem_limit_bytes=16 * 2**20),
        cost_estimate=pl.CostEstimate(flops=10**9, bytes_accessed=6 * 10**6, transcendentals=0),
        name="rim",
    )(pairs, tiles, inner)

    message = pl.pallas_call(
        functools.partial(outer_kernel, subs),
        out_shape=shape((64 * ROWS, CH), jnp.int16),
        in_specs=[VMEM] * 9 + [HBM],
        out_specs=VMEM,
        scratch_shapes=[
            pltpu.VMEM((K, units * RIM), bf16),
            pltpu.VMEM((HALF, units * RIM), bf16),
            pltpu.VMEM((TAPS, HALF, CH), f32),
            pltpu.VMEM((4, GROUP * ROWS, CH), f32),
            pltpu.VMEM((8, CH), jnp.int32),
            pltpu.VMEM((units * CH // 2, 2 * CH), bf16),
            pltpu.VMEM((TAPS, HALF, CH), f32),
            pltpu.SemaphoreType.DMA((2,)),
        ],
        compiler_params=pltpu.CompilerParams(vmem_limit_bytes=28 * 2**20),
        name="outer",
    )(
        tiles,
        tiles_other,
        halo_index,
        halo_other,
        matrix,
        energy,
        mask_row,
        rim,
        first,
        inner,
    )

    groups = [[f * samples + s for f in range(c, faces, 2) for s in range(samples)] for c in range(2)]
    landed = lax.all_to_all(message.reshape(64, -1, 2, CH), AXES, 0, 0, axis_index_groups=groups).reshape(-1, CH)
    count = 2 * subs * PIX * faces * samples
    return pl.pallas_call(
        functools.partial(rows_kernel, count),
        out_shape=shape((9, K + weight.shape[1]), f32),
        in_specs=[VMEM] * 3,
        out_specs=VMEM,
        scratch_shapes=[pltpu.VMEM((16, K), f32), pltpu.VMEM((48, K), bf16), pltpu.VMEM((4, 2 * GROUP * ROWS, CH), f32)],
        compiler_params=pltpu.CompilerParams(vmem_limit_bytes=8 * 2**20),
        name="rows",
    )(landed, weight, mask_row)


def solution(mesh):
    placed = (P("sample", "face", None, None), P("sample"), P("face", None), P(), P())
    return jax.shard_map(
        per_device,
        mesh=mesh,
        in_specs=placed,
        out_specs=P(("face", "sample"), None),
        check_vma=False,
    )
```

```python
import functools

import jax
import jax.numpy as jnp
import ml_dtypes
import numpy as np
from jax import lax
from jax.experimental import pallas as pl
from jax.experimental.pallas import tpu as pltpu
from jax.sharding import PartitionSpec as P

SIDE = 16
PIX = SIDE * SIDE
CH = 128
TAPS = 9
K = TAPS * CH
HALF = K // 2
CYCLE = 4 * SIDE + 4
RIM = 64
INNER = PIX - RIM
ROWS = 82
STEPS = 16
TOP = 32700.0
THIRD = 43
GROUP = 16
AXES = ("face", "sample")
NT = (((1,), (1,)), ((), ()))
SIDE_AT = (1, 19, 36, 52)
CORNER_AT = (0, 17, 18, 35)


def rim_sources(tap):
    lane = lax.broadcasted_iota(jnp.int32, (8, CH), 1)
    second = lane >= RIM
    place = lax.rem(lane, RIM)
    along = lax.rem(place, SIDE)
    side = place // SIDE
    y = jnp.where(side == 0, 0, jnp.where(side == 1, SIDE - 1, along))
    x = jnp.where(side == 2, 0, jnp.where(side == 3, SIDE - 1, along))
    corner = (side >= 2) & ((along == 0) | (along == SIDE - 1))
    y = jnp.where(corner, jnp.clip(along, 1, SIDE - 2), y)
    x = jnp.where(corner, jnp.where(side == 2, 1, SIDE - 2), x)
    u, v = y + tap // 3 - 1, x + tap % 3 - 1
    inside = (u >= 0) & (u < SIDE) & (v >= 0) & (v < SIDE)
    entry = jnp.where(v < 0, 2 * SIDE + 4 + u, 3 * SIDE + 4 + u)
    entry = jnp.where(u < 0, v + 1, jnp.where(u >= SIDE, SIDE + 3 + v, entry))
    pixel = jnp.where(inside, u * SIDE + v + jnp.where(second, PIX, 0), -1)
    cycle = jnp.where(inside, -1, entry + jnp.where(second, CH, 0))
    return pixel[0:1, :], cycle[0:1, :]


def inner_pixels(place):
    rest = place - 2 * (SIDE - 4)
    row = lax.shift_right_logical(jnp.maximum(rest, 0) * 147, 11)
    y = jnp.where(place < SIDE - 4, 1, jnp.where(rest < 0, SIDE - 2, row + 2))
    x = jnp.where(place < SIDE - 4, place + 2, jnp.where(rest < 0, place - SIDE + 6, rest - row * (SIDE - 2) + 1))
    return jnp.where((place >= 0) & (place < INNER), y * SIDE + x, -PIX)


def one_hot(rows, source):
    at = lax.broadcasted_iota(jnp.int32, (rows, CH), 0)
    return jnp.where(at == source, 1.0, 0.0).astype(jnp.bfloat16)


def edges_kernel(index_ref, fields_ref, copies_ref):
    subs = fields_ref.shape[1]
    row = lax.broadcasted_iota(jnp.int32, (4 * SIDE, PIX), 0)
    pixel = lax.broadcasted_iota(jnp.int32, (4 * SIDE, PIX), 1)
    along = row & (SIDE - 1)
    wanted = jnp.where(row < SIDE, along, (SIDE - 1) * SIDE + along)
    wanted = jnp.where(row >= 2 * SIDE, along * SIDE, wanted)
    wanted = jnp.where(row >= 3 * SIDE, along * SIDE + SIDE - 1, wanted)
    pick = jnp.where(pixel == wanted, 1.0, 0.0).astype(jnp.bfloat16)
    for s in range(2):
        for f in range(subs):
            x = fields_ref[index_ref[s], f]
            u = s * subs + f
            edges = lax.dot_general(pick, x, NT, preferred_element_type=jnp.float32)
            edges = edges.astype(jnp.bfloat16)
            for d in range(copies_ref.shape[0]):
                copies_ref[d, u * 4 * SIDE : (u + 1) * 4 * SIDE, :] = edges


def owned_rows(core, patches, owned):
    for c in range(2):

        @pl.when(core == c)
        def _():
            for g in range(K // 144):
                owned[g * 72 : (g + 1) * 72, :] = patches[g * 144 + c * 72 : g * 144 + c * 72 + 72, :]


def tap_blocks():
    return [slice(0, 4), slice(4, 8), slice(8, TAPS)]


def core_index():
    return lax.axis_index("face") & 1


def inner_kernel(
    index_ref,
    own_ref,
    other_ref,
    gram_ref,
    pairs_ref,
    patches,
    owned,
    gram,
    sems,
):
    subs = own_ref.shape[1]
    core = core_index()

    index = index_ref[...]
    for s in range(2):
        rows = slice(s * subs * CH, (s + 1) * subs * CH)
        chosen = [(index[:, s : s + 1] == n).astype(jnp.float32).astype(jnp.bfloat16) for n in range(own_ref.shape[0])]
        for n, ref in enumerate((own_ref, other_ref)):
            parts = [ref[k].reshape(subs * CH, PIX) * one for k, one in enumerate(chosen)]
            pairs_ref[rows, n * PIX : (n + 1) * PIX] = sum(parts[1:], parts[0])

    row_at = lax.broadcasted_iota(jnp.int32, (PIX, PIX), 0)
    place = lax.broadcasted_iota(jnp.int32, (8, PIX), 1)
    ahead = [row_at - inner_pixels(place + d)[0:1, :] for d in (0, INNER - PIX)]
    for t in range(TAPS):
        shift = (t // 3 - 1) * SIDE + t % 3 - 1
        taps = [jnp.where(d == shift, 1.0, 0.0).astype(jnp.bfloat16) for d in ahead]
        for s in range(2):
            first, second = (
                jnp.dot(
                    pairs_ref[s * subs * CH : (s + 1) * subs * CH, n * PIX : (n + 1) * PIX],
                    tap,
                    preferred_element_type=jnp.float32,
                )
                for n, tap in enumerate(taps)
            )
            columns = (first[:, :CH], first[:, CH:] + second[:, :CH], second[:, CH:])
            for n, values in enumerate(columns):
                values = values.astype(jnp.bfloat16)
                for f in range(subs):
                    at = (s * subs + f) * 2 * INNER + n * CH
                    patches[t * CH : (t + 1) * CH, at : at + CH] = values[f * CH : (f + 1) * CH, :]
    owned_rows(core, patches, owned)
    copies = []
    for n, taps in enumerate(tap_blocks()):
        right = patches[taps.start * CH : taps.stop * CH, :]
        block = lax.dot_general(owned[...], right, NT, preferred_element_type=jnp.float32)
        for l in range(taps.stop - taps.start):
            gram[taps.start + l, :, :] = block[:, l * CH : (l + 1) * CH]
        copies.append(pltpu.make_async_copy(gram.at[taps], gram_ref.at[taps], sems.at[n]))
        copies[-1].start()
    for copy in copies:
        copy.wait()


def gather_kernel(subs, halo_own_ref, halo_other_ref, table_ref, after_ref, tiles_ref):
    core = core_index()
    zero = jnp.zeros((SIDE, CH), jnp.bfloat16)
    for side, halo_ref in enumerate((halo_own_ref, halo_other_ref)):
        for f in range(subs):
            for n, at in enumerate(SIDE_AT + CORNER_AT):
                index = halo_ref[f, at]
                sub = lax.shift_right_logical(index, 6)
                device = lax.shift_right_logical(sub * THIRD, 7)
                row = (lax.shift_right_logical(device, 1) * 2 * subs + sub - device * subs) * 4 * SIDE
                row = pl.multiple_of(row + (index & (3 * SIDE)), SIDE)
                for s in range(2):
                    u = (side * 2 + s) * subs + f
                    tile = table_ref[pl.ds(pl.multiple_of(row + s * subs * 4 * SIDE, SIDE), SIDE), :]
                    tiles_ref[u * CH + n * SIDE : u * CH + (n + 1) * SIDE, :] = jnp.where((device & 1) == core, tile, zero)


def rim_kernel(subs, pairs_ref, after_ref, inner_ref, rim_ref, matrix_ref, energy_ref, gram_ref, pixels, sem):
    copy = pltpu.make_async_copy(inner_ref.at[tap_blocks()[0]], gram_ref, sem)
    copy.start()
    for t in range(TAPS):
        pixel, cycle = rim_sources(t)
        pixels[:, t * CH : (t + 1) * CH] = one_hot(2 * PIX, pixel)
        matrix_ref[:, t * CH : (t + 1) * CH] = one_hot(2 * CH, cycle)
    energy = jnp.zeros((CH, CH), jnp.float32)
    for p in range(2 * subs):
        x = pairs_ref[p * CH : (p + 1) * CH, :].astype(jnp.float32)
        for n in range(4):
            energy += x[:, n * CH : (n + 1) * CH] * x[:, n * CH : (n + 1) * CH]
    energy_ref[...] = energy
    values = jnp.dot(pairs_ref[...], pixels[...], preferred_element_type=jnp.float32).astype(jnp.bfloat16)
    for p in range(2 * subs):
        for t in range(TAPS):
            part = values[p * CH : (p + 1) * CH, t * CH : (t + 1) * CH]
            rim_ref[t * CH : (t + 1) * CH, p * CH : (p + 1) * CH] = part
    copy.wait()


def outer_kernel(
    subs,
    tiles_own_ref,
    tiles_other_ref,
    halo_rows_own_ref,
    halo_rows_other_ref,
    matrix_ref,
    energy_ref,
    mask_ref,
    rim_ref,
    first_ref,
    inner_ref,
    message_ref,
    patches,
    owned,
    gram,
    stage,
    position,
    cycles,
    inner,
    sems,
):
    core = core_index()
    units = 4 * subs
    half = units // 2
    copies = []
    for n, taps in enumerate(tap_blocks()[1:]):
        copies.append(pltpu.make_async_copy(inner_ref.at[taps], inner.at[taps], sems.at[n]))
        copies[-1].start()

    lane = lax.broadcasted_iota(jnp.int32, (8, CH), 1)
    base = jnp.full((8, CH), -1000, jnp.int32)
    for e, at in enumerate(SIDE_AT):
        base = jnp.where((lane >= at) & (lane < at + SIDE), e * SIDE, base)
    for e, at in enumerate(CORNER_AT):
        base = jnp.where(lane == at, (4 + e) * SIDE, base)
    position[...] = jnp.zeros((8, CH), jnp.int32)
    position[0:subs, 0:CYCLE] = lax.rem(halo_rows_own_ref[...], SIDE)
    position[subs : 2 * subs, 0:CYCLE] = lax.rem(halo_rows_other_ref[...], SIDE)
    source = position[...] + base

    row_at = lax.broadcasted_iota(jnp.int32, (CH, CH), 0)
    col_at = lax.broadcasted_iota(jnp.int32, (CH, CH), 1)
    diagonal = row_at == col_at
    eye = jnp.where(diagonal, 1.0, 0.0).astype(jnp.bfloat16)
    split = units * CH // 2
    energy = energy_ref[...]
    for side, (mine, theirs) in enumerate(((0, split), (split, 0))):
        tiles = tiles_own_ref[mine : mine + split, :] + tiles_other_ref[theirs : theirs + split, :]
        tiles = lax.dot_general(eye, tiles, NT, preferred_element_type=jnp.float32).astype(jnp.bfloat16)
        for p in range(half):
            at = side * subs + p % subs
            pick = jnp.where(row_at == source[at : at + 1, :], 1.0, 0.0).astype(jnp.bfloat16)
            cycle = jnp.dot(tiles[:, p * CH : (p + 1) * CH], pick, preferred_element_type=jnp.float32)
            energy += cycle * cycle
            cycles[p * CH : (p + 1) * CH, side * CH : (side + 1) * CH] = cycle.astype(jnp.bfloat16)

    values = jnp.dot(cycles[...], matrix_ref[...], preferred_element_type=jnp.float32).astype(jnp.bfloat16)
    for p in range(half):
        for t in range(TAPS):
            part = values[p * CH : (p + 1) * CH, t * CH : (t + 1) * CH]
            place = (slice(t * CH, (t + 1) * CH), slice(p * CH, (p + 1) * CH))
            patches[place] = rim_ref[place] + part

    kept = mask_ref[...].astype(jnp.float32)
    kept_row = jnp.sum(jnp.where(diagonal, kept, 0.0), axis=1, keepdims=True)
    energy = jnp.sum(energy, axis=1, keepdims=True)

    def exponent(values):
        top = jnp.full((8, CH), jnp.maximum(jnp.max(values), 2.0**-120), jnp.float32)
        return jnp.ceil(jnp.log2(top) * (STEPS / 2) + 0.1)

    kept_exp = exponent(jnp.where(kept_row > 0, energy, 0.0))
    any_exp = exponent(energy)
    lane_exps = jnp.where(kept > 0, kept_exp, any_exp) + kept_exp
    scale = jnp.exp2(lane_exps * (-1 / STEPS)) * TOP**2

    def coded(values):
        return jnp.round(values * lax.rsqrt(jnp.maximum(jnp.abs(values), 1e-30)))

    owned_rows(core, patches, owned)

    def add_block(n, at):
        taps = tap_blocks()[n]
        right = patches[taps.start * CH : taps.stop * CH, :]
        block = lax.dot_general(owned[at, :], right, NT, preferred_element_type=jnp.float32)
        if n > 0 and at.start == 0:
            copies[n - 1].wait()
        for l in range(taps.stop - taps.start):
            part = block[:, l * CH : (l + 1) * CH] + (inner if n > 0 else first_ref)[taps.start + l, at, :]
            gram[taps.start + l, at, :] = coded(part * scale[0:1, :])

    add_block(0, slice(0, HALF))
    for m in range(0, HALF, HALF // 2):
        add_block(1, slice(m, m + HALF // 2))
        add_block(2, slice(m, m + HALF // 2))

        for j in range(m // 9, (m + HALF // 2) // 9, GROUP):
            block = stage.at[j // GROUP % 4]
            for i in range(GROUP):
                for l in range(TAPS):
                    to = i * ROWS + l * 9
                    block[to : to + 9, :] = gram[l, (j + i) * 9 : (j + i + 1) * 9, :]
                block[i * ROWS + 81 : (i + 1) * ROWS, :] = lane_exps[0:1, :]
            message_ref[j * ROWS : (j + GROUP) * ROWS, :] = block[...].astype(jnp.int32).astype(jnp.int16)


def rows_kernel(count, landed_ref, weight_ref, kept_ref, out_ref, rows, split, stage):
    owner = lax.axis_index("face") * lax.axis_size("sample") + lax.axis_index("sample")
    total = jnp.zeros((ROWS, CH), jnp.float32)
    for j in range(0, landed_ref.shape[0] // ROWS, GROUP):
        block = stage.at[j // (GROUP) % 4]
        block[...] = landed_ref[j * ROWS : (j + GROUP) * ROWS, :].astype(jnp.int32).astype(jnp.float32)
        for i in range(GROUP):
            codes = block[i * ROWS : (i + 1) * ROWS, :]
            total += codes * jnp.abs(codes) * jnp.exp2(block[i * ROWS + 81 : (i + 1) * ROWS, :] * (1 / STEPS))
    total = total * TOP**-2
    rows[...] = jnp.zeros_like(rows)
    for l in range(TAPS):
        rows[0:9, l * CH : (l + 1) * CH] = total[l * 9 : (l + 1) * 9, :]

    channel = lax.rem(owner * 9 + lax.broadcasted_iota(jnp.int32, (16, CH), 0), CH)
    own = lax.broadcasted_iota(jnp.int32, (16, CH), 1) == channel
    keep = jnp.sum(jnp.where(own, kept_ref[...].astype(jnp.float32), 0.0), axis=1, keepdims=True)
    whole = rows[...]
    head = whole.astype(jnp.bfloat16)
    left = whole - head.astype(jnp.float32)
    tail = left.astype(jnp.bfloat16)
    split[0:16, :] = head
    split[16:32, :] = tail
    split[32:48, :] = (left - tail.astype(jnp.float32)).astype(jnp.bfloat16)
    product = jnp.dot(split[...], weight_ref[...], preferred_element_type=jnp.float32)
    product = product[32:48, :] + product[16:32, :] + product[0:16, :]
    kept = kept_ref[...] > 0
    for t in range(TAPS):
        part = whole[:, t * CH : (t + 1) * CH]
        part = jnp.where((keep > 0) & kept, part / count, 0.0)
        out_ref[:, t * CH : (t + 1) * CH] = part[0:9, :]
    for n in range(2):
        part = product[:, n * CH : (n + 1) * CH]
        part = jnp.where(keep > 0, part / count, 0.0)
        out_ref[:, K + n * CH : K + (n + 1) * CH] = part[0:9, :]


VMEM = pl.BlockSpec(memory_space=pltpu.VMEM)
SMEM = pl.BlockSpec(memory_space=pltpu.SMEM)
HBM = pl.BlockSpec(memory_space=pltpu.HBM)
ANY = pl.BlockSpec(memory_space=pl.ANY)


def shape(dims, kind):
    return jax.ShapeDtypeStruct(dims, kind)


def per_device(fields, sample_index, halo_index, channel_mask, weight):
    faces, samples = lax.axis_size("face"), lax.axis_size("sample")
    subs = fields.shape[1]
    units = 4 * subs
    swap = [(f, f ^ 1) for f in range(faces)]
    bf16, f32 = jnp.bfloat16, jnp.float32

    other = lax.ppermute(fields, "face", swap)
    halo_other = lax.ppermute(halo_index, "face", swap)
    copies = pl.pallas_call(
        edges_kernel,
        out_shape=shape((faces // 2, 8 * subs * SIDE, CH), bf16),
        in_specs=[SMEM, VMEM],
        out_specs=VMEM,
        compiler_params=pltpu.CompilerParams(vmem_limit_bytes=8 * 2**20),
        name="edges",
    )(*(pltpu.with_memory_space_constraint(a, pltpu.HBM) for a in (sample_index, fields)))

    same_core = [[f for f in range(c, faces, 2)] for c in range(2)]
    table = lax.all_to_all(copies, "face", 0, 0, axis_index_groups=same_core)

    mask_row = channel_mask[None]
    inner, pairs = pl.pallas_call(
        inner_kernel,
        out_shape=(
            pltpu.HBM((TAPS, HALF, CH), f32),
            shape((units * CH // 2, 2 * PIX), bf16),
        ),
        in_specs=[VMEM] * 3,
        out_specs=(HBM, VMEM),
        scratch_shapes=[
            pltpu.VMEM((K, units * INNER), bf16),
            pltpu.VMEM((HALF, units * INNER), bf16),
            pltpu.VMEM((TAPS, HALF, CH), f32),
            pltpu.SemaphoreType.DMA((3,)),
        ],
        compiler_params=pltpu.CompilerParams(vmem_limit_bytes=32 * 2**20),
        cost_estimate=pl.CostEstimate(flops=6 * 10**9, bytes_accessed=5 * 10**6, transcendentals=0),
        name="inner",
    )(sample_index[None], fields, other)

    tiles = pl.pallas_call(
        functools.partial(gather_kernel, subs),
        out_shape=shape((units * CH, CH), bf16),
        in_specs=[SMEM, SMEM, VMEM, ANY],
        out_specs=VMEM,
        compiler_params=pltpu.CompilerParams(vmem_limit_bytes=4 * 2**20),
        name="gather",
    )(halo_index, halo_other, table.reshape(-1, CH), pairs)
    tiles_other = lax.ppermute(tiles, "face", swap)

    inner = pltpu.with_memory_space_constraint(inner, pltpu.HBM)
    rim, matrix, energy, first = pl.pallas_call(
        functools.partial(rim_kernel, subs),
        out_shape=(
            shape((K, units * RIM), bf16),
            shape((2 * CH, K), bf16),
            shape((CH, CH), f32),
            shape((tap_blocks()[0].stop, HALF, CH), f32),
        ),
        in_specs=[VMEM, ANY, HBM],
        out_specs=(VMEM, VMEM, VMEM, VMEM),
        scratch_shapes=[pltpu.VMEM((2 * PIX, K), bf16), pltpu.SemaphoreType.DMA],
        compiler_params=pltpu.CompilerParams(vmem_limit_bytes=16 * 2**20),
        cost_estimate=pl.CostEstimate(flops=10**9, bytes_accessed=6 * 10**6, transcendentals=0),
        name="rim",
    )(pairs, tiles, inner)

    message = pl.pallas_call(
        functools.partial(outer_kernel, subs),
        out_shape=shape((64 * ROWS, CH), jnp.int16),
        in_specs=[VMEM] * 9 + [HBM],
        out_specs=VMEM,
        scratch_shapes=[
            pltpu.VMEM((K, units * RIM), bf16),
            pltpu.VMEM((HALF, units * RIM), bf16),
            pltpu.VMEM((TAPS, HALF, CH), f32),
            pltpu.VMEM((4, GROUP * ROWS, CH), f32),
            pltpu.VMEM((8, CH), jnp.int32),
            pltpu.VMEM((units * CH // 2, 2 * CH), bf16),
            pltpu.VMEM((TAPS, HALF, CH), f32),
            pltpu.SemaphoreType.DMA((2,)),
        ],
        compiler_params=pltpu.CompilerParams(vmem_limit_bytes=28 * 2**20),
        name="outer",
    )(
        tiles,
        tiles_other,
        halo_index,
        halo_other,
        matrix,
        energy,
        mask_row,
        rim,
        first,
        inner,
    )

    groups = [[f * samples + s for f in range(c, faces, 2) for s in range(samples)] for c in range(2)]
    landed = lax.all_to_all(message.reshape(64, -1, 2, CH), AXES, 0, 0, axis_index_groups=groups).reshape(-1, CH)
    count = 2 * subs * PIX * faces * samples
    return pl.pallas_call(
        functools.partial(rows_kernel, count),
        out_shape=shape((9, K + weight.shape[1]), f32),
        in_specs=[VMEM] * 3,
        out_specs=VMEM,
        scratch_shapes=[pltpu.VMEM((16, K), f32), pltpu.VMEM((48, K), bf16), pltpu.VMEM((4, GROUP * ROWS, CH), f32)],
        compiler_params=pltpu.CompilerParams(vmem_limit_bytes=8 * 2**20),
        name="rows",
    )(landed, weight, mask_row)


def solution(mesh):
    placed = (P("sample", "face", None, None), P("sample"), P("face", None), P(), P())
    return jax.shard_map(
        per_device,
        mesh=mesh,
        in_specs=placed,
        out_specs=P(("face", "sample"), None),
        check_vma=False,
    )
```
